32 devices in a mesh: dp: 8 (over z, x), tensor: 4 (over y, core).
Axes of the slice: x: 2, y: 2, z: 4, core: 2. Of those that a mesh axis runs over, the one named last changes fastest.
Arguments:
- queries: bfloat16 [256, 32, 128], P('dp'), may hold values from -5 to 5
- new_keys: bfloat16 [256, 2, 128], P('dp'), may hold values from -5 to 5
- new_values: bfloat16 [256, 2, 128], P('dp'), may hold values from -5 to 5
- key_cache: bfloat16 [256, 2, 128, 128], P('dp', None, 'tensor'), may hold values from -160 to 160
- value_cache: bfloat16 [256, 2, 128, 128], P('dp', None, 'tensor'), may hold values from -5 to 5
- lengths: int32 [256], P('dp'), may hold values from 2 to 128, as said below
- residual_in: bfloat16 [256, 4096], P(('dp', 'tensor')), may hold values from -24 to 24
- query_gain: float32 [128], replicated, may hold values from 0.1 to 1.9
- key_gain: float32 [128], replicated, may hold values from 0.1 to 1.9
- out_proj: bfloat16 [4096, 4096], P('tensor'), may hold values from -0.09375 to 0.09375
- norm_gain: float32 [4096], replicated, may hold values from 0.1 to 1.9
- expert_ids: int32 [256, 8], P(('dp', 'tensor')), may hold values from 0 to 31, all different within a row; in each aligned block of 8 rows (0 to 7, 8 to 15, ...) at most 3 rows name the same one
- gate_weights: float32 [256, 8], P(('dp', 'tensor')), may hold values from 0.05 to 1
- expert_gate: bfloat16 [32, 4096, 768], P(('dp', 'tensor')), may hold values from -0.09375 to 0.09375
- expert_up: bfloat16 [32, 4096, 768], P(('dp', 'tensor')), may hold values from -0.09375 to 0.09375
- expert_down: bfloat16 [32, 768, 4096], P(('dp', 'tensor')), may hold values from -0.21875 to 0.21875
Outputs:
- mixed: bfloat16 [256, 4096], P(('dp', 'tensor'))
The draws below stay inside these ranges and needn't reach their ends.
Inputs may be any that keep to these rules, and one draw needn't show every extreme that they name: `expert_ids`: rows are taken in aligned blocks of 8; within a block no expert is named by more than 3 rows, a bound that some block reaches. `lengths`: each group of 32 rows has a row with 128 positions in use.
All inputs are finite; a program needn't handle non-finite values.
Results may differ from the reference program's by a relative error of at most 0.013.
Values may be sent and summed in bfloat16 or wider, within the bound.
No kernel may reach another device: no remote copies, remote signals or barrier semaphores. Data moves between devices by JAX's collectives and lax.ppermute only.
A program may use at most 128 MiB of HBM per device.

```python
import math
import jax
import jax.numpy as jnp
import numpy as np
from jax import lax

D = 4096
QH = 32
KVH = 2
HD = 128
FFW = 768
TOPK = 8
CAP = 3
TOK_DEV = 8
GROUP = 16
EXPERTS = 32
ROWS_DEV = 32
TOKENS = 256
CACHE = 128


def query_base(key):
    return jnp.clip(jax.random.normal(key, (TOKENS, QH, HD), jnp.float32), -5.0, 5.0)


def draw_queries(key, part):
    base_values = query_base(key)
    return base_values.astype(jnp.bfloat16)


def draw_key_cache(key, part):
    key = jax.random.fold_in(key, 2)
    shape = (TOKENS, KVH, CACHE, HD)
    keys_drawn = jnp.clip(jax.random.normal(key, shape, jnp.float32), -5.0, 5.0)
    return keys_drawn.astype(jnp.bfloat16)


def draw_lengths(key, part):
    key = jax.random.fold_in(key, 3)
    key_one, key_two = jax.random.split(key)
    drawn = jax.random.randint(key_one, (TOKENS,), 2, CACHE + 1, jnp.int32)
    chosen = jax.random.randint(key_two, (TOKENS // ROWS_DEV,), 0, ROWS_DEV, jnp.int32)
    row_index = jnp.arange(TOKENS, dtype=jnp.int32)
    longest = row_index % ROWS_DEV == chosen[row_index // ROWS_DEV]
    return jnp.where(longest, CACHE, drawn).astype(jnp.int32)


def draw_residual_in(key, part):
    key = jax.random.fold_in(key, 4)
    key_one, key_two, key_three = jax.random.split(key, 3)
    row_scale = jnp.exp(jax.random.uniform(key_two, (TOKENS, 1), jnp.float32, math.log(0.2), math.log(2.0)))
    column_scale = jnp.exp(jax.random.uniform(key_three, (1, D), jnp.float32, math.log(0.3), math.log(3.0)))
    base_values = jnp.clip(jax.random.normal(key_one, (TOKENS, D), jnp.float32), -4.0, 4.0)
    return (base_values * row_scale * column_scale).astype(jnp.bfloat16)


def block_levels(own_key, shape, cuts, low, high):
    def one(dim, blocks):
        heights = jax.random.uniform(jax.random.fold_in(jax.random.fold_in(own_key, 6), dim), (blocks,), jnp.float32, low / len(cuts), high / len(cuts))
        return jnp.repeat(jnp.exp(heights), shape[dim] // blocks).reshape((-1,) + (1,) * (len(shape) - dim - 1))

    factor_of = one(*cuts[0])
    for cut in cuts[1:]:
        factor_of = factor_of * one(*cut)
    return factor_of


def shared_out(own_key, own, number, rows, amount, top, bound, lean):
    order = jax.random.permutation(own_key, amount)
    heavy_load, common = portions_of(amount, rows * top, bound, lean, True), portions_of(amount, rows * top, bound, lean, False)
    places = jnp.arange(amount)

    def named(sizes, rotation):
        used = int((sizes > 0).sum())
        fixed = max(1, used // 4)
        moved = fixed + (places - fixed + rotation * (used - fixed)) % max(1, amount - fixed)
        return jnp.zeros((amount,), jnp.int32).at[order[jnp.where(places < fixed, places, moved)]].set(jnp.asarray(sizes, jnp.int32))

    sizes = jnp.where(number % 4 == 0, named(heavy_load, number // 4), named(common, number - number // 4 - 1))
    mixed = jax.random.permutation(jax.random.fold_in(own, 3), amount)
    source_of, sink = mixed[0:amount // 2 * 2:2], mixed[1:amount // 2 * 2:2]
    room = jnp.minimum(sizes[source_of] - 1, bound - sizes[sink]) // 2
    room = jnp.where((source_of == order[0]) | (sink == order[0]) | (sizes[sink] == 0), 0, jnp.maximum(room, 0))
    moved = jax.random.randint(jax.random.fold_in(own, 4), (amount // 2,), 0, 1 << 20) % (room + 1)
    sizes = sizes.at[source_of].add(-moved).at[sink].add(moved)
    labels = jnp.searchsorted(jnp.cumsum(sizes), jnp.arange(rows * top), side="right").astype(jnp.int32)
    listing = labels.reshape(top, rows).T
    listing = listing[jax.random.permutation(jax.random.fold_in(own, 1), rows)]
    rotation = jax.random.randint(jax.random.fold_in(own, 2), (rows, 1), 0, top)
    return jnp.take_along_axis(listing, (jnp.arange(top)[None, :] + rotation) % top, axis=1)


def portions_of(amount, total, most, lean, full):
    portions = [(1 << 20) // math.isqrt(grade ** lean) + 1 for grade in range(1, amount + 1)]
    largest = most if full else min(most, max(-(-total // amount), total * portions[0] // sum(portions)))
    least = 1 if total - largest >= amount - 1 else 0
    given, surplus = [largest] + [least] * (amount - 1), total - largest - least * (amount - 1)
    while surplus > 0:
        candidates = [i for i in range(1, amount) if given[i] < largest] or [i for i in range(1, amount) if given[i] < most]
        whole, budget = sum([portions[i] for i in candidates]), surplus
        for i in candidates:
            extra = min(most - given[i], max(1, budget * portions[i] // whole), surplus)
            given[i] = given[i] + extra
            surplus = surplus - extra
    return np.array(given)


def bell_draw(key, extent, deviation, limit, pieces=(), kind=jnp.bfloat16):
    values = jax.random.normal(key, extent, jnp.float32) * deviation
    if len(pieces) > 0:
        values = block_levels(key, extent, pieces, -0.22, 0.18) * values
    return jnp.clip(values, min=-limit, max=limit).astype(kind)


def setup_inputs(seed: int = 0) -> dict:
    splits = jax.random.split(jax.random.key(seed), 17)
    queries = draw_queries(jax.random.fold_in(splits[16], 71), 0)
    new_keys = bell_draw(splits[1], (TOKENS, KVH, HD), 1.0, 5.0, ((0, 8),))
    new_values = bell_draw(splits[2], (TOKENS, KVH, HD), 1.0, 5.0, ((0, 8),))
    key_cache = draw_key_cache(jax.random.fold_in(splits[16], 71), 0)
    value_cache = bell_draw(splits[4], (TOKENS, KVH, CACHE, HD), 1.0, 5.0, ((0, 8), (2, 4)))
    lengths = draw_lengths(jax.random.fold_in(splits[16], 71), 0)
    residual_in = draw_residual_in(jax.random.fold_in(splits[16], 71), 0)
    query_gain = jnp.clip(1.0 + 0.18 * jax.random.normal(splits[7], (HD,), jnp.float32), 0.1, 1.9)
    key_gain = jnp.clip(1.0 + 0.18 * jax.random.normal(splits[8], (HD,), jnp.float32), 0.1, 1.9)
    out_proj = bell_draw(splits[9], (QH * HD, D), (QH * HD) ** -0.5, 0.09375, ((0, 4),))
    norm_gain = jnp.clip(1.0 + 0.18 * jax.random.normal(splits[10], (D,), jnp.float32), 0.1, 1.9)
    expert_ids_keys = jax.random.split(jax.random.fold_in(splits[11], 1), TOKENS // TOK_DEV)
    expert_ids_turns = jax.random.permutation(jax.random.fold_in(splits[11], 3), TOKENS // TOK_DEV)
    expert_ids = jax.vmap(lambda own, number: shared_out(jax.random.fold_in(splits[11], 2), own, number, TOK_DEV, EXPERTS, TOPK, CAP, 2))(expert_ids_keys, expert_ids_turns).reshape((TOKENS, TOPK))
    gate_weights = jnp.clip(jnp.exp(math.log(1.0) - 2.9957323 * jax.random.uniform(splits[12], (TOKENS, TOPK), jnp.float32) ** block_levels(splits[12], (TOKENS, TOPK), ((0, 32),), -0.2, 0.2)), 0.05, 1.0)
    expert_gate = bell_draw(splits[13], (EXPERTS, D, FFW), D ** -0.5, 0.09375, ((0, 32),))
    expert_up = bell_draw(splits[14], (EXPERTS, D, FFW), D ** -0.5, 0.09375, ((0, 32),))
    expert_down = bell_draw(splits[15], (EXPERTS, FFW, D), FFW ** -0.5, 0.21875, ((0, 32),))
    return {"queries": queries, "new_keys": new_keys, "new_values": new_values, "key_cache": key_cache, "value_cache": value_cache, "lengths": lengths, "residual_in": residual_in, "query_gain": query_gain, "key_gain": key_gain, "out_proj": out_proj, "norm_gain": norm_gain, "expert_ids": expert_ids, "gate_weights": gate_weights, "expert_gate": expert_gate, "expert_up": expert_up, "expert_down": expert_down}


def rms_scale(values, gain):
    mean_sq = lax.optimization_barrier(jnp.mean(values * values, axis=-1, keepdims=True))
    return values * lax.rsqrt(mean_sq + 1e-06) * gain

def reference(queries, new_keys, new_values, key_cache, value_cache, lengths, residual_in, query_gain, key_gain, out_proj, norm_gain, expert_ids, gate_weights, expert_gate, expert_up, expert_down):
    highest = lax.Precision.HIGHEST
    query_norm = rms_scale(queries.astype(jnp.float32), query_gain.astype(jnp.float32)).astype(jnp.bfloat16)
    key_norm = rms_scale(new_keys.astype(jnp.float32), key_gain.astype(jnp.float32)).astype(jnp.bfloat16)
    grouped = query_norm.astype(jnp.float32).reshape(TOKENS, KVH, GROUP, HD)
    scaling = HD ** (-0.5)
    cache_scores = jnp.einsum('tgqd,tgpd->tgqp', grouped, key_cache.astype(jnp.float32), precision=highest) * scaling
    new_score = jnp.einsum('tgqd,tgd->tgq', grouped, key_norm.astype(jnp.float32), precision=highest) * scaling
    positions = jnp.arange(CACHE, dtype=jnp.int32)
    included = (positions[None, :] < lengths[:, None])[:, None, None, :]
    score_top = jnp.maximum(lax.optimization_barrier(jnp.max(jnp.where(included, cache_scores, -1e+30), axis=-1)), new_score)
    cache_weights = jnp.where(included, jnp.exp(cache_scores - score_top[..., None]), 0.0).astype(jnp.bfloat16)
    new_weight = jnp.exp(new_score - score_top).astype(jnp.bfloat16)
    weight_sum = lax.optimization_barrier(jnp.sum(cache_weights.astype(jnp.float32), axis=-1)) + new_weight.astype(jnp.float32)
    numerator = jnp.einsum('tgqp,tgpd->tgqd', cache_weights.astype(jnp.float32), value_cache.astype(jnp.float32), precision=highest)
    numerator = numerator + new_weight.astype(jnp.float32)[..., None] * new_values.astype(jnp.float32)[:, :, None, :]
    attn_out = (numerator / weight_sum[..., None]).reshape(TOKENS, QH * HD).astype(jnp.bfloat16)
    projected = jnp.dot(attn_out, out_proj, preferred_element_type=jnp.float32)
    hidden = residual_in.astype(jnp.float32) + projected
    normed = rms_scale(hidden, norm_gain.astype(jnp.float32)).astype(jnp.bfloat16)
    assign_total = TOKENS * TOPK
    flat_ids = expert_ids.reshape(-1).astype(jnp.int32)
    token_of = jnp.arange(assign_total, dtype=jnp.int32) // TOPK
    sort_order = jnp.argsort(flat_ids, stable=True).astype(jnp.int32)
    counts = jnp.zeros((EXPERTS,), jnp.int32).at[flat_ids].add(1)
    offsets = jnp.cumsum(counts).astype(jnp.int32) - counts
    block_rows = 64
    block_count = (counts + block_rows - 1) // block_rows
    block_start = jnp.cumsum(block_count).astype(jnp.int32) - block_count
    block_total = (assign_total + block_rows - 1) // block_rows + EXPERTS

    def expert_block(index):
        owner_id = jnp.minimum(jnp.sum((block_start + block_count <= index).astype(jnp.int32)), EXPERTS - 1)
        local_block = index - block_start[owner_id]
        first_slot = offsets[owner_id] + local_block * block_rows
        slot_pos = first_slot + jnp.arange(block_rows, dtype=jnp.int32)
        is_live = (local_block < block_count[owner_id]) & (slot_pos < offsets[owner_id] + counts[owner_id])
        safe_pos = jnp.minimum(slot_pos, assign_total - 1)
        picked = normed[token_of[sort_order[safe_pos]]].astype(jnp.float32)
        gate_val = jnp.dot(picked, expert_gate[owner_id].astype(jnp.float32), precision=highest)
        up_val = jnp.dot(picked, expert_up[owner_id].astype(jnp.float32), precision=highest)
        activation = (jax.nn.silu(gate_val) * up_val).astype(jnp.bfloat16)
        result = jnp.dot(activation.astype(jnp.float32), expert_down[owner_id].astype(jnp.float32), precision=highest).astype(jnp.bfloat16)
        result = jnp.where(is_live[:, None], result, jnp.zeros((), jnp.bfloat16))
        return (result, jnp.where(is_live, slot_pos, assign_total).astype(jnp.int32))
    outputs, destinations = lax.map(expert_block, jnp.arange(block_total, dtype=jnp.int32))
    sorted_out = jnp.zeros((assign_total + 1, D), jnp.bfloat16).at[destinations.reshape(-1)].set(outputs.reshape(-1, D))
    assigned = jnp.zeros((assign_total, D), jnp.bfloat16).at[sort_order].set(sorted_out[:assign_total])
    route_weights = (gate_weights / lax.optimization_barrier(jnp.sum(gate_weights, axis=1, keepdims=True))).astype(jnp.bfloat16)
    moe_sum = lax.optimization_barrier(jnp.sum(route_weights.astype(jnp.float32)[:, :, None] * assigned.astype(jnp.float32).reshape(TOKENS, TOPK, D), axis=1))
    return (hidden + moe_sum).astype(jnp.bfloat16)
```

```python
import jax
import jax.numpy as jnp
from jax import lax
from jax.sharding import PartitionSpec as P

BF = jnp.bfloat16
F32 = jnp.float32


def rms_scale(values, gain):
    mean_sq = jnp.mean(values * values, axis=-1, keepdims=True)
    return values * lax.rsqrt(mean_sq + 1e-06) * gain


def swap(x, axis, size, flip):
    return lax.ppermute(x, axis, [(i, i ^ flip) for i in range(size)])


class Plan:
    def __init__(self, dp, tensor):
        zlen = min(4, dp)
        xlen = dp // zlen
        ylen = tensor // 2
        self.axes = {
            "z": ("dp", dp, xlen, zlen),
            "x": ("dp", dp, 1, xlen),
            "y": ("tensor", tensor, 2, ylen),
            "c": ("tensor", tensor, 1, 2),
        }

    def length(self, name):
        return self.axes[name][3]

    def swap(self, x, name, j):
        axis, size, step, _ = self.axes[name]
        return swap(x, axis, size, j * step)


NAMES = "zxyc"


def gather(plan, x, order):
    for name in order:
        dim = NAMES.index(name)
        x = jnp.concatenate(
            [x] + [plan.swap(x, name, j) for j in range(1, plan.length(name))], axis=dim
        )
    return x


def reduce_slots(plan, x, order):
    for name in order:
        dim = NAMES.index(name)
        parts = [lax.slice_in_dim(x, j, j + 1, axis=dim) for j in range(plan.length(name))]
        total = parts[0].astype(F32)
        for j in range(1, plan.length(name)):
            total = total + plan.swap(parts[j].astype(BF), name, j).astype(F32)
        x = total
    return x


def shards(
    queries,
    new_keys,
    new_values,
    key_cache,
    value_cache,
    lengths,
    residual_in,
    query_gain,
    key_gain,
    out_proj,
    norm_gain,
    expert_ids,
    gate_weights,
    expert_gate,
    expert_up,
    expert_down,
):
    tensor_pos = lax.axis_index("tensor")
    dp_pos = lax.axis_index("dp")
    tensor = lax.axis_size("tensor")
    dp = lax.axis_size("dp")
    plan = Plan(dp, tensor)
    rows, heads, hd = queries.shape
    kvh = key_cache.shape[1]
    cache_local = key_cache.shape[2]
    share = residual_in.shape[0]
    width = residual_in.shape[1]
    expert_total = dp * tensor

    query_norm = rms_scale(queries.astype(F32), query_gain).astype(BF)
    key_norm = rms_scale(new_keys.astype(F32), key_gain).astype(BF)
    grouped = query_norm.reshape(rows, kvh, heads // kvh, hd)
    scaling = hd ** (-0.5)
    scores = jnp.einsum("rgqd,rgpd->rgqp", grouped, key_cache, preferred_element_type=F32) * scaling
    new_score = jnp.einsum("rgqd,rgd->rgq", grouped, key_norm, preferred_element_type=F32) * scaling
    positions = tensor_pos * cache_local + jnp.arange(cache_local, dtype=jnp.int32)
    included = (positions[None, :] < lengths[:, None])[:, None, None, :]
    top = jnp.maximum(jnp.max(jnp.where(included, scores, -1e30), axis=-1), new_score)
    top = top.astype(BF).astype(F32)
    weights = jnp.where(included, jnp.exp(scores - top[..., None]), 0.0).astype(BF)
    new_weight = jnp.exp(new_score - top).astype(BF).astype(F32)
    own_new = (tensor_pos == 0).astype(F32) * new_weight
    numer = jnp.einsum("rgqp,rgpd->rgqd", weights, value_cache, preferred_element_type=F32)
    numer = numer + own_new[..., None] * new_values.astype(F32)[:, :, None, :]
    denom = jnp.sum(weights.astype(F32), axis=-1) + own_new

    heads_own = heads // tensor
    numer = numer.reshape(rows, heads, hd).astype(BF)
    denom = denom.reshape(rows, heads)
    denom_hi = denom.astype(BF)
    denom_lo = (denom - denom_hi.astype(F32)).astype(BF)
    side = jnp.stack([top.reshape(rows, heads).astype(BF), denom_hi, denom_lo], axis=1)

    def for_device(j):
        first = (tensor_pos ^ j) * heads_own
        body = lax.dynamic_slice_in_dim(numer, first, heads_own, 1).reshape(rows, heads_own * hd)
        extra = lax.dynamic_slice_in_dim(side, first, heads_own, 2).reshape(rows, 3 * heads_own)
        extra = jnp.pad(extra, ((0, 0), (0, 128 - 3 * heads_own)))
        return jnp.concatenate([body, extra], axis=1)

    got = [for_device(0)] + [
        swap(for_device(j), "tensor", tensor, j) for j in range(1, tensor)
    ]
    got = jnp.stack(got).astype(F32)
    body = got[:, :, : heads_own * hd].reshape(tensor, rows, heads_own, hd)
    extra = got[:, :, heads_own * hd : heads_own * (hd + 3)].reshape(tensor, rows, 3, heads_own)
    tops = extra[:, :, 0]
    factor = jnp.exp(tops - jnp.max(tops, axis=0, keepdims=True))
    denom_all = jnp.sum(factor * (extra[:, :, 1] + extra[:, :, 2]), axis=0)
    attn = jnp.sum(body * factor[..., None], axis=0) / denom_all[..., None]
    attn = attn.reshape(rows, heads_own * hd).astype(BF)

    attn = jnp.concatenate(
        [
            lax.dynamic_slice_in_dim(attn, (tensor_pos ^ j) * share, share, 0)
            for j in range(tensor)
        ]
    )
    partial = jnp.dot(attn, out_proj, preferred_element_type=F32)
    projected = partial[:share]
    sent = partial.astype(BF)
    for j in range(1, tensor):
        projected = projected + swap(
            sent[j * share : (j + 1) * share], "tensor", tensor, j
        ).astype(F32)
    hidden = residual_in.astype(F32) + projected
    normed = rms_scale(hidden, norm_gain).astype(BF)

    route = (gate_weights / jnp.sum(gate_weights, axis=1, keepdims=True)).astype(BF)
    named = expert_ids[:, :, None] == jnp.arange(expert_total, dtype=jnp.int32)
    table = jnp.sum(jnp.where(named, route[:, :, None], jnp.zeros((), BF)), axis=1)
    table = jnp.pad(table, ((0, 0), (0, -expert_total % 128)))

    third = (width // 3) // 128 * 128
    cuts = [0, third, 2 * third, width]
    pieces = [normed[:, cuts[i] : cuts[i + 1]] for i in range(3)]
    pieces[0] = jnp.concatenate([pieces[0], table], axis=1)
    orders = ["zxyc", "xyzc", "yzxc"]
    gathered = [
        gather(plan, piece.reshape(1, 1, 1, 1, *piece.shape), order)
        for piece, order in zip(pieces, orders)
    ]
    total_rows = expert_total * share
    flat = [g.reshape(total_rows, g.shape[-1]) for g in gathered]
    every = jnp.concatenate([flat[0][:, :third], flat[1], flat[2]], axis=1)
    own = dp_pos * tensor + tensor_pos
    tables = flat[0][:, third:].astype(F32)
    mine = jnp.sum(
        jnp.where(jnp.arange(tables.shape[1], dtype=jnp.int32) == own, tables, 0.0),
        axis=1,
        keepdims=True,
    )
    gate_val = jnp.dot(every, expert_gate[0], preferred_element_type=F32)
    up_val = jnp.dot(every, expert_up[0], preferred_element_type=F32)
    activation = (jax.nn.silu(gate_val) * up_val).astype(BF)
    result = jnp.dot(activation, expert_down[0], preferred_element_type=F32)
    result = jnp.where(mine == 0.0, 0.0, result * mine)
    result = result.reshape(*[plan.length(n) for n in NAMES], share, width)
    first = reduce_slots(plan, result, "c")
    outs = []
    for i, order in enumerate(["yxz", "zyx", "xzy"]):
        outs.append(reduce_slots(plan, first[..., cuts[i] : cuts[i + 1]], order))
    moe_sum = jnp.concatenate(outs, axis=-1).reshape(share, width)
    return (hidden + moe_sum).astype(BF)


def solution(mesh):
    return jax.shard_map(
        shards,
        mesh=mesh,
        in_specs=(
            P("dp", None, None),
            P("dp", None, None),
            P("dp", None, None),
            P("dp", None, "tensor", None),
            P("dp", None, "tensor", None),
            P("dp"),
            P(("dp", "tensor"), None),
            P(),
            P(),
            P("tensor", None),
            P(),
            P(("dp", "tensor"), None),
            P(("dp", "tensor"), None),
            P(("dp", "tensor"), None, None),
            P(("dp", "tensor"), None, None),
            P(("dp", "tensor"), None, None),
        ),
        out_specs=P(("dp", "tensor"), None),
        check_vma=False,
    )
```

```python
import functools

import jax
import jax.numpy as jnp
from jax import lax
from jax.experimental import pallas as pl
from jax.experimental.pallas import tpu as pltpu
from jax.sharding import PartitionSpec as P

BF = jnp.bfloat16
F32 = jnp.float32
I32 = jnp.int32
MIB = 1 << 20
LANES = 128


def rms_scale(values, gain):
    mean_sq = jnp.mean(values * values, axis=-1, keepdims=True)
    return values * lax.rsqrt(mean_sq + 1e-06) * gain


def matmul(a, b):
    return jnp.dot(a, b, preferred_element_type=F32)


def matmul_t(a, b):
    return lax.dot_general(a, b, (((1,), (1,)), ((), ())), preferred_element_type=F32)


def iota(shape, dim):
    return lax.broadcasted_iota(I32, shape, dim)


def attention_kernel(
    lengths, q_ref, nk_ref, nv_ref, k_ref, v_ref, qg_ref, kg_ref, out_ref, nk_scr, nv_scr, num, stat
):
    tensor_pos = lax.axis_index("tensor")
    rows, heads, hd = q_ref.shape
    kvh, cache = k_ref.shape[1], k_ref.shape[2]
    group = heads // kvh
    parts = out_ref.shape[0]
    heads_own = heads // parts
    step = 4
    many, cols = step * heads, step * kvh * cache
    scaling = hd ** (-0.5)
    query_gain, key_gain = qg_ref[...], kg_ref[...]
    for r in range(rows):
        nk_scr[r * kvh : (r + 1) * kvh, :] = rms_scale(nk_ref[r].astype(F32), key_gain)
        nv_scr[r * kvh : (r + 1) * kvh, :] = nv_ref[r].astype(F32)
    new_keys = nk_scr[...].astype(BF)
    new_values = nv_scr[...].astype(BF)
    own = jnp.where(tensor_pos == 0, 1.0, 0.0).astype(F32)

    row_group = iota((many, cols), 0) // group
    col = iota((many, cols), 1)
    same = row_group == col // cache
    col_row = iota((1, cols), 1) // (kvh * cache)
    col_pos = iota((1, cols), 1) % cache + tensor_pos * cache
    new_col = iota((many, rows * kvh), 1)
    new_row = iota((many, rows * kvh), 0) // group
    lane = iota((many, LANES), 1)

    for b in range(rows // step):
        first = b * step
        query = q_ref[first : first + step].reshape(many, hd).astype(F32)
        query = rms_scale(query, query_gain).astype(BF)
        keys = k_ref[first : first + step].reshape(cols, hd)
        values = v_ref[first : first + step].reshape(cols, hd)
        limit = jnp.zeros((1, cols), I32)
        for i in range(step):
            limit = jnp.where(col_row == i, lengths[first + i], limit)
        included = same & (col_pos < limit)
        scores = matmul_t(query, keys) * scaling
        new_here = new_col == new_row + first * kvh
        new_score = jnp.sum(
            jnp.where(new_here, matmul_t(query, new_keys) * scaling, 0.0), axis=1, keepdims=True
        )
        top = jnp.max(jnp.where(included, scores, -1e30), axis=1, keepdims=True)
        top = jnp.maximum(top, new_score).astype(BF).astype(F32)
        weights = jnp.where(included, jnp.exp(scores - top), 0.0).astype(BF)
        new_weight = jnp.exp(new_score - top).astype(BF).astype(F32) * own
        total = jnp.sum(weights.astype(F32), axis=1, keepdims=True) + new_weight
        new_weights = jnp.where(new_here, new_weight, 0.0).astype(BF)
        num[b * many : (b + 1) * many, :] = matmul(weights, values) + matmul(
            new_weights, new_values
        )
        stat[b * many : (b + 1) * many, :] = jnp.where(lane == 0, top, total)

    lane = iota((rows, LANES), 1)
    for t in range(parts):
        side = jnp.zeros((rows, LANES), F32)
        for h in range(heads_own):
            which = pl.ds(t * heads_own + h, rows, stride=heads)
            out_ref[t, :, h * hd : (h + 1) * hd] = num[which, :].astype(BF)
            stats = stat[which, :]
            top, total = stats[:, 0:1], stats[:, 1:2]
            high = total.astype(BF).astype(F32)
            side = jnp.where(lane == h, top, side)
            side = jnp.where(lane == heads_own + h, high, side)
            side = jnp.where(lane == 2 * heads_own + h, total - high, side)
        out_ref[t, :, heads_own * hd :] = side.astype(BF)


def attention(lengths, queries, new_keys, new_values, key_cache, value_cache, qg, kg, parts):
    rows, heads, hd = queries.shape
    kvh = key_cache.shape[1]
    vmem = pl.BlockSpec(memory_space=pltpu.VMEM)
    return pl.pallas_call(
        attention_kernel,
        out_shape=jax.ShapeDtypeStruct((parts, rows, heads // parts * hd + LANES), BF),
        in_specs=[pl.BlockSpec(memory_space=pltpu.SMEM)] + [vmem] * 7,
        out_specs=vmem,
        scratch_shapes=[
            pltpu.VMEM((rows * kvh, hd), F32),
            pltpu.VMEM((rows * kvh, hd), F32),
            pltpu.VMEM((rows * heads, hd), F32),
            pltpu.VMEM((rows * heads, LANES), F32),
        ],
        compiler_params=pltpu.CompilerParams(vmem_limit_bytes=24 * MIB),
        name="attention",
    )(
        lengths,
        queries,
        new_keys,
        new_values,
        key_cache,
        value_cache,
        qg.reshape(1, -1),
        kg.reshape(1, -1),
    )


def projection_kernel(chunks, got_ref, w_hbm, out_ref, w_scr, attn, sem):
    parts, rows, _ = got_ref.shape
    depth, width = w_hbm.shape
    hd = LANES
    heads_own = depth // hd
    size = width // chunks

    def copy(i):
        cols = pl.ds(i * size, size)
        return pltpu.make_async_copy(w_hbm.at[:, cols], w_scr.at[:, cols], sem.at[i])

    for i in range(chunks):
        copy(i).start()
    sides = [got_ref[t, :, depth:].astype(F32) for t in range(parts)]
    tops = [s[:, :heads_own] for s in sides]
    top = functools.reduce(jnp.maximum, tops)
    factors = [jnp.exp(t - top) for t in tops]
    totals = [
        f * (s[:, heads_own : 2 * heads_own] + s[:, 2 * heads_own : 3 * heads_own])
        for f, s in zip(factors, sides)
    ]
    total = functools.reduce(jnp.add, totals)
    factors = [f / total for f in factors]
    for h in range(heads_own):
        cols = slice(h * hd, (h + 1) * hd)
        terms = [
            got_ref[t, :, cols].astype(F32) * factors[t][:, h : h + 1] for t in range(parts)
        ]
        attn[:, cols] = functools.reduce(jnp.add, terms).astype(BF)
    for i in range(chunks):
        copy(i).wait()
        cols = slice(i * size, (i + 1) * size)
        out_ref[:, cols] = matmul(attn[...], w_scr[:, cols]).astype(BF)


def projection(got, out_proj):
    rows = got.shape[1]
    depth, width = out_proj.shape
    chunks = 8
    return pl.pallas_call(
        functools.partial(projection_kernel, chunks),
        out_shape=jax.ShapeDtypeStruct((rows, width), BF),
        in_specs=[pl.BlockSpec(memory_space=pltpu.VMEM), pl.BlockSpec(memory_space=pl.ANY)],
        out_specs=pl.BlockSpec(memory_space=pltpu.VMEM),
        scratch_shapes=[
            pltpu.VMEM((depth, width), BF),
            pltpu.VMEM((rows, depth), BF),
            pltpu.SemaphoreType.DMA((chunks,)),
        ],
        compiler_params=pltpu.CompilerParams(vmem_limit_bytes=24 * MIB),
        name="projection",
    )(got, out_proj)


def expert_kernel(
    c0, c1, gate_hbm, up_hbm, down_hbm, kept, sent, x, table, gate, up, down, act, sem, wsem
):
    own = lax.axis_index("dp") * lax.axis_size("tensor") + lax.axis_index("tensor")
    half = c0.shape[0]
    _, width, hidden = gate_hbm.shape
    fsize = 256
    fchunks = hidden // fsize
    dsize = 1024
    dchunks = width // dsize

    def rows_copies():
        copies = []
        for i, ref in enumerate((c0, c1)):
            rows = pl.ds(i * half, half)
            copies.append(
                pltpu.make_async_copy(ref.at[:, pl.ds(0, width)], x.at[rows], sem.at[2 * i])
            )
            copies.append(
                pltpu.make_async_copy(
                    ref.at[:, pl.ds(width, table.shape[1])], table.at[rows], sem.at[2 * i + 1]
                )
            )
        return copies

    def up_copies(i):
        cols = pl.ds(i * fsize, fsize)
        return [
            pltpu.make_async_copy(gate_hbm.at[0, :, cols], gate.at[:, cols], wsem.at[2 * i]),
            pltpu.make_async_copy(up_hbm.at[0, :, cols], up.at[:, cols], wsem.at[2 * i + 1]),
        ]

    def down_copy(i):
        cols = pl.ds(i * dsize, dsize)
        return pltpu.make_async_copy(
            down_hbm.at[0, :, cols], down.at[:, cols], wsem.at[2 * fchunks + i]
        )

    for c in rows_copies():
        c.start()
    for i in range(fchunks):
        for c in up_copies(i):
            c.start()
    for i in range(dchunks):
        down_copy(i).start()
    for c in rows_copies():
        c.wait()
    tables = table[...].astype(F32)
    weight = jnp.sum(jnp.where(iota(tables.shape, 1) == own, tables, 0.0), axis=1, keepdims=True)
    for i in range(fchunks):
        for c in up_copies(i):
            c.wait()
        cols = slice(i * fsize, (i + 1) * fsize)
        g = matmul(x[...], gate[:, cols])
        u = matmul(x[...], up[:, cols])
        act[:, cols] = (g / (1.0 + jnp.exp(-g)) * u).astype(BF)
    for i in range(dchunks):
        down_copy(i).wait()
        cols = slice(i * dsize, (i + 1) * dsize)
        result = matmul(act[...], down[:, cols])
        result = jnp.where(weight == 0.0, 0.0, result * weight).astype(BF)
        kept[:, cols] = result[:half]
        sent[:, cols] = result[half:]


def experts(c0, c1, expert_gate, expert_up, expert_down):
    half, whole_width = c0.shape
    _, width, hidden = expert_gate.shape
    out = jax.ShapeDtypeStruct((half, width), BF)
    any_space = pl.BlockSpec(memory_space=pl.ANY)
    vmem = pl.BlockSpec(memory_space=pltpu.VMEM)
    return pl.pallas_call(
        expert_kernel,
        out_shape=(out, out),
        in_specs=[any_space] * 5,
        out_specs=(vmem, vmem),
        scratch_shapes=[
            pltpu.VMEM((2 * half, width), BF),
            pltpu.VMEM((2 * half, whole_width - width), BF),
            pltpu.VMEM((width, hidden), BF),
            pltpu.VMEM((width, hidden), BF),
            pltpu.VMEM((hidden, width), BF),
            pltpu.VMEM((2 * half, hidden), BF),
            pltpu.SemaphoreType.DMA((4,)),
            pltpu.SemaphoreType.DMA((2 * hidden // 256 + width // 1024,)),
        ],
        compiler_params=pltpu.CompilerParams(vmem_limit_bytes=48 * MIB),
        name="experts",
    )(c0, c1, expert_gate, expert_up, expert_down)


class Plan:
    def __init__(self, dp, tensor):
        self.zlen = min(4, dp)
        xlen = dp // self.zlen
        self.axes = {
            "x": ("dp", dp, 1, xlen),
            "y": ("tensor", tensor, 2, tensor // 2),
            "c": ("tensor", tensor, 1, 2),
        }
        self.zgroups = [[z * xlen + x for z in range(self.zlen)] for x in range(xlen)]

    def length(self, name):
        return self.axes[name][3]

    def swap(self, value, name, j):
        axis, size, step, _ = self.axes[name]
        return lax.ppermute(value, axis, [(i, i ^ (j * step)) for i in range(size)])

    def trade_z(self, value):
        return lax.all_to_all(
            value, "dp", split_axis=0, concat_axis=0, axis_index_groups=self.zgroups, tiled=True
        )

    def gather(self, value, name, dim):
        return jnp.concatenate(
            [value] + [self.swap(value, name, j) for j in range(1, self.length(name))], axis=dim
        )

    def reduce(self, value, name, dim):
        parts = [lax.slice_in_dim(value, j, j + 1, axis=dim) for j in range(self.length(name))]
        total = parts[0].astype(F32)
        for j in range(1, self.length(name)):
            total = total + self.swap(parts[j].astype(BF), name, j).astype(F32)
        return total


def shards(
    queries,
    new_keys,
    new_values,
    key_cache,
    value_cache,
    lengths,
    residual_in,
    query_gain,
    key_gain,
    out_proj,
    norm_gain,
    expert_ids,
    gate_weights,
    expert_gate,
    expert_up,
    expert_down,
):
    tensor = lax.axis_size("tensor")
    dp = lax.axis_size("dp")
    plan = Plan(dp, tensor)
    share, width = residual_in.shape
    expert_total = dp * tensor
    zlen, xlen, ylen = plan.zlen, plan.length("x"), plan.length("y")

    route = (gate_weights / jnp.sum(gate_weights, axis=1, keepdims=True)).astype(BF)
    named = expert_ids[:, :, None] == jnp.arange(expert_total, dtype=I32)
    table = jnp.sum(jnp.where(named, route[:, :, None], jnp.zeros((), BF)), axis=1)
    table = jnp.pad(table, ((0, 0), (0, -expert_total % LANES)))

    local = attention(
        lengths, queries, new_keys, new_values, key_cache, value_cache, query_gain, key_gain, tensor
    )
    got = lax.all_to_all(local, "tensor", split_axis=0, concat_axis=0, tiled=True)
    partial = projection(got, out_proj)
    sums = lax.all_to_all(partial, "tensor", split_axis=0, concat_axis=0, tiled=True)
    projected = jnp.sum(sums.reshape(tensor, share, width).astype(F32), axis=0)
    hidden = residual_in.astype(F32) + projected
    normed = rms_scale(hidden, norm_gain).astype(BF)

    full = jnp.concatenate([normed, table], axis=1)
    every_z = plan.trade_z(jnp.broadcast_to(full, (zlen, *full.shape)))
    every_z = every_z.reshape(zlen, 1, 1, share, full.shape[1])
    middle = width // 2
    a = plan.gather(every_z[..., :middle], "x", 1)
    b = plan.gather(every_z[..., middle:], "y", 2)
    a = plan.gather(a, "y", 2)
    b = plan.gather(b, "x", 1)
    c0 = jnp.concatenate([a, b], axis=-1).reshape(zlen * xlen * ylen * share, full.shape[1])
    c1 = plan.swap(c0, "c", 1)

    kept, sent = experts(c0, c1, expert_gate, expert_up, expert_down)
    total = kept.astype(F32) + plan.swap(sent, "c", 1).astype(F32)
    total = total.reshape(zlen, xlen, ylen, share, width)
    a = plan.reduce(total[..., :middle], "y", 2)
    b = plan.reduce(total[..., middle:], "x", 1)
    a = plan.reduce(a, "x", 1)
    b = plan.reduce(b, "y", 2)
    total = jnp.concatenate([a.astype(BF), b.astype(BF)], axis=-1).reshape(zlen, share, width)
    moe_sum = jnp.sum(plan.trade_z(total).astype(F32), axis=0)
    return (hidden + moe_sum).astype(BF)


def solution(mesh):
    return jax.shard_map(
        shards,
        mesh=mesh,
        in_specs=(
            P("dp", None, None),
            P("dp", None, None),
            P("dp", None, None),
            P("dp", None, "tensor", None),
            P("dp", None, "tensor", None),
            P("dp"),
            P(("dp", "tensor"), None),
            P(),
            P(),
            P("tensor", None),
            P(),
            P(("dp", "tensor"), None),
            P(("dp", "tensor"), None),
            P(("dp", "tensor"), None, None),
            P(("dp", "tensor"), None, None),
            P(("dp", "tensor"), None, None),
        ),
        out_specs=P(("dp", "tensor"), None),
        check_vma=False,
    )
```

```python
import functools

import jax
import jax.numpy as jnp
from jax import lax
from jax.experimental import pallas as pl
from jax.experimental.pallas import tpu as pltpu
from jax.sharding import PartitionSpec as P

BF = jnp.bfloat16
F32 = jnp.float32
I32 = jnp.int32
MIB = 1 << 20
LANES = 128


def rms_scale(values, gain):
    mean_sq = jnp.mean(values * values, axis=-1, keepdims=True)
    return values * lax.rsqrt(mean_sq + 1e-06) * gain


def matmul(a, b):
    return jnp.dot(a, b, preferred_element_type=F32)


def matmul_t(a, b):
    return lax.dot_general(a, b, (((1,), (1,)), ((), ())), preferred_element_type=F32)


def iota(shape, dim):
    return lax.broadcasted_iota(I32, shape, dim)


def in_hbm(value):
    return pltpu.with_memory_space_constraint(value, pltpu.HBM)


def attention_kernel(
    len_hbm,
    q_hbm,
    nk_hbm,
    nv_hbm,
    k_hbm,
    v_hbm,
    qg_hbm,
    kg_hbm,
    ids_hbm,
    gates_hbm,
    w0_hbm,
    w1_hbm,
    out_ref,
    table_ref,
    w0_ref,
    w1_ref,
    lengths,
    q_ref,
    nk_ref,
    nv_ref,
    k_ref,
    v_ref,
    qg_ref,
    kg_ref,
    ids_ref,
    gates_ref,
    nk_scr,
    nv_scr,
    num,
    tops,
    totals,
    sem,
):
    sources = (len_hbm, nk_hbm, nv_hbm, qg_hbm, kg_hbm, ids_hbm, gates_hbm, q_hbm, k_hbm, v_hbm)
    targets = (lengths, nk_ref, nv_ref, qg_ref, kg_ref, ids_ref, gates_ref, q_ref, k_ref, v_ref)
    copies = [
        pltpu.make_async_copy(a, b, sem.at[i]) for i, (a, b) in enumerate(zip(sources, targets))
    ]
    ahead = [
        pltpu.make_async_copy(w0_hbm, w0_ref, sem.at[10]),
        pltpu.make_async_copy(w1_hbm, w1_ref, sem.at[11]),
    ]
    for c in copies + ahead:
        c.start()
    tensor_pos = lax.axis_index("tensor")
    rows, heads, hd = q_ref.shape
    kvh, cache = k_ref.shape[1], k_ref.shape[2]
    group = heads // kvh
    parts = out_ref.shape[0]
    heads_own = heads // parts
    step = 4
    many, cols = step * heads, step * kvh * cache
    scaling = hd ** (-0.5)
    own = jnp.where(tensor_pos == 0, 1.0, 0.0).astype(F32)

    row_group = iota((many, cols), 0) // group
    col = iota((many, cols), 1)
    same = row_group == col // cache
    col_row = iota((1, cols), 1) // (kvh * cache)
    col_pos = iota((1, cols), 1) % cache + tensor_pos * cache
    new_col = iota((many, rows * kvh), 1)
    new_row = iota((many, rows * kvh), 0) // group

    for c in copies[:7]:
        c.wait()
    gates = gates_ref[...]
    route = (gates / jnp.sum(gates, axis=1, keepdims=True)).astype(BF).astype(F32)
    expert = iota(table_ref.shape, 1)
    table = jnp.zeros(table_ref.shape, F32)
    for k in range(gates.shape[1]):
        table = jnp.where(expert == ids_ref[:, k : k + 1], route[:, k : k + 1], table)
    table_ref[...] = table.astype(BF)
    for r in range(rows):
        nk_scr[r * kvh : (r + 1) * kvh, :] = nk_ref[r].astype(F32)
        nv_scr[r * kvh : (r + 1) * kvh, :] = nv_ref[r].astype(F32)
    query_gain = qg_ref[...]
    new_keys = rms_scale(nk_scr[...], kg_ref[...]).astype(BF)
    new_values = nv_scr[...].astype(BF)
    for c in copies[7:]:
        c.wait()

    for b in range(rows // step):
        first = b * step
        query = q_ref[first : first + step].reshape(many, hd).astype(F32)
        query = rms_scale(query, query_gain).astype(BF)
        keys = k_ref[first : first + step].reshape(cols, hd)
        values = v_ref[first : first + step].reshape(cols, hd)
        limit = jnp.zeros((1, cols), I32)
        for i in range(step):
            limit = jnp.where(col_row == i, lengths[first + i], limit)
        included = same & (col_pos < limit)
        scores = matmul_t(query, keys) * scaling
        new_here = new_col == new_row + first * kvh
        new_score = jnp.sum(
            jnp.where(new_here, matmul_t(query, new_keys) * scaling, 0.0), axis=1, keepdims=True
        )
        top = jnp.max(jnp.where(included, scores, -1e30), axis=1, keepdims=True)
        top = jnp.maximum(top, new_score).astype(BF).astype(F32)
        weights = jnp.where(included, jnp.exp(scores - top), 0.0).astype(BF)
        new_weight = jnp.exp(new_score - top).astype(BF).astype(F32) * own
        total = jnp.sum(weights.astype(F32), axis=1, keepdims=True) + new_weight
        new_weights = jnp.where(new_here, new_weight, 0.0).astype(BF)
        block = slice(b * many, (b + 1) * many)
        num[block, :] = matmul(weights, values) + matmul(new_weights, new_values)
        tops[block, :] = jnp.broadcast_to(top, (many, LANES))
        totals[block, :] = jnp.broadcast_to(total, (many, LANES))

    lane = iota((rows, LANES), 1)
    for t in range(parts):
        slot = tensor_pos ^ t
        side = jnp.zeros((rows, LANES), F32)
        for h in range(heads_own):
            which = pl.ds(t * heads_own + h, rows, stride=heads)
            out_ref[slot, :, h * hd : (h + 1) * hd] = num[which, :].astype(BF)
            total = totals[which, :]
            high = total.astype(BF).astype(F32)
            side = jnp.where(lane == h, tops[which, :], side)
            side = jnp.where(lane == heads_own + h, high, side)
            side = jnp.where(lane == 2 * heads_own + h, total - high, side)
        out_ref[slot, :, heads_own * hd :] = side.astype(BF)
    for c in ahead:
        c.wait()


def attention(
    lengths,
    queries,
    new_keys,
    new_values,
    key_cache,
    value_cache,
    qg,
    kg,
    expert_ids,
    gate_weights,
    parts,
    lanes,
    weights,
):
    rows, heads, hd = queries.shape
    kvh = key_cache.shape[1]
    args = (
        lengths,
        queries,
        new_keys,
        new_values,
        key_cache,
        value_cache,
        qg.reshape(1, -1),
        kg.reshape(1, -1),
        expert_ids,
        gate_weights,
    )
    return pl.pallas_call(
        attention_kernel,
        out_shape=(
            jax.ShapeDtypeStruct((parts, rows, heads // parts * hd + LANES), BF),
            jax.ShapeDtypeStruct((expert_ids.shape[0], lanes), BF),
            *[pltpu.VMEM(w.shape, w.dtype) for w in weights],
        ),
        in_specs=[pl.BlockSpec(memory_space=pltpu.HBM)] * 12,
        out_specs=(pl.BlockSpec(memory_space=pltpu.VMEM),) * 4,
        scratch_shapes=[pltpu.SMEM(args[0].shape, I32)]
        + [pltpu.VMEM(a.shape, a.dtype) for a in args[1:]]
        + [
            pltpu.VMEM((rows * kvh, hd), F32),
            pltpu.VMEM((rows * kvh, hd), F32),
            pltpu.VMEM((rows * heads, hd), F32),
            pltpu.VMEM((rows * heads, LANES), F32),
            pltpu.VMEM((rows * heads, LANES), F32),
            pltpu.SemaphoreType.DMA((12,)),
        ],
        compiler_params=pltpu.CompilerParams(vmem_limit_bytes=16 * MIB),
        name="attention",
    )(*[in_hbm(a) for a in (*args, *weights)])


def projection_kernel(parts, *refs):
    got = refs[:parts]
    w_ref, ahead_hbm, out_ref, ahead_ref, attn, sem = refs[parts:]
    ahead = pltpu.make_async_copy(ahead_hbm, ahead_ref, sem)
    ahead.start()
    tensor_pos = lax.axis_index("tensor")
    depth, width = w_ref.shape
    share = out_ref.shape[2]
    hd = LANES
    heads_own = depth // hd
    size = 512
    sides = [g[:, depth:].astype(F32) for g in got]
    tops = [s[:, :heads_own] for s in sides]
    top = functools.reduce(jnp.maximum, tops)
    factors = [jnp.exp(t - top) for t in tops]
    totals = [
        f * (s[:, heads_own : 2 * heads_own] + s[:, 2 * heads_own : 3 * heads_own])
        for f, s in zip(factors, sides)
    ]
    total = functools.reduce(jnp.add, totals)
    factors = [f / total for f in factors]
    for h in range(heads_own):
        cols = slice(h * hd, (h + 1) * hd)
        terms = [g[:, cols].astype(F32) * f[:, h : h + 1] for g, f in zip(got, factors)]
        attn[:, cols] = functools.reduce(jnp.add, terms).astype(BF)
    for i in range(width // size):
        cols = slice(i * size, (i + 1) * size)
        result = matmul(attn[...], w_ref[:, cols])
        for t in range(parts):
            slot = tensor_pos ^ t
            out_ref[slot & 1, slot >> 1, :, cols] = result[t * share : (t + 1) * share].astype(BF)
    ahead.wait()


def projection(got, out_proj, share, weight):
    parts = len(got)
    rows = got[0].shape[0]
    depth, width = out_proj.shape
    vmem = pl.BlockSpec(memory_space=pltpu.VMEM)
    return pl.pallas_call(
        functools.partial(projection_kernel, parts),
        out_shape=(
            jax.ShapeDtypeStruct((2, parts // 2, share, width), BF),
            pltpu.VMEM(weight.shape, weight.dtype),
        ),
        in_specs=[vmem] * (parts + 1) + [pl.BlockSpec(memory_space=pltpu.HBM)],
        out_specs=(vmem, vmem),
        scratch_shapes=[pltpu.VMEM((rows, depth), BF), pltpu.SemaphoreType.DMA],
        compiler_params=pltpu.CompilerParams(vmem_limit_bytes=12 * MIB),
        name="projection",
    )(*got, out_proj, in_hbm(weight))


def expert_kernel(xlen, ylen, *refs):
    count = 2 * (xlen + ylen)
    pieces = refs[:count]
    gate, up, down_hbm = refs[count : count + 3]
    outs = refs[count + 3 : 2 * count + 3]
    x, table, down, act, sem = refs[2 * count + 3 :]
    own = lax.axis_index("dp") * lax.axis_size("tensor") + lax.axis_index("tensor")
    block = x.shape[0] // (2 * xlen * ylen)
    _, width, hidden = gate.shape
    middle = width // 2
    fsize = 256
    dsize = 1024
    dchunks = width // dsize

    def down_copy(i):
        cols = pl.ds(i * dsize, dsize)
        return pltpu.make_async_copy(down_hbm.at[0, :, cols], down.at[:, cols], sem.at[i])

    halves = ([], [])
    for core in range(2):
        for iy in range(ylen):
            for ix in range(xlen):
                row = ((core * ylen + iy) * xlen + ix) * block
                first = core * (xlen + ylen)
                halves[0].append((first + iy, ix * block, row))
                halves[1].append((first + ylen + ix, iy * block, row))

    for i in range(dchunks):
        down_copy(i).start()
    for i, row, there in halves[0]:
        x[there : there + block, :middle] = pieces[i][row : row + block, :]
    for i, row, there in halves[1]:
        x[there : there + block, middle:] = pieces[i][row : row + block, :middle]
        table[there : there + block, :] = pieces[i][row : row + block, middle:]
    tables = table[...].astype(F32)
    weight = jnp.sum(jnp.where(iota(tables.shape, 1) == own, tables, 0.0), axis=1, keepdims=True)
    for i in range(hidden // fsize):
        cols = slice(i * fsize, (i + 1) * fsize)
        g = matmul(x[...], gate[0, :, cols])
        u = matmul(x[...], up[0, :, cols])
        act[:, cols] = (g / (1.0 + jnp.exp(-g)) * u).astype(BF)
    for i in range(dchunks):
        down_copy(i).wait()
        result = matmul(act[...], down[:, i * dsize : (i + 1) * dsize])
        result = jnp.where(weight == 0.0, 0.0, result * weight).astype(BF)
        half, start = divmod(i * dsize, middle)
        for k, row, there in halves[half]:
            outs[k][row : row + block, start : start + dsize] = result[there : there + block]


def experts(pieces, expert_gate, expert_up, expert_down, xlen, ylen):
    count = len(pieces)
    _, width, hidden = expert_gate.shape
    middle = width // 2
    vmem = pl.BlockSpec(memory_space=pltpu.VMEM)
    every = 2 * ylen * pieces[0].shape[0]
    lanes = pieces[-1].shape[1] - middle
    return pl.pallas_call(
        functools.partial(expert_kernel, xlen, ylen),
        out_shape=tuple(jax.ShapeDtypeStruct((p.shape[0], middle), BF) for p in pieces),
        in_specs=[vmem] * (count + 2) + [pl.BlockSpec(memory_space=pltpu.HBM)],
        out_specs=(vmem,) * count,
        scratch_shapes=[
            pltpu.VMEM((every, width), BF),
            pltpu.VMEM((every, lanes), BF),
            pltpu.VMEM((hidden, width), BF),
            pltpu.VMEM((every, hidden), BF),
            pltpu.SemaphoreType.DMA((width // 1024,)),
        ],
        compiler_params=pltpu.CompilerParams(vmem_limit_bytes=(16 + every // 32) * MIB),
        name="experts",
    )(*pieces, expert_gate, expert_up, in_hbm(expert_down))


class Plan:
    def __init__(self, dp, tensor):
        self.z = min(4, dp)
        self.x = dp // self.z
        self.y = tensor // 2
        self.count = dp * tensor
        self.flip = {"c": 1, "y": 2, "x": tensor, "z": tensor * self.x}
        self.length = {"c": 2, "y": self.y, "x": self.x, "z": self.z}

    def swap(self, value, name, j=1):
        flip = j * self.flip[name]
        return lax.ppermute(value, ("dp", "tensor"), [(i, i ^ flip) for i in range(self.count)])

    def gather(self, value, name):
        far_first = [self.swap(value, name, j) for j in reversed(range(1, self.length[name]))]
        return far_first[::-1]

    def reduce(self, values, name):
        far_first = [
            self.swap(values[j].astype(BF), name, j) for j in reversed(range(1, len(values)))
        ]
        return total_of([values[0]] + far_first)


def total_of(values):
    return functools.reduce(jnp.add, [v.astype(F32) for v in values])


def shards(
    queries,
    new_keys,
    new_values,
    key_cache,
    value_cache,
    lengths,
    residual_in,
    query_gain,
    key_gain,
    out_proj,
    norm_gain,
    expert_ids,
    gate_weights,
    expert_gate,
    expert_up,
    expert_down,
):
    tensor = lax.axis_size("tensor")
    dp = lax.axis_size("dp")
    plan = Plan(dp, tensor)
    share, width = residual_in.shape
    middle = width // 2
    lanes = -(-dp * tensor // LANES) * LANES

    local, table, out_proj, expert_gate = attention(
        lengths,
        queries,
        new_keys,
        new_values,
        key_cache,
        value_cache,
        query_gain,
        key_gain,
        expert_ids,
        gate_weights,
        tensor,
        lanes,
        (out_proj, expert_gate),
    )
    got = [plan.swap(local[j], "c", j) for j in reversed(range(1, tensor))]
    got = [local[0]] + got[::-1]
    partial, expert_up = projection(got, out_proj, share, expert_up)
    pair = total_of([partial[0], plan.swap(partial[1], "c")])
    projected = plan.reduce(list(pair), "y")
    hidden = residual_in.astype(F32) + projected
    normed = rms_scale(hidden, norm_gain).astype(BF)

    mine = jnp.concatenate([normed, table], axis=1)
    column = jnp.concatenate([mine] + plan.gather(mine, "z"))
    halves = (column[:, :middle], column[:, middle:])
    orders = ("xy", "yx")
    early = [
        jnp.concatenate([half] + plan.gather(half, order[0]))
        for half, order in zip(halves, orders)
    ]
    pieces = []
    for half, order in zip(early, orders):
        pieces += [half] + plan.gather(half, order[1])
    pieces = pieces + [plan.swap(piece, "c") for piece in pieces]

    results = experts(pieces, expert_gate, expert_up, expert_down, plan.x, plan.y)

    half = len(results) // 2
    sums = [total_of([results[i], plan.swap(results[half + i], "c")]) for i in range(half)]
    halves = (sums[: plan.y], sums[plan.y :])
    early = [plan.reduce(half, order[1]) for half, order in zip(halves, orders)]
    column = [
        plan.reduce(list(half.reshape(-1, plan.z * share, middle)), order[0])
        for half, order in zip(early, orders)
    ]
    column = jnp.concatenate(column, axis=1).reshape(plan.z, share, width)
    moe_sum = plan.reduce(list(column), "z")
    return (hidden + moe_sum).astype(BF)


def solution(mesh):
    return jax.shard_map(
        shards,
        mesh=mesh,
        in_specs=(
            P("dp", None, None),
            P("dp", None, None),
            P("dp", None, None),
            P("dp", None, "tensor", None),
            P("dp", None, "tensor", None),
            P("dp"),
            P(("dp", "tensor"), None),
            P(),
            P(),
            P("tensor", None),
            P(),
            P(("dp", "tensor"), None),
            P(("dp", "tensor"), None),
            P(("dp", "tensor"), None, None),
            P(("dp", "tensor"), None, None),
            P(("dp", "tensor"), None, None),
        ),
        out_specs=P(("dp", "tensor"), None),
        check_vma=False,
    )
```

```python
import functools

import jax
import jax.numpy as jnp
from jax import lax
from jax.experimental import pallas as pl
from jax.experimental.pallas import tpu as pltpu
from jax.sharding import PartitionSpec as P

BF = jnp.bfloat16
F32 = jnp.float32
I32 = jnp.int32
MIB = 1 << 20
LANES = 128
CAP = 3


def rms_scale(values, gain):
    mean_sq = jnp.mean(values * values, axis=-1, keepdims=True)
    return values * lax.rsqrt(mean_sq + 1e-06) * gain


def matmul(a, b):
    return jnp.dot(a, b, preferred_element_type=F32)


def matmul_t(a, b):
    return lax.dot_general(a, b, (((1,), (1,)), ((), ())), preferred_element_type=F32)


def iota(shape, dim):
    return lax.broadcasted_iota(I32, shape, dim)


def in_hbm(value):
    return pltpu.with_memory_space_constraint(value, pltpu.HBM)


def attention_kernel(
    len_hbm,
    q_hbm,
    nk_hbm,
    nv_hbm,
    k_hbm,
    v_hbm,
    qg_hbm,
    kg_hbm,
    ids_hbm,
    gates_hbm,
    w0_hbm,
    w1_hbm,
    out_ref,
    table_ref,
    w0_ref,
    w1_ref,
    lengths,
    q_ref,
    nk_ref,
    nv_ref,
    k_ref,
    v_ref,
    qg_ref,
    kg_ref,
    ids_ref,
    gates_ref,
    nk_scr,
    nv_scr,
    num,
    tops,
    totals,
    sem,
):
    sources = (len_hbm, nk_hbm, nv_hbm, qg_hbm, kg_hbm, ids_hbm, gates_hbm, q_hbm, k_hbm, v_hbm)
    targets = (lengths, nk_ref, nv_ref, qg_ref, kg_ref, ids_ref, gates_ref, q_ref, k_ref, v_ref)
    copies = [
        pltpu.make_async_copy(a, b, sem.at[i]) for i, (a, b) in enumerate(zip(sources, targets))
    ]
    ahead = [
        pltpu.make_async_copy(w0_hbm, w0_ref, sem.at[10]),
        pltpu.make_async_copy(w1_hbm, w1_ref, sem.at[11]),
    ]
    for c in copies + ahead:
        c.start()
    tensor_pos = lax.axis_index("tensor")
    rows, heads, hd = q_ref.shape
    kvh, cache = k_ref.shape[1], k_ref.shape[2]
    group = heads // kvh
    parts = out_ref.shape[0]
    heads_own = heads // parts
    step = 4
    many, cols = step * heads, step * kvh * cache
    scaling = hd ** (-0.5)
    own = jnp.where(tensor_pos == 0, 1.0, 0.0).astype(F32)

    row_group = iota((many, cols), 0) // group
    col = iota((many, cols), 1)
    same = row_group == col // cache
    col_row = iota((1, cols), 1) // (kvh * cache)
    col_pos = iota((1, cols), 1) % cache + tensor_pos * cache
    new_col = iota((many, rows * kvh), 1)
    new_row = iota((many, rows * kvh), 0) // group

    for c in copies[:7]:
        c.wait()
    gates = gates_ref[...]
    route = (gates / jnp.sum(gates, axis=1, keepdims=True)).astype(BF).astype(F32)
    expert = iota(table_ref.shape, 1)
    table = jnp.zeros(table_ref.shape, F32)
    for k in range(gates.shape[1]):
        table = jnp.where(expert == ids_ref[:, k : k + 1], route[:, k : k + 1], table)
    table_ref[...] = table.astype(BF)
    for r in range(rows):
        nk_scr[r * kvh : (r + 1) * kvh, :] = nk_ref[r].astype(F32)
        nv_scr[r * kvh : (r + 1) * kvh, :] = nv_ref[r].astype(F32)
    query_gain = qg_ref[...]
    new_keys = rms_scale(nk_scr[...], kg_ref[...]).astype(BF)
    new_values = nv_scr[...].astype(BF)
    for c in copies[7:]:
        c.wait()

    for b in range(rows // step):
        first = b * step
        query = q_ref[first : first + step].reshape(many, hd).astype(F32)
        query = rms_scale(query, query_gain).astype(BF)
        keys = k_ref[first : first + step].reshape(cols, hd)
        values = v_ref[first : first + step].reshape(cols, hd)
        limit = jnp.zeros((1, cols), I32)
        for i in range(step):
            limit = jnp.where(col_row == i, lengths[first + i], limit)
        included = same & (col_pos < limit)
        scores = matmul_t(query, keys) * scaling
        new_here = new_col == new_row + first * kvh
        new_score = jnp.sum(
            jnp.where(new_here, matmul_t(query, new_keys) * scaling, 0.0), axis=1, keepdims=True
        )
        top = jnp.max(jnp.where(included, scores, -1e30), axis=1, keepdims=True)
        top = jnp.maximum(top, new_score).astype(BF).astype(F32)
        weights = jnp.where(included, jnp.exp(scores - top), 0.0).astype(BF)
        new_weight = jnp.exp(new_score - top).astype(BF).astype(F32) * own
        total = jnp.sum(weights.astype(F32), axis=1, keepdims=True) + new_weight
        new_weights = jnp.where(new_here, new_weight, 0.0).astype(BF)
        block = slice(b * many, (b + 1) * many)
        num[block, :] = matmul(weights, values) + matmul(new_weights, new_values)
        tops[block, :] = jnp.broadcast_to(top, (many, LANES))
        totals[block, :] = jnp.broadcast_to(total, (many, LANES))

    lane = iota((rows, LANES), 1)
    for t in range(parts):
        slot = tensor_pos ^ t
        side = jnp.zeros((rows, LANES), F32)
        for h in range(heads_own):
            which = pl.ds(t * heads_own + h, rows, stride=heads)
            out_ref[slot, :, h * hd : (h + 1) * hd] = num[which, :].astype(BF)
            total = totals[which, :]
            high = total.astype(BF).astype(F32)
            side = jnp.where(lane == h, tops[which, :], side)
            side = jnp.where(lane == heads_own + h, high, side)
            side = jnp.where(lane == 2 * heads_own + h, total - high, side)
        out_ref[slot, :, heads_own * hd :] = side.astype(BF)
    for c in ahead:
        c.wait()


def attention(
    lengths,
    queries,
    new_keys,
    new_values,
    key_cache,
    value_cache,
    qg,
    kg,
    expert_ids,
    gate_weights,
    parts,
    lanes,
    weights,
):
    rows, heads, hd = queries.shape
    kvh = key_cache.shape[1]
    args = (
        lengths,
        queries,
        new_keys,
        new_values,
        key_cache,
        value_cache,
        qg.reshape(1, -1),
        kg.reshape(1, -1),
        expert_ids,
        gate_weights,
    )
    return pl.pallas_call(
        attention_kernel,
        out_shape=(
            jax.ShapeDtypeStruct((parts, rows, heads // parts * hd + LANES), BF),
            jax.ShapeDtypeStruct((expert_ids.shape[0], lanes), BF),
            *[pltpu.VMEM(w.shape, w.dtype) for w in weights],
        ),
        in_specs=[pl.BlockSpec(memory_space=pltpu.HBM)] * 12,
        out_specs=(pl.BlockSpec(memory_space=pltpu.VMEM),) * 4,
        scratch_shapes=[pltpu.SMEM(args[0].shape, I32)]
        + [pltpu.VMEM(a.shape, a.dtype) for a in args[1:]]
        + [
            pltpu.VMEM((rows * kvh, hd), F32),
            pltpu.VMEM((rows * kvh, hd), F32),
            pltpu.VMEM((rows * heads, hd), F32),
            pltpu.VMEM((rows * heads, LANES), F32),
            pltpu.VMEM((rows * heads, LANES), F32),
            pltpu.SemaphoreType.DMA((12,)),
        ],
        compiler_params=pltpu.CompilerParams(vmem_limit_bytes=16 * MIB),
        name="attention",
    )(*[in_hbm(a) for a in (*args, *weights)])


def projection_kernel(parts, *refs):
    got = refs[:parts]
    w_ref, ahead_hbm, out_ref, ahead_ref, attn, sem = refs[parts:]
    ahead = pltpu.make_async_copy(ahead_hbm, ahead_ref, sem)
    ahead.start()
    tensor_pos = lax.axis_index("tensor")
    depth, width = w_ref.shape
    share = out_ref.shape[2]
    hd = LANES
    heads_own = depth // hd
    size = 512
    sides = [g[:, depth:].astype(F32) for g in got]
    tops = [s[:, :heads_own] for s in sides]
    top = functools.reduce(jnp.maximum, tops)
    factors = [jnp.exp(t - top) for t in tops]
    totals = [
        f * (s[:, heads_own : 2 * heads_own] + s[:, 2 * heads_own : 3 * heads_own])
        for f, s in zip(factors, sides)
    ]
    total = functools.reduce(jnp.add, totals)
    factors = [f / total for f in factors]
    for h in range(heads_own):
        cols = slice(h * hd, (h + 1) * hd)
        terms = [g[:, cols].astype(F32) * f[:, h : h + 1] for g, f in zip(got, factors)]
        attn[:, cols] = functools.reduce(jnp.add, terms).astype(BF)
    for i in range(width // size):
        cols = slice(i * size, (i + 1) * size)
        result = matmul(attn[...], w_ref[:, cols])
        for t in range(parts):
            slot = tensor_pos ^ t
            out_ref[slot & 1, slot >> 1, :, cols] = result[t * share : (t + 1) * share].astype(BF)
    ahead.wait()


def projection(got, out_proj, share, weight):
    parts = len(got)
    rows = got[0].shape[0]
    depth, width = out_proj.shape
    vmem = pl.BlockSpec(memory_space=pltpu.VMEM)
    return pl.pallas_call(
        functools.partial(projection_kernel, parts),
        out_shape=(
            jax.ShapeDtypeStruct((2, parts // 2, share, width), BF),
            pltpu.VMEM(weight.shape, weight.dtype),
        ),
        in_specs=[vmem] * (parts + 1) + [pl.BlockSpec(memory_space=pltpu.HBM)],
        out_specs=(vmem, vmem),
        scratch_shapes=[pltpu.VMEM((rows, depth), BF), pltpu.SemaphoreType.DMA],
        compiler_params=pltpu.CompilerParams(vmem_limit_bytes=12 * MIB),
        name="projection",
    )(*got, out_proj, in_hbm(weight))


def expert_kernel(slots, x_ref, gate, up, down_hbm, out_ref, down, xc, act, res, sem):
    own = lax.axis_index("dp") * lax.axis_size("tensor") + lax.axis_index("tensor")
    rows = x_ref.shape[0]
    _, width, hidden = gate.shape
    padded = res.shape[0]
    fsize = 256
    dsize = 1024
    chunks = width // dsize

    def down_copy(i):
        cols = pl.ds(i * dsize, dsize)
        return pltpu.make_async_copy(down_hbm.at[0, :, cols], down.at[:, cols], sem.at[i])

    for i in range(chunks):
        down_copy(i).start()
    table = x_ref[:, width:]
    pick = (iota((16, table.shape[1]), 1) == own).astype(F32).astype(BF)
    named = matmul_t(pick, table) != 0.0
    before = (iota((rows, rows), 0) < iota((rows, rows), 1)).astype(F32).astype(BF)
    place = matmul(named.astype(F32).astype(BF), before)
    place = jnp.where(named, place, -1.0)[:1]
    take = (iota((slots, rows), 0).astype(F32) == place).astype(F32).astype(BF)
    for i in range(chunks):
        cols = slice(i * dsize, (i + 1) * dsize)
        xc[:, cols] = matmul(take, x_ref[:, cols]).astype(BF)

    lane = iota(table.shape, 1)
    weight = jnp.sum(jnp.where(lane == own, table.astype(F32), 0.0), axis=1, keepdims=True)
    named = jnp.broadcast_to((weight != 0.0).astype(F32), (rows, LANES)).astype(BF)
    after = (iota((rows, rows), 1) < iota((rows, rows), 0)).astype(F32).astype(BF)
    place = matmul(after, named)[:, :1]
    spread = jnp.where(iota((rows, padded), 1).astype(F32) == place, weight, 0.0).astype(BF)
    if padded > slots:
        res[slots:, :] = jnp.zeros((padded - slots, dsize), BF)

    for i in range(hidden // fsize):
        cols = slice(i * fsize, (i + 1) * fsize)
        g = matmul(xc[...], gate[0, :, cols])
        u = matmul(xc[...], up[0, :, cols])
        act[:, cols] = (g / (1.0 + jnp.exp(-g)) * u).astype(BF)
    for i in range(chunks):
        down_copy(i).wait()
        cols = slice(i * dsize, (i + 1) * dsize)
        res[:slots, :] = matmul(act[...], down[:, cols]).astype(BF)
        out_ref[:, cols] = matmul(spread, res[...]).astype(BF)


def experts(x, expert_gate, expert_up, expert_down, share):
    rows = x.shape[0]
    _, width, hidden = expert_gate.shape
    slots = rows // share * CAP
    vmem = pl.BlockSpec(memory_space=pltpu.VMEM)
    return pl.pallas_call(
        functools.partial(expert_kernel, slots),
        out_shape=jax.ShapeDtypeStruct((rows, width), BF),
        in_specs=[vmem] * 3 + [pl.BlockSpec(memory_space=pltpu.HBM)],
        out_specs=vmem,
        scratch_shapes=[
            pltpu.VMEM((hidden, width), BF),
            pltpu.VMEM((slots, width), BF),
            pltpu.VMEM((slots, hidden), BF),
            pltpu.VMEM((-(-slots // LANES) * LANES, 1024), BF),
            pltpu.SemaphoreType.DMA((width // 1024,)),
        ],
        compiler_params=pltpu.CompilerParams(vmem_limit_bytes=(16 + rows // 32) * MIB),
        name="experts",
    )(x, expert_gate, expert_up, in_hbm(expert_down))


class Plan:
    def __init__(self, dp, tensor):
        self.zlen = min(4, dp)
        xlen, ylen = dp // self.zlen, tensor // 2
        self.count = dp * tensor
        self.core = 1
        self.y = [2 * j for j in range(1, ylen)]
        self.z = [tensor * xlen * j for j in range(1, self.zlen)]
        self.plane = [
            tensor * jx + 2 * jy for jx in range(xlen) for jy in range(ylen) if jx or jy
        ]

    def swap(self, value, flip):
        return lax.ppermute(value, ("dp", "tensor"), [(i, i ^ flip) for i in range(self.count)])

    def swaps(self, values, flips):
        pairs = list(zip(values, flips))[::-1]
        return [self.swap(value.astype(BF), flip) for value, flip in pairs][::-1]

    def spread(self, value, flips):
        return self.swaps([value] * len(flips), flips)


def total_of(values):
    return functools.reduce(jnp.add, [v.astype(F32) for v in values])


def shards(
    queries,
    new_keys,
    new_values,
    key_cache,
    value_cache,
    lengths,
    residual_in,
    query_gain,
    key_gain,
    out_proj,
    norm_gain,
    expert_ids,
    gate_weights,
    expert_gate,
    expert_up,
    expert_down,
):
    tensor = lax.axis_size("tensor")
    dp = lax.axis_size("dp")
    plan = Plan(dp, tensor)
    share, width = residual_in.shape
    lanes = -(-dp * tensor // LANES) * LANES

    local, table, out_proj, expert_gate = attention(
        lengths,
        queries,
        new_keys,
        new_values,
        key_cache,
        value_cache,
        query_gain,
        key_gain,
        expert_ids,
        gate_weights,
        tensor,
        lanes,
        (out_proj, expert_gate),
    )
    got = [local[0]] + plan.swaps(list(local[1:]), list(range(1, tensor)))
    partial, expert_up = projection(got, out_proj, share, expert_up)
    pair = total_of([partial[0], plan.swap(partial[1], plan.core)])
    projected = total_of([pair[0]] + plan.swaps(list(pair[1:]), plan.y))
    hidden = residual_in.astype(F32) + projected
    normed = rms_scale(hidden, norm_gain).astype(BF)

    mine = jnp.concatenate([normed, table], axis=1)
    others = plan.spread(mine, plan.z)
    near = plan.spread(mine, plan.plane)
    far = plan.spread(jnp.concatenate(others), plan.plane)
    pieces = [jnp.concatenate([mine] + others + near)] + far
    x = jnp.concatenate(pieces + [plan.swap(piece, plan.core) for piece in pieces])

    result = experts(x, expert_gate, expert_up, expert_down, share)

    sizes = [piece.shape[0] for piece in pieces]
    starts = [sum(sizes[:i]) for i in range(len(sizes) + 1)]
    every = starts[-1]
    sums = [
        total_of(
            [
                result[starts[i] : starts[i + 1]],
                plan.swap(result[every + starts[i] : every + starts[i + 1]], plan.core),
            ]
        )
        for i in reversed(range(len(sizes)))
    ][::-1]
    blocks = sums[0].reshape(-1, share, width)
    far = plan.swaps(sums[1:], plan.plane)
    others = total_of([sums[0][share : plan.zlen * share]] + far).reshape(-1, share, width)
    near = plan.swaps(list(blocks[plan.zlen :]), plan.plane)
    moe_sum = total_of([blocks[0]] + near + plan.swaps(list(others), plan.z))
    return (hidden + moe_sum).astype(BF)


def solution(mesh):
    return jax.shard_map(
        shards,
        mesh=mesh,
        in_specs=(
            P("dp", None, None),
            P("dp", None, None),
            P("dp", None, None),
            P("dp", None, "tensor", None),
            P("dp", None, "tensor", None),
            P("dp"),
            P(("dp", "tensor"), None),
            P(),
            P(),
            P("tensor", None),
            P(),
            P(("dp", "tensor"), None),
            P(("dp", "tensor"), None),
            P(("dp", "tensor"), None, None),
            P(("dp", "tensor"), None, None),
            P(("dp", "tensor"), None, None),
        ),
        out_specs=P(("dp", "tensor"), None),
        check_vma=False,
    )
```

```python
import functools

import jax
import jax.numpy as jnp
from jax import lax
from jax.experimental import pallas as pl
from jax.experimental.pallas import tpu as pltpu
from jax.sharding import PartitionSpec as P

BF = jnp.bfloat16
F32 = jnp.float32
I32 = jnp.int32
MIB = 1 << 20
LANES = 128
CAP = 3


def rms_scale(values, gain):
    mean_sq = jnp.mean(values * values, axis=-1, keepdims=True)
    return values * lax.rsqrt(mean_sq + 1e-06) * gain


def matmul(a, b):
    return jnp.dot(a, b, preferred_element_type=F32)


def matmul_t(a, b):
    return lax.dot_general(a, b, (((1,), (1,)), ((), ())), preferred_element_type=F32)


def iota(shape, dim):
    return lax.broadcasted_iota(I32, shape, dim)


def in_hbm(value):
    return pltpu.with_memory_space_constraint(value, pltpu.HBM)


def attention_kernel(
    len_hbm,
    q_hbm,
    nk_hbm,
    nv_hbm,
    k_hbm,
    v_hbm,
    qg_hbm,
    kg_hbm,
    ids_hbm,
    gates_hbm,
    w_hbm,
    out_ref,
    table_ref,
    w_ref,
    lengths,
    q_ref,
    nk_ref,
    nv_ref,
    k_ref,
    v_ref,
    qg_ref,
    kg_ref,
    ids_ref,
    gates_ref,
    nk_scr,
    nv_scr,
    num,
    tops,
    totals,
    score,
    weight,
    sem,
):
    sources = (len_hbm, nk_hbm, nv_hbm, qg_hbm, kg_hbm, ids_hbm, gates_hbm, q_hbm, k_hbm, v_hbm)
    targets = (lengths, nk_ref, nv_ref, qg_ref, kg_ref, ids_ref, gates_ref, q_ref, k_ref, v_ref)
    copies = [
        pltpu.make_async_copy(a, b, sem.at[i]) for i, (a, b) in enumerate(zip(sources, targets))
    ]
    ahead = pltpu.make_async_copy(w_hbm, w_ref, sem.at[10])
    for c in copies + [ahead]:
        c.start()
    tensor_pos = lax.axis_index("tensor")
    rows, heads, hd = q_ref.shape
    kvh, cache = k_ref.shape[1], k_ref.shape[2]
    group = heads // kvh
    parts = out_ref.shape[0]
    heads_own = heads // parts
    step = 4
    blocks = rows // step
    many, cols, fresh = step * heads, step * kvh * cache, step * kvh
    scaling = hd ** (-0.5)

    row_group = iota((many, cols), 0) // group
    same = row_group == iota((many, cols), 1) // cache
    col_row = iota((1, cols), 1) // (kvh * cache)
    col_pos = iota((1, cols), 1) % cache + tensor_pos * cache
    new_col = iota((many, 2 * fresh), 1)
    new_here = (new_col == iota((many, 2 * fresh), 0) // group) & (tensor_pos == 0)

    for c in copies[:7]:
        c.wait()
    gates = gates_ref[...]
    route = (gates / jnp.sum(gates, axis=1, keepdims=True)).astype(BF).astype(F32)
    expert = iota(table_ref.shape, 1)
    table = jnp.zeros(table_ref.shape, F32)
    for k in range(gates.shape[1]):
        table = jnp.where(expert == ids_ref[:, k : k + 1], route[:, k : k + 1], table)
    table_ref[...] = table.astype(BF)
    for r in range(rows):
        nk_scr[r * kvh : (r + 1) * kvh, :] = nk_ref[r].astype(F32)
        nv_scr[r * kvh : (r + 1) * kvh, :] = nv_ref[r].astype(F32)
    query_gain = qg_ref[...]
    key_norm = rms_scale(nk_scr[...], kg_ref[...])
    empty = jnp.zeros((fresh, hd), F32)
    for c in copies[7:]:
        c.wait()

    def rows_of(ref, b, size):
        return ref[b * step : (b + 1) * step].reshape(size, hd)

    queries = []
    for b in range(blocks):
        query = rows_of(q_ref, b, many).astype(F32)
        queries.append(rms_scale(query, query_gain).astype(BF))
    for b in range(blocks):
        limit = jnp.zeros((1, cols), I32)
        for i in range(step):
            limit = jnp.where(col_row == i, lengths[b * step + i], limit)
        included = same & (col_pos < limit)
        scores = matmul_t(queries[b], rows_of(k_ref, b, cols)) * scaling
        score[b, :, :cols] = jnp.where(included, scores, -1e30)
        new_keys = jnp.concatenate([key_norm[b * fresh : (b + 1) * fresh], empty]).astype(BF)
        scores = matmul_t(queries[b], new_keys) * scaling
        score[b, :, cols:] = jnp.where(new_here, scores, -1e30)
    for b in range(blocks):
        top = jnp.maximum(jnp.max(score[b], axis=1, keepdims=True), -1e29).astype(BF).astype(F32)
        tops[b * many : (b + 1) * many, :] = jnp.broadcast_to(top, (many, LANES))
    for b in range(blocks):
        top = tops[b * many : (b + 1) * many, 0:1]
        weights = jnp.exp(score[b] - top).astype(BF)
        weight[b] = weights
        total = jnp.sum(weights.astype(F32), axis=1, keepdims=True)
        totals[b * many : (b + 1) * many, :] = jnp.broadcast_to(total, (many, LANES))
    for b in range(blocks):
        values = nv_scr[b * fresh : (b + 1) * fresh, :]
        new_values = jnp.concatenate([values, empty]).astype(BF)
        num[b * many : (b + 1) * many, :] = matmul(
            weight[b, :, :cols], rows_of(v_ref, b, cols)
        ) + matmul(weight[b, :, cols:], new_values)

    lane = iota((rows, LANES), 1)
    for t in range(parts):
        slot = tensor_pos ^ t
        side = jnp.zeros((rows, LANES), F32)
        for h in range(heads_own):
            which = pl.ds(t * heads_own + h, rows, stride=heads)
            out_ref[slot, :, h * hd : (h + 1) * hd] = num[which, :].astype(BF)
            total = totals[which, :]
            high = total.astype(BF).astype(F32)
            side = jnp.where(lane == h, tops[which, :], side)
            side = jnp.where(lane == heads_own + h, high, side)
            side = jnp.where(lane == 2 * heads_own + h, total - high, side)
        out_ref[slot, :, heads_own * hd :] = side.astype(BF)
    ahead.wait()


def attention(
    lengths,
    queries,
    new_keys,
    new_values,
    key_cache,
    value_cache,
    qg,
    kg,
    expert_ids,
    gate_weights,
    parts,
    lanes,
    later,
):
    rows, heads, hd = queries.shape
    kvh, cache = key_cache.shape[1:3]
    args = (
        lengths,
        queries,
        new_keys,
        new_values,
        key_cache,
        value_cache,
        qg.reshape(1, -1),
        kg.reshape(1, -1),
        expert_ids,
        gate_weights,
    )
    return pl.pallas_call(
        attention_kernel,
        out_shape=(
            jax.ShapeDtypeStruct((parts, rows, heads // parts * hd + LANES), BF),
            jax.ShapeDtypeStruct((expert_ids.shape[0], lanes), BF),
            pltpu.VMEM(later.shape, later.dtype),
        ),
        in_specs=[pl.BlockSpec(memory_space=pltpu.HBM)] * 11,
        out_specs=(pl.BlockSpec(memory_space=pltpu.VMEM),) * 3,
        scratch_shapes=[pltpu.SMEM(args[0].shape, I32)]
        + [pltpu.VMEM(a.shape, a.dtype) for a in args[1:]]
        + [
            pltpu.VMEM((rows * kvh, hd), F32),
            pltpu.VMEM((rows * kvh, hd), F32),
            pltpu.VMEM((rows * heads, hd), F32),
            pltpu.VMEM((rows * heads, LANES), F32),
            pltpu.VMEM((rows * heads, LANES), F32),
            pltpu.VMEM((rows // 4, 4 * heads, 4 * kvh * (cache + 2)), F32),
            pltpu.VMEM((rows // 4, 4 * heads, 4 * kvh * (cache + 2)), BF),
            pltpu.SemaphoreType.DMA((11,)),
        ],
        compiler_params=pltpu.CompilerParams(vmem_limit_bytes=16 * MIB),
        name="attention",
    )(*[in_hbm(a) for a in (*args, later)])


def projection_kernel(parts, *refs):
    got = refs[:parts]
    w_ref, w0_hbm, w1_hbm, out_ref, w0_ref, w1_ref, attn, sem = refs[parts:]
    ahead = [
        pltpu.make_async_copy(w0_hbm, w0_ref, sem.at[0]),
        pltpu.make_async_copy(w1_hbm, w1_ref, sem.at[1]),
    ]
    for c in ahead:
        c.start()
    tensor_pos = lax.axis_index("tensor")
    depth, width = w_ref.shape
    share = out_ref.shape[2]
    hd = LANES
    heads_own = depth // hd
    size = 512
    sides = [g[:, depth:].astype(F32) for g in got]
    tops = [s[:, :heads_own] for s in sides]
    top = functools.reduce(jnp.maximum, tops)
    factors = [jnp.exp(t - top) for t in tops]
    totals = [
        f * (s[:, heads_own : 2 * heads_own] + s[:, 2 * heads_own : 3 * heads_own])
        for f, s in zip(factors, sides)
    ]
    total = functools.reduce(jnp.add, totals)
    factors = [f / total for f in factors]
    for h in range(heads_own):
        cols = slice(h * hd, (h + 1) * hd)
        terms = [g[:, cols].astype(F32) * f[:, h : h + 1] for g, f in zip(got, factors)]
        attn[:, cols] = functools.reduce(jnp.add, terms).astype(BF)
    for i in range(width // size):
        cols = slice(i * size, (i + 1) * size)
        result = matmul(attn[...], w_ref[:, cols])
        for t in range(parts):
            slot = tensor_pos ^ t
            out_ref[slot & 1, slot >> 1, :, cols] = result[t * share : (t + 1) * share].astype(BF)
    for c in ahead:
        c.wait()


def projection(got, out_proj, share, later):
    parts = len(got)
    rows = got[0].shape[0]
    depth, width = out_proj.shape
    vmem = pl.BlockSpec(memory_space=pltpu.VMEM)
    return pl.pallas_call(
        functools.partial(projection_kernel, parts),
        out_shape=(
            jax.ShapeDtypeStruct((2, parts // 2, share, width), BF),
            *[pltpu.VMEM(w.shape, w.dtype) for w in later],
        ),
        in_specs=[vmem] * (parts + 1) + [pl.BlockSpec(memory_space=pltpu.HBM)] * 2,
        out_specs=(vmem,) * 3,
        scratch_shapes=[pltpu.VMEM((rows, depth), BF), pltpu.SemaphoreType.DMA((2,))],
        compiler_params=pltpu.CompilerParams(vmem_limit_bytes=12 * MIB),
        name="projection",
    )(*got, out_proj, *[in_hbm(w) for w in later])


def expert_kernel(slots, x_ref, gate, up, down_hbm, out_ref, down, xc, act, res, sem):
    own = lax.axis_index("dp") * lax.axis_size("tensor") + lax.axis_index("tensor")
    rows = x_ref.shape[0]
    _, width, hidden = gate.shape
    padded = res.shape[0]
    fsize = 256
    dsize = 1024
    chunks = width // dsize

    def down_copy(i):
        cols = pl.ds(i * dsize, dsize)
        return pltpu.make_async_copy(down_hbm.at[0, :, cols], down.at[:, cols], sem.at[i])

    for i in range(chunks):
        down_copy(i).start()
    table = x_ref[:, width:]
    pick = (iota((16, table.shape[1]), 1) == own).astype(F32).astype(BF)
    named = matmul_t(pick, table) != 0.0
    before = (iota((rows, rows), 0) < iota((rows, rows), 1)).astype(F32).astype(BF)
    place = matmul(named.astype(F32).astype(BF), before)
    place = jnp.where(named, place, -1.0)[:1]
    take = (iota((slots, rows), 0).astype(F32) == place).astype(F32).astype(BF)
    for i in range(chunks):
        cols = slice(i * dsize, (i + 1) * dsize)
        xc[:, cols] = matmul(take, x_ref[:, cols]).astype(BF)

    lane = iota(table.shape, 1)
    weight = jnp.sum(jnp.where(lane == own, table.astype(F32), 0.0), axis=1, keepdims=True)
    named = jnp.broadcast_to((weight != 0.0).astype(F32), (rows, LANES)).astype(BF)
    after = (iota((rows, rows), 1) < iota((rows, rows), 0)).astype(F32).astype(BF)
    place = matmul(after, named)[:, :1]
    spread = jnp.where(iota((rows, padded), 1).astype(F32) == place, weight, 0.0).astype(BF)
    if padded > slots:
        res[slots:, :] = jnp.zeros((padded - slots, dsize), BF)

    for i in range(hidden // fsize):
        cols = slice(i * fsize, (i + 1) * fsize)
        g = matmul(xc[...], gate[0, :, cols])
        u = matmul(xc[...], up[0, :, cols])
        act[:, cols] = (g / (1.0 + jnp.exp(-g)) * u).astype(BF)
    for i in range(chunks):
        down_copy(i).wait()
        cols = slice(i * dsize, (i + 1) * dsize)
        res[:slots, :] = matmul(act[...], down[:, cols]).astype(BF)
        out_ref[:, cols] = matmul(spread, res[...]).astype(BF)


def experts(x, expert_gate, expert_up, expert_down, share):
    rows = x.shape[0]
    _, width, hidden = expert_gate.shape
    slots = rows // share * CAP
    vmem = pl.BlockSpec(memory_space=pltpu.VMEM)
    return pl.pallas_call(
        functools.partial(expert_kernel, slots),
        out_shape=jax.ShapeDtypeStruct((rows, width), BF),
        in_specs=[vmem] * 3 + [pl.BlockSpec(memory_space=pltpu.HBM)],
        out_specs=vmem,
        scratch_shapes=[
            pltpu.VMEM((hidden, width), BF),
            pltpu.VMEM((slots, width), BF),
            pltpu.VMEM((slots, hidden), BF),
            pltpu.VMEM((-(-slots // LANES) * LANES, 1024), BF),
            pltpu.SemaphoreType.DMA((width // 1024,)),
        ],
        compiler_params=pltpu.CompilerParams(vmem_limit_bytes=(16 + rows // 32) * MIB),
        name="experts",
    )(x, expert_gate, expert_up, in_hbm(expert_down))


class Plan:
    def __init__(self, dp, tensor):
        self.zlen = min(4, dp)
        xlen, ylen = dp // self.zlen, tensor // 2
        self.count = dp * tensor
        self.core = 1
        self.y = [2 * j for j in range(1, ylen)]
        self.z = [tensor * xlen * j for j in range(1, self.zlen)]
        self.plane = [
            tensor * jx + 2 * jy for jx in range(xlen) for jy in range(ylen) if jx or jy
        ]

    def swap(self, value, flip):
        return lax.ppermute(value, ("dp", "tensor"), [(i, i ^ flip) for i in range(self.count)])

    def swaps(self, values, flips):
        pairs = list(zip(values, flips))[::-1]
        return [self.swap(value.astype(BF), flip) for value, flip in pairs][::-1]

    def spread(self, value, flips):
        return self.swaps([value] * len(flips), flips)


def total_of(values):
    return functools.reduce(jnp.add, [v.astype(F32) for v in values])


def shards(
    queries,
    new_keys,
    new_values,
    key_cache,
    value_cache,
    lengths,
    residual_in,
    query_gain,
    key_gain,
    out_proj,
    norm_gain,
    expert_ids,
    gate_weights,
    expert_gate,
    expert_up,
    expert_down,
):
    tensor = lax.axis_size("tensor")
    dp = lax.axis_size("dp")
    plan = Plan(dp, tensor)
    share, width = residual_in.shape
    lanes = -(-dp * tensor // LANES) * LANES

    local, table, out_proj = attention(
        lengths,
        queries,
        new_keys,
        new_values,
        key_cache,
        value_cache,
        query_gain,
        key_gain,
        expert_ids,
        gate_weights,
        tensor,
        lanes,
        out_proj,
    )
    got = [local[0]] + plan.swaps(list(local[1:]), list(range(1, tensor)))
    partial, expert_gate, expert_up = projection(
        got, out_proj, share, (expert_gate, expert_up)
    )
    pair = total_of([partial[0], plan.swap(partial[1], plan.core)])
    projected = total_of([pair[0]] + plan.swaps(list(pair[1:]), plan.y))
    hidden = residual_in.astype(F32) + projected
    normed = rms_scale(hidden, norm_gain).astype(BF)

    mine = jnp.concatenate([normed, table], axis=1)
    others = plan.spread(mine, plan.z)
    near = plan.spread(mine + others[0][:, :1] * 0, plan.plane)
    far = plan.spread(jnp.concatenate(others), plan.plane)
    pieces = [jnp.concatenate([mine] + others + near)] + far
    x = jnp.concatenate(pieces + [plan.swap(piece, plan.core) for piece in pieces])

    result = experts(x, expert_gate, expert_up, expert_down, share)

    sizes = [piece.shape[0] for piece in pieces]
    starts = [sum(sizes[:i]) for i in range(len(sizes) + 1)]
    every = starts[-1]
    sums = [
        total_of(
            [
                result[starts[i] : starts[i + 1]],
                plan.swap(result[every + starts[i] : every + starts[i + 1]], plan.core),
            ]
        )
        for i in reversed(range(len(sizes)))
    ][::-1]
    blocks = sums[0].reshape(-1, share, width)
    sent = [
        jnp.concatenate([near.astype(BF), far.astype(BF)])
        for near, far in zip(blocks[plan.zlen :], sums[1:])
    ]
    column = total_of(
        [sums[0][: plan.zlen * share]] + plan.swaps(sent, plan.plane)
    ).reshape(-1, share, width)
    moe_sum = total_of([column[0]] + plan.swaps(list(column[1:]), plan.z))
    return (hidden + moe_sum).astype(BF)


def solution(mesh):
    return jax.shard_map(
        shards,
        mesh=mesh,
        in_specs=(
            P("dp", None, None),
            P("dp", None, None),
            P("dp", None, None),
            P("dp", None, "tensor", None),
            P("dp", None, "tensor", None),
            P("dp"),
            P(("dp", "tensor"), None),
            P(),
            P(),
            P("tensor", None),
            P(),
            P(("dp", "tensor"), None),
            P(("dp", "tensor"), None),
            P(("dp", "tensor"), None, None),
            P(("dp", "tensor"), None, None),
            P(("dp", "tensor"), None, None),
        ),
        out_specs=P(("dp", "tensor"), None),
        check_vma=False,
    )
```

```python
import functools

import jax
import jax.numpy as jnp
from jax import lax
from jax.experimental import pallas as pl
from jax.experimental.pallas import tpu as pltpu
from jax.sharding import PartitionSpec as P

BF = jnp.bfloat16
F32 = jnp.float32
I32 = jnp.int32
MIB = 1 << 20
LANES = 128
CAP = 3


def rms_scale(values, gain):
    mean_sq = jnp.mean(values * values, axis=-1, keepdims=True)
    return values * lax.rsqrt(mean_sq + 1e-06) * gain


def matmul(a, b):
    return jnp.dot(a, b, preferred_element_type=F32)


def matmul_t(a, b):
    return lax.dot_general(a, b, (((1,), (1,)), ((), ())), preferred_element_type=F32)


def iota(shape, dim):
    return lax.broadcasted_iota(I32, shape, dim)


def in_hbm(value):
    return pltpu.with_memory_space_constraint(value, pltpu.HBM)


def attention_kernel(
    len_hbm,
    q_hbm,
    nk_hbm,
    nv_hbm,
    k_hbm,
    v_hbm,
    qg_hbm,
    kg_hbm,
    ids_hbm,
    gates_hbm,
    w_hbm,
    out_ref,
    table_ref,
    w_ref,
    lengths,
    q_ref,
    nk_ref,
    nv_ref,
    k_ref,
    v_ref,
    qg_ref,
    kg_ref,
    ids_ref,
    gates_ref,
    nk_scr,
    nv_scr,
    num,
    tops,
    totals,
    score,
    weight,
    sem,
):
    sources = (len_hbm, nk_hbm, nv_hbm, qg_hbm, kg_hbm, ids_hbm, gates_hbm, q_hbm, k_hbm, v_hbm)
    targets = (lengths, nk_ref, nv_ref, qg_ref, kg_ref, ids_ref, gates_ref, q_ref, k_ref, v_ref)
    copies = [
        pltpu.make_async_copy(a, b, sem.at[i]) for i, (a, b) in enumerate(zip(sources, targets))
    ]
    ahead = pltpu.make_async_copy(w_hbm, w_ref, sem.at[10])
    for c in copies + [ahead]:
        c.start()
    tensor_pos = lax.axis_index("tensor")
    rows, heads, hd = q_ref.shape
    kvh, cache = k_ref.shape[1], k_ref.shape[2]
    group = heads // kvh
    parts = out_ref.shape[0]
    heads_own = heads // parts
    step = 4
    blocks = rows // step
    many, cols, fresh = step * heads, step * kvh * cache, step * kvh
    scaling = hd ** (-0.5)

    row_group = iota((many, cols), 0) // group
    same = row_group == iota((many, cols), 1) // cache
    col_row = iota((1, cols), 1) // (kvh * cache)
    col_pos = iota((1, cols), 1) % cache + tensor_pos * cache
    new_col = iota((many, 2 * fresh), 1)
    new_here = (new_col == iota((many, 2 * fresh), 0) // group) & (tensor_pos == 0)

    for c in copies[:7]:
        c.wait()
    gates = gates_ref[...]
    route = (gates / jnp.sum(gates, axis=1, keepdims=True)).astype(BF).astype(F32)
    expert = iota(table_ref.shape, 1)
    table = jnp.zeros(table_ref.shape, F32)
    for k in range(gates.shape[1]):
        table = jnp.where(expert == ids_ref[:, k : k + 1], route[:, k : k + 1], table)
    table_ref[...] = table.astype(BF)
    for r in range(rows):
        nk_scr[r * kvh : (r + 1) * kvh, :] = nk_ref[r].astype(F32)
        nv_scr[r * kvh : (r + 1) * kvh, :] = nv_ref[r].astype(F32)
    query_gain = qg_ref[...]
    key_norm = rms_scale(nk_scr[...], kg_ref[...])
    empty = jnp.zeros((fresh, hd), F32)
    for c in copies[7:]:
        c.wait()

    def rows_of(ref, b, size):
        return ref[b * step : (b + 1) * step].reshape(size, hd)

    queries = []
    for b in range(blocks):
        query = rows_of(q_ref, b, many).astype(F32)
        queries.append(rms_scale(query, query_gain).astype(BF))
    for b in range(blocks):
        limit = jnp.zeros((1, cols), I32)
        for i in range(step):
            limit = jnp.where(col_row == i, lengths[b * step + i], limit)
        included = same & (col_pos < limit)
        scores = matmul_t(queries[b], rows_of(k_ref, b, cols)) * scaling
        score[b, :, :cols] = jnp.where(included, scores, -1e30)
        new_keys = jnp.concatenate([key_norm[b * fresh : (b + 1) * fresh], empty]).astype(BF)
        scores = matmul_t(queries[b], new_keys) * scaling
        score[b, :, cols:] = jnp.where(new_here, scores, -1e30)
    for b in range(blocks):
        top = jnp.maximum(jnp.max(score[b], axis=1, keepdims=True), -1e29).astype(BF).astype(F32)
        tops[b * many : (b + 1) * many, :] = jnp.broadcast_to(top, (many, LANES))
    for b in range(blocks):
        top = tops[b * many : (b + 1) * many, 0:1]
        weights = jnp.exp(score[b] - top).astype(BF)
        weight[b] = weights
        total = jnp.sum(weights.astype(F32), axis=1, keepdims=True)
        totals[b * many : (b + 1) * many, :] = jnp.broadcast_to(total, (many, LANES))
    for b in range(blocks):
        values = nv_scr[b * fresh : (b + 1) * fresh, :]
        new_values = jnp.concatenate([values, empty]).astype(BF)
        num[b * many : (b + 1) * many, :] = matmul(
            weight[b, :, :cols], rows_of(v_ref, b, cols)
        ) + matmul(weight[b, :, cols:], new_values)

    lane = iota((rows, LANES), 1)
    for t in range(parts):
        slot = tensor_pos ^ t
        side = jnp.zeros((rows, LANES), F32)
        for h in range(heads_own):
            which = pl.ds(t * heads_own + h, rows, stride=heads)
            out_ref[slot, :, h * hd : (h + 1) * hd] = num[which, :].astype(BF)
            total = totals[which, :]
            high = total.astype(BF).astype(F32)
            side = jnp.where(lane == h, tops[which, :], side)
            side = jnp.where(lane == heads_own + h, high, side)
            side = jnp.where(lane == 2 * heads_own + h, total - high, side)
        out_ref[slot, :, heads_own * hd :] = side.astype(BF)
    ahead.wait()


def attention(
    lengths,
    queries,
    new_keys,
    new_values,
    key_cache,
    value_cache,
    qg,
    kg,
    expert_ids,
    gate_weights,
    parts,
    lanes,
    later,
):
    rows, heads, hd = queries.shape
    kvh, cache = key_cache.shape[1:3]
    args = (
        lengths,
        queries,
        new_keys,
        new_values,
        key_cache,
        value_cache,
        qg.reshape(1, -1),
        kg.reshape(1, -1),
        expert_ids,
        gate_weights,
    )
    return pl.pallas_call(
        attention_kernel,
        out_shape=(
            jax.ShapeDtypeStruct((parts, rows, heads // parts * hd + LANES), BF),
            jax.ShapeDtypeStruct((expert_ids.shape[0], lanes), BF),
            pltpu.VMEM(later.shape, later.dtype),
        ),
        in_specs=[pl.BlockSpec(memory_space=pltpu.HBM)] * 11,
        out_specs=(pl.BlockSpec(memory_space=pltpu.VMEM),) * 3,
        scratch_shapes=[pltpu.SMEM(args[0].shape, I32)]
        + [pltpu.VMEM(a.shape, a.dtype) for a in args[1:]]
        + [
            pltpu.VMEM((rows * kvh, hd), F32),
            pltpu.VMEM((rows * kvh, hd), F32),
            pltpu.VMEM((rows * heads, hd), F32),
            pltpu.VMEM((rows * heads, LANES), F32),
            pltpu.VMEM((rows * heads, LANES), F32),
            pltpu.VMEM((rows // 4, 4 * heads, 4 * kvh * (cache + 2)), F32),
            pltpu.VMEM((rows // 4, 4 * heads, 4 * kvh * (cache + 2)), BF),
            pltpu.SemaphoreType.DMA((11,)),
        ],
        compiler_params=pltpu.CompilerParams(vmem_limit_bytes=16 * MIB),
        name="attention",
    )(*[in_hbm(a) for a in (*args, later)])


def projection_kernel(parts, *refs):
    got = refs[:parts]
    w_ref, ahead_hbm, out_ref, ahead_ref, attn, sem = refs[parts:]
    ahead = pltpu.make_async_copy(ahead_hbm, ahead_ref, sem)
    ahead.start()
    tensor_pos = lax.axis_index("tensor")
    depth, width = w_ref.shape
    share = out_ref.shape[2]
    hd = LANES
    heads_own = depth // hd
    size = 512
    sides = [g[:, depth:].astype(F32) for g in got]
    tops = [s[:, :heads_own] for s in sides]
    top = functools.reduce(jnp.maximum, tops)
    factors = [jnp.exp(t - top) for t in tops]
    totals = [
        f * (s[:, heads_own : 2 * heads_own] + s[:, 2 * heads_own : 3 * heads_own])
        for f, s in zip(factors, sides)
    ]
    total = functools.reduce(jnp.add, totals)
    factors = [f / total for f in factors]
    for h in range(heads_own):
        cols = slice(h * hd, (h + 1) * hd)
        terms = [g[:, cols].astype(F32) * f[:, h : h + 1] for g, f in zip(got, factors)]
        attn[:, cols] = functools.reduce(jnp.add, terms).astype(BF)
    for i in range(width // size):
        cols = slice(i * size, (i + 1) * size)
        result = matmul(attn[...], w_ref[:, cols])
        for t in range(parts):
            slot = tensor_pos ^ t
            out_ref[slot & 1, slot >> 1, :, cols] = result[t * share : (t + 1) * share].astype(BF)
    ahead.wait()


def projection(got, out_proj, share, later):
    parts = len(got)
    rows = got[0].shape[0]
    depth, width = out_proj.shape
    vmem = pl.BlockSpec(memory_space=pltpu.VMEM)
    return pl.pallas_call(
        functools.partial(projection_kernel, parts),
        out_shape=(
            jax.ShapeDtypeStruct((2, parts // 2, share, width), BF),
            pltpu.VMEM(later.shape, later.dtype),
        ),
        in_specs=[vmem] * (parts + 1) + [pl.BlockSpec(memory_space=pltpu.HBM)],
        out_specs=(vmem, vmem),
        scratch_shapes=[pltpu.VMEM((rows, depth), BF), pltpu.SemaphoreType.DMA],
        compiler_params=pltpu.CompilerParams(vmem_limit_bytes=12 * MIB),
        name="projection",
    )(*got, out_proj, in_hbm(later))


def expert_kernel(
    slots, x_ref, gate, up_hbm, down_hbm, o0, o1, o2, o3, up, down, xc, gated, act, res, sem
):
    own = lax.axis_index("dp") * lax.axis_size("tensor") + lax.axis_index("tensor")
    rows = x_ref.shape[0]
    _, width, hidden = gate.shape
    padded = res.shape[0]
    fsize = 256
    dsize = 1024
    chunks = width // dsize

    fchunks = hidden // fsize

    def up_copy(i):
        cols = pl.ds(i * fsize, fsize)
        return pltpu.make_async_copy(up_hbm.at[0, :, cols], up.at[:, cols], sem.at[chunks + i])

    def down_copy(i):
        cols = pl.ds(i * dsize, dsize)
        return pltpu.make_async_copy(down_hbm.at[0, :, cols], down.at[:, cols], sem.at[i])

    for i in range(fchunks):
        up_copy(i).start()
    for i in range(chunks):
        down_copy(i).start()
    table = x_ref[:, width:]
    pick = (iota((16, table.shape[1]), 1) == own).astype(F32).astype(BF)
    named = matmul_t(pick, table) != 0.0
    before = (iota((rows, rows), 0) < iota((rows, rows), 1)).astype(F32).astype(BF)
    place = matmul(named.astype(F32).astype(BF), before)
    place = jnp.where(named, place, -1.0)[:1]
    take = (iota((slots, rows), 0).astype(F32) == place).astype(F32).astype(BF)
    for i in range(chunks):
        cols = slice(i * dsize, (i + 1) * dsize)
        xc[:, cols] = matmul(take, x_ref[:, cols]).astype(BF)

    lane = iota(table.shape, 1)
    weight = jnp.sum(jnp.where(lane == own, table.astype(F32), 0.0), axis=1, keepdims=True)
    named = jnp.broadcast_to((weight != 0.0).astype(F32), (rows, LANES)).astype(BF)
    after = (iota((rows, rows), 1) < iota((rows, rows), 0)).astype(F32).astype(BF)
    place = matmul(after, named)[:, :1]
    spread = jnp.where(iota((rows, padded), 1).astype(F32) == place, weight, 0.0).astype(BF)
    if padded > slots:
        res[slots:, :] = jnp.zeros((padded - slots, dsize), BF)

    for i in range(fchunks):
        cols = slice(i * fsize, (i + 1) * fsize)
        g = matmul(xc[...], gate[0, :, cols])
        gated[:, cols] = g / (1.0 + jnp.exp(-g))
    for i in range(fchunks):
        up_copy(i).wait()
        cols = slice(i * fsize, (i + 1) * fsize)
        u = matmul(xc[...], up[:, cols])
        act[:, cols] = (gated[:, cols] * u).astype(BF)
    for i in range(chunks):
        down_copy(i).wait()
        cols = slice(i * dsize, (i + 1) * dsize)
        res[:slots, :] = matmul(act[...], down[:, cols]).astype(BF)
        result = matmul(spread, res[...]).astype(BF)
        for k, out in enumerate((o0, o1, o2, o3)):
            out[:, cols] = result[k * rows // 4 : (k + 1) * rows // 4]


def experts(x, expert_gate, expert_up, expert_down, share):
    rows = x.shape[0]
    _, width, hidden = expert_gate.shape
    slots = rows // share * CAP
    vmem = pl.BlockSpec(memory_space=pltpu.VMEM)
    return pl.pallas_call(
        functools.partial(expert_kernel, slots),
        out_shape=(jax.ShapeDtypeStruct((rows // 4, width), BF),) * 4,
        in_specs=[vmem] * 2 + [pl.BlockSpec(memory_space=pltpu.HBM)] * 2,
        out_specs=(vmem,) * 4,
        scratch_shapes=[
            pltpu.VMEM((width, hidden), BF),
            pltpu.VMEM((hidden, width), BF),
            pltpu.VMEM((slots, width), BF),
            pltpu.VMEM((slots, hidden), F32),
            pltpu.VMEM((slots, hidden), BF),
            pltpu.VMEM((-(-slots // LANES) * LANES, 1024), BF),
            pltpu.SemaphoreType.DMA((width // 1024 + hidden // 256,)),
        ],
        compiler_params=pltpu.CompilerParams(vmem_limit_bytes=(22 + rows // 32) * MIB),
        name="experts",
    )(x, expert_gate, in_hbm(expert_up), in_hbm(expert_down))


class Plan:
    def __init__(self, dp, tensor):
        self.zlen = min(4, dp)
        xlen, ylen = dp // self.zlen, tensor // 2
        self.count = dp * tensor
        self.core = 1
        self.y = [2 * j for j in range(1, ylen)]
        self.z = [tensor * xlen * j for j in range(1, self.zlen)]
        self.plane = [
            tensor * jx + 2 * jy for jx in range(xlen) for jy in range(ylen) if jx or jy
        ]

    def swap(self, value, flip):
        return lax.ppermute(value, ("dp", "tensor"), [(i, i ^ flip) for i in range(self.count)])

    def swaps(self, values, flips):
        pairs = list(zip(values, flips))[::-1]
        return [self.swap(value.astype(BF), flip) for value, flip in pairs][::-1]

    def spread(self, value, flips):
        return self.swaps([value] * len(flips), flips)


def total_of(values):
    return functools.reduce(jnp.add, [v.astype(F32) for v in values])


def shards(
    queries,
    new_keys,
    new_values,
    key_cache,
    value_cache,
    lengths,
    residual_in,
    query_gain,
    key_gain,
    out_proj,
    norm_gain,
    expert_ids,
    gate_weights,
    expert_gate,
    expert_up,
    expert_down,
):
    tensor = lax.axis_size("tensor")
    dp = lax.axis_size("dp")
    plan = Plan(dp, tensor)
    share, width = residual_in.shape
    lanes = -(-dp * tensor // LANES) * LANES

    local, table, out_proj = attention(
        lengths,
        queries,
        new_keys,
        new_values,
        key_cache,
        value_cache,
        query_gain,
        key_gain,
        expert_ids,
        gate_weights,
        tensor,
        lanes,
        out_proj,
    )
    got = [local[0]] + plan.swaps(list(local[1:]), list(range(1, tensor)))
    partial, expert_gate = projection(got, out_proj, share, expert_gate)
    pair = total_of([partial[0], plan.swap(partial[1], plan.core)])
    projected = total_of([pair[0]] + plan.swaps(list(pair[1:]), plan.y))
    hidden = residual_in.astype(F32) + projected
    normed = rms_scale(hidden, norm_gain).astype(BF)

    mine = jnp.concatenate([normed, table], axis=1)
    column = [mine] + plan.spread(mine, plan.z)
    cut = len(column) // 2
    near, far = jnp.concatenate(column[:cut]), jnp.concatenate(column[cut:])
    nears = plan.spread(near, plan.plane)
    far_in = far + nears[0][:, :1] * 0
    fars = plan.spread(far_in, plan.plane)
    group = far.shape[0]
    first = plan.swap(jnp.concatenate([far, near]), plan.core)
    first = list(first.reshape(-1, group, first.shape[1]))
    rest = [plan.swap(piece, plan.core) for piece in nears[0:] + fars]
    there = first + rest
    here = [far, near] + nears + fars

    def grouped(pieces, last):
        count = len(nears)
        pairs = zip([pieces[1]] + pieces[2 : 2 + count], [pieces[0]] + pieces[2 + count :])
        cuts = []
        for front, back in pairs:
            both = jnp.concatenate([front, back])
            if last:
                cuts += [both[:share], both[-share:]]
            else:
                cuts.append(both[share:-share])
        return cuts

    x = jnp.concatenate(
        grouped(here, True) + grouped(here, False) + grouped(there, True) + grouped(there, False)
    )

    kept_a, kept_b, sent_a, sent_b = experts(x, expert_gate, expert_up, expert_down, share)

    def plane_sums(kept, sent):
        value = total_of([kept, plan.swap(sent, plan.core)])
        value = value.reshape(1 + len(plan.plane), -1, width)
        value = total_of([value[0]] + plan.swaps(list(value[1:]), plan.plane))
        return list(value.reshape(-1, share, width))

    ends = plane_sums(kept_a, sent_a)
    last = plan.swap(ends[1].astype(BF), plan.z[-1])
    middle = plan.swaps(plane_sums(kept_b, sent_b), plan.z[:-1])
    moe_sum = total_of([ends[0], last] + middle)
    return (hidden + moe_sum).astype(BF)


def solution(mesh):
    return jax.shard_map(
        shards,
        mesh=mesh,
        in_specs=(
            P("dp", None, None),
            P("dp", None, None),
            P("dp", None, None),
            P("dp", None, "tensor", None),
            P("dp", None, "tensor", None),
            P("dp"),
            P(("dp", "tensor"), None),
            P(),
            P(),
            P("tensor", None),
            P(),
            P(("dp", "tensor"), None),
            P(("dp", "tensor"), None),
            P(("dp", "tensor"), None, None),
            P(("dp", "tensor"), None, None),
            P(("dp", "tensor"), None, None),
        ),
        out_specs=P(("dp", "tensor"), None),
        check_vma=False,
    )
```

```python
import functools

import jax
import jax.numpy as jnp
from jax import lax
from jax.experimental import pallas as pl
from jax.experimental.pallas import tpu as pltpu
from jax.sharding import PartitionSpec as P

BF = jnp.bfloat16
F32 = jnp.float32
I32 = jnp.int32
MIB = 1 << 20
LANES = 128
CAP = 3


def rms_scale(values, gain):
    mean_sq = jnp.mean(values * values, axis=-1, keepdims=True)
    return values * lax.rsqrt(mean_sq + 1e-06) * gain


def matmul(a, b):
    return jnp.dot(a, b, preferred_element_type=F32)


def matmul_t(a, b):
    return lax.dot_general(a, b, (((1,), (1,)), ((), ())), preferred_element_type=F32)


def iota(shape, dim):
    return lax.broadcasted_iota(I32, shape, dim)


def in_hbm(value):
    return pltpu.with_memory_space_constraint(value, pltpu.HBM)


def attention_kernel(
    len_hbm,
    q_hbm,
    nk_hbm,
    nv_hbm,
    k_hbm,
    v_hbm,
    qg_hbm,
    kg_hbm,
    ids_hbm,
    gates_hbm,
    w_hbm,
    out_ref,
    table_ref,
    w_ref,
    lengths,
    q_ref,
    nk_ref,
    nv_ref,
    k_ref,
    v_ref,
    qg_ref,
    kg_ref,
    ids_ref,
    gates_ref,
    nk_scr,
    nv_scr,
    num,
    tops,
    totals,
    score,
    weight,
    sem,
):
    sources = (len_hbm, nk_hbm, nv_hbm, qg_hbm, kg_hbm, ids_hbm, gates_hbm, q_hbm, k_hbm, v_hbm)
    targets = (lengths, nk_ref, nv_ref, qg_ref, kg_ref, ids_ref, gates_ref, q_ref, k_ref, v_ref)
    copies = [
        pltpu.make_async_copy(a, b, sem.at[i]) for i, (a, b) in enumerate(zip(sources, targets))
    ]
    ahead = pltpu.make_async_copy(w_hbm, w_ref, sem.at[10])
    for c in copies + [ahead]:
        c.start()
    tensor_pos = lax.axis_index("tensor")
    rows, heads, hd = q_ref.shape
    kvh, cache = k_ref.shape[1], k_ref.shape[2]
    group = heads // kvh
    parts = out_ref.shape[0]
    heads_own = heads // parts
    step = 4
    blocks = rows // step
    many, cols, fresh = step * heads, step * kvh * cache, step * kvh
    scaling = hd ** (-0.5)

    row_group = iota((many, cols), 0) // group
    same = row_group == iota((many, cols), 1) // cache
    col_row = iota((1, cols), 1) // (kvh * cache)
    col_pos = iota((1, cols), 1) % cache + tensor_pos * cache
    new_col = iota((many, 2 * fresh), 1)
    new_here = (new_col == iota((many, 2 * fresh), 0) // group) & (tensor_pos == 0)

    for c in copies[:7]:
        c.wait()
    gates = gates_ref[...]
    route = (gates / jnp.sum(gates, axis=1, keepdims=True)).astype(BF).astype(F32)
    expert = iota(table_ref.shape, 1)
    table = jnp.zeros(table_ref.shape, F32)
    for k in range(gates.shape[1]):
        table = jnp.where(expert == ids_ref[:, k : k + 1], route[:, k : k + 1], table)
    table_ref[...] = table.astype(BF)
    for r in range(rows):
        nk_scr[r * kvh : (r + 1) * kvh, :] = nk_ref[r].astype(F32)
        nv_scr[r * kvh : (r + 1) * kvh, :] = nv_ref[r].astype(F32)
    query_gain = qg_ref[...]
    key_norm = rms_scale(nk_scr[...], kg_ref[...])
    empty = jnp.zeros((fresh, hd), F32)
    for c in copies[7:]:
        c.wait()

    def rows_of(ref, b, size):
        return ref[b * step : (b + 1) * step].reshape(size, hd)

    queries = []
    for b in range(blocks):
        query = rows_of(q_ref, b, many).astype(F32)
        queries.append(rms_scale(query, query_gain).astype(BF))
    for b in range(blocks):
        limit = jnp.zeros((1, cols), I32)
        for i in range(step):
            limit = jnp.where(col_row == i, lengths[b * step + i], limit)
        included = same & (col_pos < limit)
        scores = matmul_t(queries[b], rows_of(k_ref, b, cols)) * scaling
        score[b, :, :cols] = jnp.where(included, scores, -1e30)
        new_keys = jnp.concatenate([key_norm[b * fresh : (b + 1) * fresh], empty]).astype(BF)
        scores = matmul_t(queries[b], new_keys) * scaling
        score[b, :, cols:] = jnp.where(new_here, scores, -1e30)
    for b in range(blocks):
        top = jnp.maximum(jnp.max(score[b], axis=1, keepdims=True), -1e29).astype(BF).astype(F32)
        tops[b * many : (b + 1) * many, :] = jnp.broadcast_to(top, (many, LANES))
    for b in range(blocks):
        top = tops[b * many : (b + 1) * many, 0:1]
        weights = jnp.exp(score[b] - top).astype(BF)
        weight[b] = weights
        total = jnp.sum(weights.astype(F32), axis=1, keepdims=True)
        totals[b * many : (b + 1) * many, :] = jnp.broadcast_to(total, (many, LANES))
    for b in range(blocks):
        values = nv_scr[b * fresh : (b + 1) * fresh, :]
        new_values = jnp.concatenate([values, empty]).astype(BF)
        num[b * many : (b + 1) * many, :] = matmul(
            weight[b, :, :cols], rows_of(v_ref, b, cols)
        ) + matmul(weight[b, :, cols:], new_values)

    lane = iota((rows, LANES), 1)
    for t in range(parts):
        slot = tensor_pos ^ t
        side = jnp.zeros((rows, LANES), F32)
        for h in range(heads_own):
            which = pl.ds(t * heads_own + h, rows, stride=heads)
            out_ref[slot, :, h * hd : (h + 1) * hd] = num[which, :].astype(BF)
            total = totals[which, :]
            high = total.astype(BF).astype(F32)
            side = jnp.where(lane == h, tops[which, :], side)
            side = jnp.where(lane == heads_own + h, high, side)
            side = jnp.where(lane == 2 * heads_own + h, total - high, side)
        out_ref[slot, :, heads_own * hd :] = side.astype(BF)
    ahead.wait()


def attention(
    lengths,
    queries,
    new_keys,
    new_values,
    key_cache,
    value_cache,
    qg,
    kg,
    expert_ids,
    gate_weights,
    parts,
    lanes,
    later,
):
    rows, heads, hd = queries.shape
    kvh, cache = key_cache.shape[1:3]
    args = (
        lengths,
        queries,
        new_keys,
        new_values,
        key_cache,
        value_cache,
        qg.reshape(1, -1),
        kg.reshape(1, -1),
        expert_ids,
        gate_weights,
    )
    return pl.pallas_call(
        attention_kernel,
        out_shape=(
            jax.ShapeDtypeStruct((parts, rows, heads // parts * hd + LANES), BF),
            jax.ShapeDtypeStruct((expert_ids.shape[0], lanes), BF),
            pltpu.VMEM(later.shape, later.dtype),
        ),
        in_specs=[pl.BlockSpec(memory_space=pltpu.HBM)] * 11,
        out_specs=(pl.BlockSpec(memory_space=pltpu.VMEM),) * 3,
        scratch_shapes=[pltpu.SMEM(args[0].shape, I32)]
        + [pltpu.VMEM(a.shape, a.dtype) for a in args[1:]]
        + [
            pltpu.VMEM((rows * kvh, hd), F32),
            pltpu.VMEM((rows * kvh, hd), F32),
            pltpu.VMEM((rows * heads, hd), F32),
            pltpu.VMEM((rows * heads, LANES), F32),
            pltpu.VMEM((rows * heads, LANES), F32),
            pltpu.VMEM((rows // 4, 4 * heads, 4 * kvh * (cache + 2)), F32),
            pltpu.VMEM((rows // 4, 4 * heads, 4 * kvh * (cache + 2)), BF),
            pltpu.SemaphoreType.DMA((11,)),
        ],
        compiler_params=pltpu.CompilerParams(vmem_limit_bytes=16 * MIB),
        name="attention",
    )(*[in_hbm(a) for a in (*args, later)])


def projection_kernel(parts, *refs):
    got = refs[:parts]
    w_ref, ahead_hbm, out_ref, ahead_ref, attn, sem = refs[parts:]
    ahead = pltpu.make_async_copy(ahead_hbm, ahead_ref, sem)
    ahead.start()
    tensor_pos = lax.axis_index("tensor")
    depth, width = w_ref.shape
    share = out_ref.shape[2]
    hd = LANES
    heads_own = depth // hd
    size = 512
    sides = [g[:, depth:].astype(F32) for g in got]
    tops = [s[:, :heads_own] for s in sides]
    top = functools.reduce(jnp.maximum, tops)
    factors = [jnp.exp(t - top) for t in tops]
    totals = [
        f * (s[:, heads_own : 2 * heads_own] + s[:, 2 * heads_own : 3 * heads_own])
        for f, s in zip(factors, sides)
    ]
    total = functools.reduce(jnp.add, totals)
    factors = [f / total for f in factors]
    for h in range(heads_own):
        cols = slice(h * hd, (h + 1) * hd)
        terms = [g[:, cols].astype(F32) * f[:, h : h + 1] for g, f in zip(got, factors)]
        attn[:, cols] = functools.reduce(jnp.add, terms).astype(BF)
    for i in range(width // size):
        cols = slice(i * size, (i + 1) * size)
        result = matmul(attn[...], w_ref[:, cols])
        for t in range(parts):
            slot = tensor_pos ^ t
            out_ref[slot & 1, slot >> 1, :, cols] = result[t * share : (t + 1) * share].astype(BF)
    ahead.wait()


def projection(got, out_proj, share, later):
    parts = len(got)
    rows = got[0].shape[0]
    depth, width = out_proj.shape
    vmem = pl.BlockSpec(memory_space=pltpu.VMEM)
    return pl.pallas_call(
        functools.partial(projection_kernel, parts),
        out_shape=(
            jax.ShapeDtypeStruct((2, parts // 2, share, width), BF),
            pltpu.VMEM(later.shape, later.dtype),
        ),
        in_specs=[vmem] * (parts + 1) + [pl.BlockSpec(memory_space=pltpu.HBM)],
        out_specs=(vmem, vmem),
        scratch_shapes=[pltpu.VMEM((rows, depth), BF), pltpu.SemaphoreType.DMA],
        compiler_params=pltpu.CompilerParams(vmem_limit_bytes=12 * MIB),
        name="projection",
    )(*got, out_proj, in_hbm(later))


def expert_kernel(slots, x_ref, gate, up, down_hbm, out_ref, down, xc, act, res, sem):
    own = lax.axis_index("dp") * lax.axis_size("tensor") + lax.axis_index("tensor")
    rows = x_ref.shape[0]
    _, width, hidden = gate.shape
    padded = res.shape[0]
    fsize = 384
    dsize = 1024
    chunks = width // dsize

    def down_copy(i):
        cols = pl.ds(i * dsize, dsize)
        return pltpu.make_async_copy(down_hbm.at[0, :, cols], down.at[:, cols], sem.at[i])

    for i in range(chunks):
        down_copy(i).start()
    table = x_ref[:, width:]
    pick = (iota((16, table.shape[1]), 1) == own).astype(F32).astype(BF)
    named = matmul_t(pick, table) != 0.0
    before = (iota((rows, rows), 0) < iota((rows, rows), 1)).astype(F32).astype(BF)
    place = matmul(named.astype(F32).astype(BF), before)
    place = jnp.where(named, place, -1.0)[:1]
    take = (iota((slots, rows), 0).astype(F32) == place).astype(F32).astype(BF)
    for i in range(chunks):
        cols = slice(i * dsize, (i + 1) * dsize)
        xc[:, cols] = matmul(take, x_ref[:, cols]).astype(BF)

    lane = iota(table.shape, 1)
    weight = jnp.sum(jnp.where(lane == own, table.astype(F32), 0.0), axis=1, keepdims=True)
    named = jnp.broadcast_to((weight != 0.0).astype(F32), (rows, LANES)).astype(BF)
    after = (iota((rows, rows), 1) < iota((rows, rows), 0)).astype(F32).astype(BF)
    place = matmul(after, named)[:, :1]
    spread = jnp.where(iota((rows, padded), 1).astype(F32) == place, weight, 0.0).astype(BF)
    if padded > slots:
        res[slots:, :] = jnp.zeros((padded - slots, dsize), BF)

    for i in range(hidden // fsize):
        cols = slice(i * fsize, (i + 1) * fsize)
        g = matmul(xc[...], gate[0, :, cols])
        u = matmul(xc[...], up[0, :, cols])
        act[:, cols] = (g / (1.0 + jnp.exp(-g)) * u).astype(BF)
    for i in range(chunks):
        down_copy(i).wait()
        cols = slice(i * dsize, (i + 1) * dsize)
        res[:slots, :] = matmul(act[...], down[:, cols]).astype(BF)
        out_ref[:, cols] = matmul(spread, res[...]).astype(BF)


def experts(x, expert_gate, expert_up, expert_down, share):
    rows = x.shape[0]
    _, width, hidden = expert_gate.shape
    slots = rows // share * CAP
    vmem = pl.BlockSpec(memory_space=pltpu.VMEM)
    return pl.pallas_call(
        functools.partial(expert_kernel, slots),
        out_shape=jax.ShapeDtypeStruct((rows, width), BF),
        in_specs=[vmem] * 3 + [pl.BlockSpec(memory_space=pltpu.HBM)],
        out_specs=vmem,
        scratch_shapes=[
            pltpu.VMEM((hidden, width), BF),
            pltpu.VMEM((slots, width), BF),
            pltpu.VMEM((slots, hidden), BF),
            pltpu.VMEM((-(-slots // LANES) * LANES, 1024), BF),
            pltpu.SemaphoreType.DMA((width // 1024,)),
        ],
        compiler_params=pltpu.CompilerParams(vmem_limit_bytes=(16 + rows // 32) * MIB),
        name="experts",
    )(x, expert_gate, expert_up, in_hbm(expert_down))


class Plan:
    def __init__(self, dp, tensor):
        self.zlen = min(4, dp)
        xlen, ylen = dp // self.zlen, tensor // 2
        self.count = dp * tensor
        self.core = 1
        self.y = [2 * j for j in range(1, ylen)]
        self.z = [tensor * xlen * j for j in range(1, self.zlen)]
        self.plane = [
            tensor * jx + 2 * jy for jx in range(xlen) for jy in range(ylen) if jx or jy
        ]

    def swap(self, value, flip):
        return lax.ppermute(value, ("dp", "tensor"), [(i, i ^ flip) for i in range(self.count)])

    def swaps(self, values, flips):
        pairs = list(zip(values, flips))[::-1]
        return [self.swap(value.astype(BF), flip) for value, flip in pairs][::-1]

    def spread(self, value, flips):
        return self.swaps([value] * len(flips), flips)


def total_of(values):
    return functools.reduce(jnp.add, [v.astype(F32) for v in values])


def shards(
    queries,
    new_keys,
    new_values,
    key_cache,
    value_cache,
    lengths,
    residual_in,
    query_gain,
    key_gain,
    out_proj,
    norm_gain,
    expert_ids,
    gate_weights,
    expert_gate,
    expert_up,
    expert_down,
):
    tensor = lax.axis_size("tensor")
    dp = lax.axis_size("dp")
    plan = Plan(dp, tensor)
    share, width = residual_in.shape
    lanes = -(-dp * tensor // LANES) * LANES

    local, table, out_proj = attention(
        lengths,
        queries,
        new_keys,
        new_values,
        key_cache,
        value_cache,
        query_gain,
        key_gain,
        expert_ids,
        gate_weights,
        tensor,
        lanes,
        out_proj,
    )
    got = [local[0]] + plan.swaps(list(local[1:]), list(range(1, tensor)))
    partial, expert_gate = projection(got, out_proj, share, expert_gate)
    pair = total_of([partial[0], plan.swap(partial[1], plan.core)])
    projected = total_of([pair[0]] + plan.swaps(list(pair[1:]), plan.y))
    hidden = residual_in.astype(F32) + projected
    normed = rms_scale(hidden, norm_gain).astype(BF)

    mine = jnp.concatenate([normed, table], axis=1)
    others = plan.spread(mine, plan.z)
    near = plan.spread(mine + others[0][:, :1] * 0, plan.plane)
    far = plan.spread(jnp.concatenate(others), plan.plane)
    pieces = [jnp.concatenate([mine] + others + near)] + far
    x = jnp.concatenate(pieces + [plan.swap(piece, plan.core) for piece in pieces])

    result = experts(x, expert_gate, expert_up, expert_down, share)

    sizes = [piece.shape[0] for piece in pieces]
    starts = [sum(sizes[:i]) for i in range(len(sizes) + 1)]
    every = starts[-1]
    sums = [
        total_of(
            [
                result[starts[i] : starts[i + 1]],
                plan.swap(result[every + starts[i] : every + starts[i + 1]], plan.core),
            ]
        )
        for i in reversed(range(len(sizes)))
    ][::-1]
    blocks = sums[0].reshape(-1, share, width)
    far = plan.swaps(sums[1:], plan.plane)
    others = total_of([sums[0][share : plan.zlen * share]] + far).reshape(-1, share, width)
    near = plan.swaps(list(blocks[plan.zlen :]), plan.plane)
    moe_sum = total_of([blocks[0]] + near + plan.swaps(list(others), plan.z))
    return (hidden + moe_sum).astype(BF)


def solution(mesh):
    return jax.shard_map(
        shards,
        mesh=mesh,
        in_specs=(
            P("dp", None, None),
            P("dp", None, None),
            P("dp", None, None),
            P("dp", None, "tensor", None),
            P("dp", None, "tensor", None),
            P("dp"),
            P(("dp", "tensor"), None),
            P(),
            P(),
            P("tensor", None),
            P(),
            P(("dp", "tensor"), None),
            P(("dp", "tensor"), None),
            P(("dp", "tensor"), None, None),
            P(("dp", "tensor"), None, None),
            P(("dp", "tensor"), None, None),
        ),
        out_specs=P(("dp", "tensor"), None),
        check_vma=False,
    )
```

```python
import functools

import jax
import jax.numpy as jnp
from jax import lax
from jax.experimental import pallas as pl
from jax.experimental.pallas import tpu as pltpu
from jax.sharding import PartitionSpec as P

BF = jnp.bfloat16
F32 = jnp.float32
I32 = jnp.int32
MIB = 1 << 20
LANES = 128
CAP = 3


def rms_scale(values, gain):
    mean_sq = jnp.mean(values * values, axis=-1, keepdims=True)
    return values * lax.rsqrt(mean_sq + 1e-06) * gain


def matmul(a, b):
    return jnp.dot(a, b, preferred_element_type=F32)


def matmul_t(a, b):
    return lax.dot_general(a, b, (((1,), (1,)), ((), ())), preferred_element_type=F32)


def iota(shape, dim):
    return lax.broadcasted_iota(I32, shape, dim)


def in_hbm(value):
    return pltpu.with_memory_space_constraint(value, pltpu.HBM)


def attention_kernel(flip, *refs):
    sources, refs = refs[:8], refs[8:]
    if flip == 0:
        ids_hbm, gates_hbm, w_hbm, _, out_ref, table_ref, w_ref = refs[:7]
        refs = refs[7:]
    else:
        out_ref, refs = refs[0], refs[1:]
    len_hbm, q_hbm, nk_hbm, nv_hbm, k_hbm, v_hbm, qg_hbm, kg_hbm = sources
    lengths, q_ref, nk_ref, nv_ref, k_ref, v_ref, qg_ref, kg_ref = refs[:8]
    nk_scr, nv_scr, num, tops, totals, score, weight, sem = refs[8:16]
    tensor_pos = lax.axis_index("tensor")
    rows, group, hd = q_ref.shape
    kvh, cache = k_hbm.shape[1], k_ref.shape[1]
    heads_own = q_hbm.shape[1] // lax.axis_size("tensor")
    parts = group // heads_own
    which = (tensor_pos // parts) ^ flip
    heads = pl.ds(pl.multiple_of(which * group, group), group)
    pairs = [
        (len_hbm, lengths),
        (nk_hbm, nk_ref),
        (nv_hbm, nv_ref),
        (qg_hbm, qg_ref),
        (kg_hbm, kg_ref),
        (q_hbm.at[:, heads], q_ref),
        (k_hbm.at[:, which], k_ref),
        (v_hbm.at[:, which], v_ref),
    ]
    if flip == 0:
        ids_ref, gates_ref = refs[16:]
        pairs = [(ids_hbm, ids_ref), (gates_hbm, gates_ref)] + pairs + [(w_hbm, w_ref)]
    copies = [pltpu.make_async_copy(src, dst, sem.at[i]) for i, (src, dst) in enumerate(pairs)]
    for c in copies:
        c.start()
    if flip == 0:
        for c in copies[:2]:
            c.wait()
        ahead = copies[-1]
        copies = copies[2:-1]
        gates = gates_ref[...]
        route = (gates / jnp.sum(gates, axis=1, keepdims=True)).astype(BF).astype(F32)
        expert = iota(table_ref.shape, 1)
        table = jnp.zeros(table_ref.shape, F32)
        for k in range(gates.shape[1]):
            table = jnp.where(expert == ids_ref[:, k : k + 1], route[:, k : k + 1], table)
        table_ref[...] = table.astype(BF)

    step = 8
    blocks = rows // step
    many, cols = step * group, step * cache
    scaling = hd ** (-0.5)
    same = iota((many, cols), 0) // group == iota((many, cols), 1) // cache
    col_row = iota((1, cols), 1) // cache
    col_pos = iota((1, cols), 1) % cache + tensor_pos * cache
    new_here = iota((many, 2 * step), 1) == iota((many, 2 * step), 0) // group
    new_here = new_here & (tensor_pos == 0)

    for c in copies[:5]:
        c.wait()
    for r in range(rows):
        nk_scr[r * kvh : (r + 1) * kvh, :] = nk_ref[r].astype(F32)
        nv_scr[r * kvh : (r + 1) * kvh, :] = nv_ref[r].astype(F32)
    query_gain = qg_ref[...]
    new_rows = pl.ds(which, rows, stride=kvh)
    key_norm = rms_scale(nk_scr[new_rows, :], kg_ref[...])
    new_value = nv_scr[new_rows, :]
    empty = jnp.zeros((step, hd), F32)
    for c in copies[5:]:
        c.wait()

    def rows_of(ref, b, size):
        return ref[b * step : (b + 1) * step].reshape(size, hd)

    def with_empty(value, b):
        return jnp.concatenate([value[b * step : (b + 1) * step], empty]).astype(BF)

    queries = []
    for b in range(blocks):
        query = rows_of(q_ref, b, many).astype(F32)
        queries.append(rms_scale(query, query_gain).astype(BF))
    for b in range(blocks):
        limit = jnp.zeros((1, cols), I32)
        for i in range(step):
            limit = jnp.where(col_row == i, lengths[b * step + i], limit)
        included = same & (col_pos < limit)
        scores = matmul_t(queries[b], rows_of(k_ref, b, cols)) * scaling
        score[b, :, :cols] = jnp.where(included, scores, -1e30)
        scores = matmul_t(queries[b], with_empty(key_norm, b)) * scaling
        score[b, :, cols:] = jnp.where(new_here, scores, -1e30)
    for b in range(blocks):
        top = jnp.maximum(jnp.max(score[b], axis=1, keepdims=True), -1e29).astype(BF).astype(F32)
        tops[b * many : (b + 1) * many, :] = jnp.broadcast_to(top, (many, LANES))
    for b in range(blocks):
        top = tops[b * many : (b + 1) * many, 0:1]
        weights = jnp.exp(score[b] - top).astype(BF)
        weight[b] = weights
        total = jnp.sum(weights.astype(F32), axis=1, keepdims=True)
        totals[b * many : (b + 1) * many, :] = jnp.broadcast_to(total, (many, LANES))
    for b in range(blocks):
        num[b * many : (b + 1) * many, :] = matmul(
            weight[b, :, :cols], rows_of(v_ref, b, cols)
        ) + matmul(weight[b, :, cols:], with_empty(new_value, b))

    lane = iota((rows, LANES), 1)
    for t in range(parts):
        slot = (tensor_pos % parts) ^ t
        side = jnp.zeros((rows, LANES), F32)
        for h in range(heads_own):
            own = pl.ds(t * heads_own + h, rows, stride=group)
            out_ref[slot, :, h * hd : (h + 1) * hd] = num[own, :].astype(BF)
            total = totals[own, :]
            high = total.astype(BF).astype(F32)
            side = jnp.where(lane == h, tops[own, :], side)
            side = jnp.where(lane == heads_own + h, high, side)
            side = jnp.where(lane == 2 * heads_own + h, total - high, side)
        out_ref[slot, :, heads_own * hd :] = side.astype(BF)
    if flip == 0:
        ahead.wait()


def attention(
    flip, lengths, queries, new_keys, new_values, key_cache, value_cache, qg, kg, parts, more
):
    rows, heads, hd = queries.shape
    kvh, cache = key_cache.shape[1:3]
    group = heads // kvh
    blocks = rows // 8
    args = [lengths, queries, new_keys, new_values, key_cache, value_cache]
    args = [in_hbm(a) for a in (*args, qg.reshape(1, -1), kg.reshape(1, -1))]
    outs = [jax.ShapeDtypeStruct((parts // kvh, rows, heads // parts * hd + LANES), BF)]
    scratch = [
        pltpu.SMEM((rows,), I32),
        pltpu.VMEM((rows, group, hd), BF),
        pltpu.VMEM(new_keys.shape, BF),
        pltpu.VMEM(new_values.shape, BF),
        pltpu.VMEM((rows, cache, hd), BF),
        pltpu.VMEM((rows, cache, hd), BF),
        pltpu.VMEM((1, hd), F32),
        pltpu.VMEM((1, hd), F32),
        pltpu.VMEM((rows * kvh, hd), F32),
        pltpu.VMEM((rows * kvh, hd), F32),
        pltpu.VMEM((rows * group, hd), F32),
        pltpu.VMEM((rows * group, LANES), F32),
        pltpu.VMEM((rows * group, LANES), F32),
        pltpu.VMEM((blocks, 8 * group, 8 * (cache + 2)), F32),
        pltpu.VMEM((blocks, 8 * group, 8 * (cache + 2)), BF),
        pltpu.SemaphoreType.DMA((11,)),
    ]
    specs = [pl.BlockSpec(memory_space=pltpu.HBM)] * len(args)
    size = 2 * rows * group * hd * 8
    if flip == 0:
        expert_ids, gate_weights, lanes, later, earlier = more
        args += [in_hbm(a) for a in (expert_ids, gate_weights, later)] + [earlier]
        specs += [pl.BlockSpec(memory_space=pltpu.HBM)] * 3 + [pl.BlockSpec(memory_space=pl.ANY)]
        outs.append(jax.ShapeDtypeStruct((expert_ids.shape[0], lanes), BF))
        outs.append(pltpu.VMEM(later.shape, later.dtype))
        scratch += [pltpu.VMEM(expert_ids.shape, I32), pltpu.VMEM(gate_weights.shape, F32)]
        size = size + 2 * later.size
    return pl.pallas_call(
        functools.partial(attention_kernel, flip),
        out_shape=tuple(outs),
        in_specs=specs,
        out_specs=(pl.BlockSpec(memory_space=pltpu.VMEM),) * len(outs),
        scratch_shapes=scratch,
        compiler_params=pltpu.CompilerParams(vmem_limit_bytes=16 * MIB),
        cost_estimate=pl.CostEstimate(flops=size, bytes_accessed=size, transcendentals=0),
        name="attention",
    )(*args)


def projection_kernel(parts, *refs):
    got = refs[:parts]
    w_ref, ahead_hbm, out_ref, ahead_ref, attn, sem = refs[parts:]
    ahead = pltpu.make_async_copy(ahead_hbm, ahead_ref, sem)
    ahead.start()
    tensor_pos = lax.axis_index("tensor")
    depth, width = w_ref.shape
    share = out_ref.shape[2]
    hd = LANES
    heads_own = depth // hd
    size = 512
    sides = [g[:, depth:].astype(F32) for g in got]
    tops = [s[:, :heads_own] for s in sides]
    top = functools.reduce(jnp.maximum, tops)
    factors = [jnp.exp(t - top) for t in tops]
    totals = [
        f * (s[:, heads_own : 2 * heads_own] + s[:, 2 * heads_own : 3 * heads_own])
        for f, s in zip(factors, sides)
    ]
    total = functools.reduce(jnp.add, totals)
    factors = [f / total for f in factors]
    for h in range(heads_own):
        cols = slice(h * hd, (h + 1) * hd)
        terms = [g[:, cols].astype(F32) * f[:, h : h + 1] for g, f in zip(got, factors)]
        attn[:, cols] = functools.reduce(jnp.add, terms).astype(BF)
    for i in range(width // size):
        cols = slice(i * size, (i + 1) * size)
        result = matmul(attn[...], w_ref[:, cols])
        for t in range(parts):
            slot = tensor_pos ^ t
            out_ref[slot & 1, slot >> 1, :, cols] = result[t * share : (t + 1) * share].astype(BF)
    ahead.wait()


def projection(got, out_proj, share, later):
    parts = len(got)
    rows = got[0].shape[0]
    depth, width = out_proj.shape
    vmem = pl.BlockSpec(memory_space=pltpu.VMEM)
    return pl.pallas_call(
        functools.partial(projection_kernel, parts),
        out_shape=(
            jax.ShapeDtypeStruct((2, parts // 2, share, width), BF),
            pltpu.VMEM(later.shape, later.dtype),
        ),
        in_specs=[vmem] * (parts + 1) + [pl.BlockSpec(memory_space=pltpu.HBM)],
        out_specs=(vmem, vmem),
        scratch_shapes=[pltpu.VMEM((rows, depth), BF), pltpu.SemaphoreType.DMA],
        compiler_params=pltpu.CompilerParams(vmem_limit_bytes=12 * MIB),
        name="projection",
    )(*got, out_proj, in_hbm(later))


def expert_kernel(slots, sizes, *refs):
    x_ref, gate, up, down_hbm = refs[:4]
    outs = refs[4 : 4 + len(sizes)]
    down, xc, act, res, sem = refs[4 + len(sizes) :]
    own = lax.axis_index("dp") * lax.axis_size("tensor") + lax.axis_index("tensor")
    rows = x_ref.shape[0]
    _, width, hidden = gate.shape
    padded = res.shape[0]
    fsize = 384
    dsize = 1024
    chunks = width // dsize

    def down_copy(i):
        cols = pl.ds(i * dsize, dsize)
        return pltpu.make_async_copy(down_hbm.at[0, :, cols], down.at[:, cols], sem.at[i])

    for i in range(chunks):
        down_copy(i).start()
    table = x_ref[:, width:]
    pick = (iota((16, table.shape[1]), 1) == own).astype(F32).astype(BF)
    named = matmul_t(pick, table) != 0.0
    before = (iota((rows, rows), 0) < iota((rows, rows), 1)).astype(F32).astype(BF)
    place = matmul(named.astype(F32).astype(BF), before)
    place = jnp.where(named, place, -1.0)[:1]
    take = (iota((slots, rows), 0).astype(F32) == place).astype(F32).astype(BF)
    for i in range(chunks):
        cols = slice(i * dsize, (i + 1) * dsize)
        xc[:, cols] = matmul(take, x_ref[:, cols]).astype(BF)

    lane = iota(table.shape, 1)
    weight = jnp.sum(jnp.where(lane == own, table.astype(F32), 0.0), axis=1, keepdims=True)
    named = jnp.broadcast_to((weight != 0.0).astype(F32), (rows, LANES)).astype(BF)
    after = (iota((rows, rows), 1) < iota((rows, rows), 0)).astype(F32).astype(BF)
    place = matmul(after, named)[:, :1]
    spread = jnp.where(iota((rows, padded), 1).astype(F32) == place, weight, 0.0).astype(BF)
    if padded > slots:
        res[slots:, :] = jnp.zeros((padded - slots, dsize), BF)

    for i in range(hidden // fsize):
        cols = slice(i * fsize, (i + 1) * fsize)
        g = matmul(xc[...], gate[0, :, cols])
        u = matmul(xc[...], up[0, :, cols])
        act[:, cols] = (g / (1.0 + jnp.exp(-g)) * u).astype(BF)
    for i in range(chunks):
        down_copy(i).wait()
        cols = slice(i * dsize, (i + 1) * dsize)
        res[:slots, :] = matmul(act[...], down[:, cols]).astype(BF)
        result, start = matmul(spread, res[...]), 0
        for size, out in zip(sizes, outs):
            out[:, cols] = result[start : start + size].astype(BF)
            start += size


def experts(x, expert_gate, expert_up, expert_down, share, sizes):
    rows = x.shape[0]
    _, width, hidden = expert_gate.shape
    slots = rows // share * CAP
    vmem = pl.BlockSpec(memory_space=pltpu.VMEM)
    return pl.pallas_call(
        functools.partial(expert_kernel, slots, sizes),
        out_shape=tuple(jax.ShapeDtypeStruct((size, width), BF) for size in sizes),
        in_specs=[vmem] * 3 + [pl.BlockSpec(memory_space=pltpu.HBM)],
        out_specs=(vmem,) * len(sizes),
        scratch_shapes=[
            pltpu.VMEM((hidden, width), BF),
            pltpu.VMEM((slots, width), BF),
            pltpu.VMEM((slots, hidden), BF),
            pltpu.VMEM((-(-slots // LANES) * LANES, 1024), BF),
            pltpu.SemaphoreType.DMA((width // 1024,)),
        ],
        compiler_params=pltpu.CompilerParams(vmem_limit_bytes=(16 + rows // 32) * MIB),
        name="experts",
    )(x, expert_gate, expert_up, in_hbm(expert_down))


class Plan:
    def __init__(self, dp, tensor):
        self.zlen = min(4, dp)
        xlen, ylen = dp // self.zlen, tensor // 2
        self.count = dp * tensor
        self.core = 1
        self.y = [2 * j for j in range(1, ylen)]
        self.z = [tensor * xlen * j for j in range(1, self.zlen)]
        self.plane = [
            tensor * jx + 2 * jy for jx in range(xlen) for jy in range(ylen) if jx or jy
        ]

    def swap(self, value, flip):
        return lax.ppermute(value, ("dp", "tensor"), [(i, i ^ flip) for i in range(self.count)])

    def swaps(self, values, flips):
        pairs = list(zip(values, flips))[::-1]
        return [self.swap(value.astype(BF), flip) for value, flip in pairs][::-1]

    def spread(self, value, flips):
        return self.swaps([value] * len(flips), flips)


def total_of(values):
    return functools.reduce(jnp.add, [v.astype(F32) for v in values])


def shards(
    queries,
    new_keys,
    new_values,
    key_cache,
    value_cache,
    lengths,
    residual_in,
    query_gain,
    key_gain,
    out_proj,
    norm_gain,
    expert_ids,
    gate_weights,
    expert_gate,
    expert_up,
    expert_down,
):
    tensor = lax.axis_size("tensor")
    dp = lax.axis_size("dp")
    plan = Plan(dp, tensor)
    share, width = residual_in.shape
    lanes = -(-dp * tensor // LANES) * LANES

    inputs = (lengths, queries, new_keys, new_values, key_cache, value_cache, query_gain, key_gain)
    groups = key_cache.shape[1]
    got, local = [], None
    for flip in reversed(range(groups)):
        more = (expert_ids, gate_weights, lanes, out_proj, local)
        results = attention(flip, *inputs, tensor, more)
        local = results[0]
        for j in range(0, tensor // groups, 2):
            far = flip * (tensor // groups) + j
            pair = local[j : j + 2]
            if far:
                pair = plan.swap(pair, far)
            got += [pair[0], plan.swap(pair[1], plan.core)]
    _, table, out_proj = results
    partial, expert_gate = projection(got, out_proj, share, expert_gate)
    pair = total_of([partial[0], plan.swap(partial[1], plan.core)])
    projected = total_of([pair[0]] + plan.swaps(list(pair[1:]), plan.y))
    hidden = residual_in.astype(F32) + projected
    normed = rms_scale(hidden, norm_gain).astype(BF)

    mine = jnp.concatenate([normed, table], axis=1)
    others = plan.spread(mine, plan.z)
    near = plan.spread(mine + others[0][:, :1] * 0, plan.plane)
    far = plan.spread(jnp.concatenate(others), plan.plane)
    pieces = [jnp.concatenate([mine] + others + near)] + far
    x = jnp.concatenate(pieces + [plan.swap(piece, plan.core) for piece in pieces])

    sizes = [piece.shape[0] for piece in pieces] * 2
    results = experts(x, expert_gate, expert_up, expert_down, share, sizes)

    half = len(pieces)
    sums = [
        total_of([results[i], plan.swap(results[half + i], plan.core)])
        for i in reversed(range(half))
    ][::-1]
    blocks = sums[0].reshape(-1, share, width)
    far = plan.swaps(sums[1:], plan.plane)
    others = total_of([sums[0][share : plan.zlen * share]] + far).reshape(-1, share, width)
    near = plan.swaps(list(blocks[plan.zlen :]), plan.plane)
    moe_sum = total_of([blocks[0]] + near + plan.swaps(list(others), plan.z))
    return (hidden + moe_sum).astype(BF)


def solution(mesh):
    return jax.shard_map(
        shards,
        mesh=mesh,
        in_specs=(
            P("dp", None, None),
            P("dp", None, None),
            P("dp", None, None),
            P("dp", None, "tensor", None),
            P("dp", None, "tensor", None),
            P("dp"),
            P(("dp", "tensor"), None),
            P(),
            P(),
            P("tensor", None),
            P(),
            P(("dp", "tensor"), None),
            P(("dp", "tensor"), None),
            P(("dp", "tensor"), None, None),
            P(("dp", "tensor"), None, None),
            P(("dp", "tensor"), None, None),
        ),
        out_specs=P(("dp", "tensor"), None),
        check_vma=False,
    )
```

```python
import functools

import jax
import jax.numpy as jnp
from jax import lax
from jax.experimental import pallas as pl
from jax.experimental.pallas import tpu as pltpu
from jax.sharding import PartitionSpec as P

BF = jnp.bfloat16
F32 = jnp.float32
I32 = jnp.int32
MIB = 1 << 20
LANES = 128
CAP = 3


def rms_scale(values, gain):
    mean_sq = jnp.mean(values * values, axis=-1, keepdims=True)
    return values * lax.rsqrt(mean_sq + 1e-06) * gain


def matmul(a, b):
    return jnp.dot(a, b, preferred_element_type=F32)


def matmul_t(a, b):
    return lax.dot_general(a, b, (((1,), (1,)), ((), ())), preferred_element_type=F32)


def iota(shape, dim):
    return lax.broadcasted_iota(I32, shape, dim)


def in_hbm(value):
    return pltpu.with_memory_space_constraint(value, pltpu.HBM)


def attention_kernel(flip, *refs):
    sources, refs = refs[:8], refs[8:]
    w_hbm, refs = refs[0], refs[1:]
    if flip == 0:
        ids_hbm, gates_hbm, _, out_ref, w_ref, table_ref = refs[:6]
        refs = refs[6:]
    else:
        out_ref, w_ref = refs[:2]
        refs = refs[2:]
    len_hbm, q_hbm, nk_hbm, nv_hbm, k_hbm, v_hbm, qg_hbm, kg_hbm = sources
    lengths, q_ref, nk_ref, nv_ref, k_ref, v_ref, qg_ref, kg_ref = refs[:8]
    nk_scr, nv_scr, num, tops, totals, score, weight, sem = refs[8:16]
    tensor_pos = lax.axis_index("tensor")
    rows, group, hd = q_ref.shape
    kvh, cache = k_hbm.shape[1], k_ref.shape[1]
    heads_own = q_hbm.shape[1] // lax.axis_size("tensor")
    parts = group // heads_own
    which = (tensor_pos // parts) ^ flip
    heads = pl.ds(pl.multiple_of(which * group, group), group)
    pairs = [
        (len_hbm, lengths),
        (nk_hbm, nk_ref),
        (nv_hbm, nv_ref),
        (qg_hbm, qg_ref),
        (kg_hbm, kg_ref),
        (q_hbm.at[:, heads], q_ref),
        (k_hbm.at[:, which], k_ref),
        (v_hbm.at[:, which], v_ref),
    ]
    if flip == 0:
        ids_ref, gates_ref = refs[16:]
        pairs = [(ids_hbm, ids_ref), (gates_hbm, gates_ref)] + pairs
    copies = [pltpu.make_async_copy(src, dst, sem.at[i]) for i, (src, dst) in enumerate(pairs)]
    width = w_ref.shape[1]
    ahead = pltpu.make_async_copy(w_hbm.at[:, pl.ds(flip * width, width)], w_ref, sem.at[10])
    for c in copies:
        c.start()
    if flip == 0:
        for c in copies[:2]:
            c.wait()
        copies = copies[2:]
        gates = gates_ref[...]
        route = (gates / jnp.sum(gates, axis=1, keepdims=True)).astype(BF).astype(F32)
        expert = iota(table_ref.shape, 1)
        table = jnp.zeros(table_ref.shape, F32)
        for k in range(gates.shape[1]):
            table = jnp.where(expert == ids_ref[:, k : k + 1], route[:, k : k + 1], table)
        table_ref[...] = table.astype(BF)

    step = 8
    blocks = rows // step
    many, cols = step * group, step * cache
    scaling = hd ** (-0.5)
    same = iota((many, cols), 0) // group == iota((many, cols), 1) // cache
    col_row = iota((1, cols), 1) // cache
    col_pos = iota((1, cols), 1) % cache + tensor_pos * cache
    new_here = iota((many, 2 * step), 1) == iota((many, 2 * step), 0) // group
    new_here = new_here & (tensor_pos == 0)

    for c in copies[:5]:
        c.wait()
    for r in range(rows):
        nk_scr[r * kvh : (r + 1) * kvh, :] = nk_ref[r].astype(F32)
        nv_scr[r * kvh : (r + 1) * kvh, :] = nv_ref[r].astype(F32)
    query_gain = qg_ref[...]
    new_rows = pl.ds(which, rows, stride=kvh)
    key_norm = rms_scale(nk_scr[new_rows, :], kg_ref[...])
    new_value = nv_scr[new_rows, :]
    empty = jnp.zeros((step, hd), F32)
    for c in copies[5:]:
        c.wait()
    ahead.start()

    def rows_of(ref, b, size):
        return ref[b * step : (b + 1) * step].reshape(size, hd)

    def with_empty(value, b):
        return jnp.concatenate([value[b * step : (b + 1) * step], empty]).astype(BF)

    queries = []
    for b in range(blocks):
        query = rows_of(q_ref, b, many).astype(F32)
        queries.append(rms_scale(query, query_gain).astype(BF))
    for b in range(blocks):
        limit = jnp.zeros((1, cols), I32)
        for i in range(step):
            limit = jnp.where(col_row == i, lengths[b * step + i], limit)
        included = same & (col_pos < limit)
        scores = matmul_t(queries[b], rows_of(k_ref, b, cols)) * scaling
        score[b, :, :cols] = jnp.where(included, scores, -1e30)
        scores = matmul_t(queries[b], with_empty(key_norm, b)) * scaling
        score[b, :, cols:] = jnp.where(new_here, scores, -1e30)
    for b in range(blocks):
        top = jnp.maximum(jnp.max(score[b], axis=1, keepdims=True), -1e29).astype(BF).astype(F32)
        tops[b * many : (b + 1) * many, :] = jnp.broadcast_to(top, (many, LANES))
    for b in range(blocks):
        top = tops[b * many : (b + 1) * many, 0:1]
        weights = jnp.exp(score[b] - top).astype(BF)
        weight[b] = weights
        total = jnp.sum(weights.astype(F32), axis=1, keepdims=True)
        totals[b * many : (b + 1) * many, :] = jnp.broadcast_to(total, (many, LANES))
    for b in range(blocks):
        num[b * many : (b + 1) * many, :] = matmul(
            weight[b, :, :cols], rows_of(v_ref, b, cols)
        ) + matmul(weight[b, :, cols:], with_empty(new_value, b))

    lane = iota((rows, LANES), 1)
    for t in range(parts):
        slot = (tensor_pos % parts) ^ t
        side = jnp.zeros((rows, LANES), F32)
        for h in range(heads_own):
            own = pl.ds(t * heads_own + h, rows, stride=group)
            out_ref[slot, :, h * hd : (h + 1) * hd] = num[own, :].astype(BF)
            total = totals[own, :]
            high = total.astype(BF).astype(F32)
            side = jnp.where(lane == h, tops[own, :], side)
            side = jnp.where(lane == heads_own + h, high, side)
            side = jnp.where(lane == 2 * heads_own + h, total - high, side)
        out_ref[slot, :, heads_own * hd :] = side.astype(BF)
    ahead.wait()


def attention(
    flip, lengths, queries, new_keys, new_values, key_cache, value_cache, qg, kg, out_proj, parts, more
):
    rows, heads, hd = queries.shape
    kvh, cache = key_cache.shape[1:3]
    group = heads // kvh
    blocks = rows // 8
    args = [lengths, queries, new_keys, new_values, key_cache, value_cache]
    args = [in_hbm(a) for a in (*args, qg.reshape(1, -1), kg.reshape(1, -1), out_proj)]
    columns = out_proj.shape[1] // kvh
    outs = [
        jax.ShapeDtypeStruct((parts // kvh, rows, heads // parts * hd + LANES), BF),
        pltpu.VMEM((out_proj.shape[0], columns), BF),
    ]
    scratch = [
        pltpu.SMEM((rows,), I32),
        pltpu.VMEM((rows, group, hd), BF),
        pltpu.VMEM(new_keys.shape, BF),
        pltpu.VMEM(new_values.shape, BF),
        pltpu.VMEM((rows, cache, hd), BF),
        pltpu.VMEM((rows, cache, hd), BF),
        pltpu.VMEM((1, hd), F32),
        pltpu.VMEM((1, hd), F32),
        pltpu.VMEM((rows * kvh, hd), F32),
        pltpu.VMEM((rows * kvh, hd), F32),
        pltpu.VMEM((rows * group, hd), F32),
        pltpu.VMEM((rows * group, LANES), F32),
        pltpu.VMEM((rows * group, LANES), F32),
        pltpu.VMEM((blocks, 8 * group, 8 * (cache + 2)), F32),
        pltpu.VMEM((blocks, 8 * group, 8 * (cache + 2)), BF),
        pltpu.SemaphoreType.DMA((11,)),
    ]
    specs = [pl.BlockSpec(memory_space=pltpu.HBM)] * len(args)
    size = 2 * out_proj.shape[0] * columns
    if flip == 0:
        expert_ids, gate_weights, lanes, earlier = more
        args += [in_hbm(expert_ids), in_hbm(gate_weights), earlier]
        specs += [pl.BlockSpec(memory_space=pltpu.HBM)] * 2 + [pl.BlockSpec(memory_space=pl.ANY)]
        outs.append(jax.ShapeDtypeStruct((expert_ids.shape[0], lanes), BF))
        scratch += [pltpu.VMEM(expert_ids.shape, I32), pltpu.VMEM(gate_weights.shape, F32)]
    return pl.pallas_call(
        functools.partial(attention_kernel, flip),
        out_shape=tuple(outs),
        in_specs=specs,
        out_specs=(pl.BlockSpec(memory_space=pltpu.VMEM),) * len(outs),
        scratch_shapes=scratch,
        compiler_params=pltpu.CompilerParams(vmem_limit_bytes=16 * MIB),
        cost_estimate=pl.CostEstimate(flops=size, bytes_accessed=size, transcendentals=0),
        name="attention",
    )(*args)


def projection_kernel(parts, cuts, *refs):
    got = refs[:parts]
    w_refs, refs = refs[parts : parts + cuts], refs[parts + cuts :]
    ahead_hbm, out_ref, ahead_ref, attn, sem = refs
    ahead = pltpu.make_async_copy(ahead_hbm, ahead_ref, sem)
    ahead.start()
    tensor_pos = lax.axis_index("tensor")
    depth, width = w_refs[0].shape
    share = out_ref.shape[2]
    hd = LANES
    heads_own = depth // hd
    size = 512
    sides = [g[:, depth:].astype(F32) for g in got]
    tops = [s[:, :heads_own] for s in sides]
    top = functools.reduce(jnp.maximum, tops)
    factors = [jnp.exp(t - top) for t in tops]
    totals = [
        f * (s[:, heads_own : 2 * heads_own] + s[:, 2 * heads_own : 3 * heads_own])
        for f, s in zip(factors, sides)
    ]
    total = functools.reduce(jnp.add, totals)
    factors = [f / total for f in factors]
    for h in range(heads_own):
        cols = slice(h * hd, (h + 1) * hd)
        terms = [g[:, cols].astype(F32) * f[:, h : h + 1] for g, f in zip(got, factors)]
        attn[:, cols] = functools.reduce(jnp.add, terms).astype(BF)
    for k, w_ref in enumerate(w_refs):
        for start in range(0, width, size):
            result = matmul(attn[...], w_ref[:, start : start + size])
            cols = slice(k * width + start, k * width + start + size)
            for t in range(parts):
                slot = tensor_pos ^ t
                block = result[t * share : (t + 1) * share].astype(BF)
                out_ref[slot & 1, slot >> 1, :, cols] = block
    ahead.wait()


def projection(got, weights, share, later):
    parts = len(got)
    rows = got[0].shape[0]
    depth = weights[0].shape[0]
    width = sum(w.shape[1] for w in weights)
    vmem = pl.BlockSpec(memory_space=pltpu.VMEM)
    return pl.pallas_call(
        functools.partial(projection_kernel, parts, len(weights)),
        out_shape=(
            jax.ShapeDtypeStruct((2, parts // 2, share, width), BF),
            pltpu.VMEM(later.shape, later.dtype),
        ),
        in_specs=[vmem] * (parts + len(weights)) + [pl.BlockSpec(memory_space=pltpu.HBM)],
        out_specs=(vmem, vmem),
        scratch_shapes=[pltpu.VMEM((rows, depth), BF), pltpu.SemaphoreType.DMA],
        compiler_params=pltpu.CompilerParams(vmem_limit_bytes=12 * MIB),
        name="projection",
    )(*got, *weights, in_hbm(later))


def expert_kernel(slots, sizes, *refs):
    x_ref, gate, up, down_hbm = refs[:4]
    outs = refs[4 : 4 + len(sizes)]
    down, xc, act, res, sem = refs[4 + len(sizes) :]
    own = lax.axis_index("dp") * lax.axis_size("tensor") + lax.axis_index("tensor")
    rows = x_ref.shape[0]
    _, width, hidden = gate.shape
    padded = res.shape[0]
    fsize = 384
    dsize = 1024
    chunks = width // dsize

    def down_copy(i):
        cols = pl.ds(i * dsize, dsize)
        return pltpu.make_async_copy(down_hbm.at[0, :, cols], down.at[:, cols], sem.at[i])

    for i in range(chunks):
        down_copy(i).start()
    table = x_ref[:, width:]
    pick = (iota((16, table.shape[1]), 1) == own).astype(F32).astype(BF)
    named = matmul_t(pick, table) != 0.0
    before = (iota((rows, rows), 0) < iota((rows, rows), 1)).astype(F32).astype(BF)
    place = matmul(named.astype(F32).astype(BF), before)
    place = jnp.where(named, place, -1.0)[:1]
    take = (iota((slots, rows), 0).astype(F32) == place).astype(F32).astype(BF)
    for i in range(chunks):
        cols = slice(i * dsize, (i + 1) * dsize)
        xc[:, cols] = matmul(take, x_ref[:, cols]).astype(BF)

    lane = iota(table.shape, 1)
    weight = jnp.sum(jnp.where(lane == own, table.astype(F32), 0.0), axis=1, keepdims=True)
    named = jnp.broadcast_to((weight != 0.0).astype(F32), (rows, LANES)).astype(BF)
    after = (iota((rows, rows), 1) < iota((rows, rows), 0)).astype(F32).astype(BF)
    place = matmul(after, named)[:, :1]
    spread = jnp.where(iota((rows, padded), 1).astype(F32) == place, weight, 0.0).astype(BF)
    if padded > slots:
        res[slots:, :] = jnp.zeros((padded - slots, dsize), BF)

    for i in range(hidden // fsize):
        cols = slice(i * fsize, (i + 1) * fsize)
        g = matmul(xc[...], gate[0, :, cols])
        u = matmul(xc[...], up[0, :, cols])
        act[:, cols] = (g / (1.0 + jnp.exp(-g)) * u).astype(BF)
    for i in range(chunks):
        down_copy(i).wait()
        cols = slice(i * dsize, (i + 1) * dsize)
        res[:slots, :] = matmul(act[...], down[:, cols]).astype(BF)
        result, start = matmul(spread, res[...]), 0
        for size, out in zip(sizes, outs):
            out[:, cols] = result[start : start + size].astype(BF)
            start += size


def experts(x, expert_gate, expert_up, expert_down, share, sizes):
    rows = x.shape[0]
    _, width, hidden = expert_gate.shape
    slots = rows // share * CAP
    vmem = pl.BlockSpec(memory_space=pltpu.VMEM)
    return pl.pallas_call(
        functools.partial(expert_kernel, slots, sizes),
        out_shape=tuple(jax.ShapeDtypeStruct((size, width), BF) for size in sizes),
        in_specs=[vmem] * 3 + [pl.BlockSpec(memory_space=pltpu.HBM)],
        out_specs=(vmem,) * len(sizes),
        scratch_shapes=[
            pltpu.VMEM((hidden, width), BF),
            pltpu.VMEM((slots, width), BF),
            pltpu.VMEM((slots, hidden), BF),
            pltpu.VMEM((-(-slots // LANES) * LANES, 1024), BF),
            pltpu.SemaphoreType.DMA((width // 1024,)),
        ],
        compiler_params=pltpu.CompilerParams(vmem_limit_bytes=(16 + rows // 32) * MIB),
        name="experts",
    )(x, expert_gate, expert_up, in_hbm(expert_down))


class Plan:
    def __init__(self, dp, tensor):
        self.zlen = min(4, dp)
        xlen, ylen = dp // self.zlen, tensor // 2
        self.count = dp * tensor
        self.core = 1
        self.y = [2 * j for j in range(1, ylen)]
        self.z = [tensor * xlen * j for j in range(1, self.zlen)]
        self.plane = [
            tensor * jx + 2 * jy for jx in range(xlen) for jy in range(ylen) if jx or jy
        ]

    def swap(self, value, flip):
        return lax.ppermute(value, ("dp", "tensor"), [(i, i ^ flip) for i in range(self.count)])

    def swaps(self, values, flips):
        pairs = list(zip(values, flips))[::-1]
        return [self.swap(value.astype(BF), flip) for value, flip in pairs][::-1]

    def spread(self, value, flips):
        return self.swaps([value] * len(flips), flips)


def total_of(values):
    return functools.reduce(jnp.add, [v.astype(F32) for v in values])


def shards(
    queries,
    new_keys,
    new_values,
    key_cache,
    value_cache,
    lengths,
    residual_in,
    query_gain,
    key_gain,
    out_proj,
    norm_gain,
    expert_ids,
    gate_weights,
    expert_gate,
    expert_up,
    expert_down,
):
    tensor = lax.axis_size("tensor")
    dp = lax.axis_size("dp")
    plan = Plan(dp, tensor)
    share, width = residual_in.shape
    lanes = -(-dp * tensor // LANES) * LANES

    inputs = (lengths, queries, new_keys, new_values, key_cache, value_cache, query_gain, key_gain)
    groups = key_cache.shape[1]
    got, local, weights = [], None, []
    for flip in reversed(range(groups)):
        more = (expert_ids, gate_weights, lanes, local)
        results = attention(flip, *inputs, out_proj, tensor, more)
        local = results[0]
        weights.insert(0, results[1])
        for j in range(0, tensor // groups, 2):
            far = flip * (tensor // groups) + j
            pair = local[j : j + 2]
            if far:
                pair = plan.swap(pair, far)
            got += [pair[0], plan.swap(pair[1], plan.core)]
    table = results[2]
    partial, expert_gate = projection(got, weights, share, expert_gate)
    pair = total_of([partial[0], plan.swap(partial[1], plan.core)])
    projected = total_of([pair[0]] + plan.swaps(list(pair[1:]), plan.y))
    hidden = residual_in.astype(F32) + projected
    normed = rms_scale(hidden, norm_gain).astype(BF)

    mine = jnp.concatenate([normed, table], axis=1)
    others = plan.spread(mine, plan.z)
    near = plan.spread(mine + others[0][:, :1] * 0, plan.plane)
    far = plan.spread(jnp.concatenate(others), plan.plane)
    pieces = [jnp.concatenate([mine] + others + near)] + far
    x = jnp.concatenate(pieces + [plan.swap(piece, plan.core) for piece in pieces])

    sizes = [piece.shape[0] for piece in pieces] * 2
    results = experts(x, expert_gate, expert_up, expert_down, share, sizes)

    half = len(pieces)
    sums = [
        total_of([results[i], plan.swap(results[half + i], plan.core)])
        for i in reversed(range(half))
    ][::-1]
    blocks = sums[0].reshape(-1, share, width)
    far = plan.swaps(sums[1:], plan.plane)[::-1]
    others = total_of(far + [sums[0][share : plan.zlen * share]]).reshape(-1, share, width)
    near = plan.swaps(list(blocks[plan.zlen :]), plan.plane)[::-1]
    moe_sum = total_of(plan.swaps(list(others), plan.z)[::-1] + near + [blocks[0]])
    return (hidden + moe_sum).astype(BF)


def solution(mesh):
    return jax.shard_map(
        shards,
        mesh=mesh,
        in_specs=(
            P("dp", None, None),
            P("dp", None, None),
            P("dp", None, None),
            P("dp", None, "tensor", None),
            P("dp", None, "tensor", None),
            P("dp"),
            P(("dp", "tensor"), None),
            P(),
            P(),
            P("tensor", None),
            P(),
            P(("dp", "tensor"), None),
            P(("dp", "tensor"), None),
            P(("dp", "tensor"), None, None),
            P(("dp", "tensor"), None, None),
            P(("dp", "tensor"), None, None),
        ),
        out_specs=P(("dp", "tensor"), None),
        check_vma=False,
    )
```

```python
import functools

import jax
import jax.numpy as jnp
from jax import lax
from jax.experimental import pallas as pl
from jax.experimental.pallas import tpu as pltpu
from jax.sharding import PartitionSpec as P

BF = jnp.bfloat16
F32 = jnp.float32
I32 = jnp.int32
MIB = 1 << 20
LANES = 128
CAP = 3


def rms_scale(values, gain):
    mean_sq = jnp.mean(values * values, axis=-1, keepdims=True)
    return values * lax.rsqrt(mean_sq + 1e-06) * gain


def matmul(a, b):
    return jnp.dot(a, b, preferred_element_type=F32)


def matmul_t(a, b):
    return lax.dot_general(a, b, (((1,), (1,)), ((), ())), preferred_element_type=F32)


def iota(shape, dim):
    return lax.broadcasted_iota(I32, shape, dim)


def in_hbm(value):
    return pltpu.with_memory_space_constraint(value, pltpu.HBM)


def attend(lengths, q_ref, k_ref, v_ref, key_norm, new_value, query_gain, out_ref, scratch):
    num, tops, totals, score, weight = scratch
    tensor_pos = lax.axis_index("tensor")
    rows, group, hd = q_ref.shape
    cache = k_ref.shape[1]
    parts = out_ref.shape[0]
    heads_own = group // parts
    step = 8
    blocks = rows // step
    many, cols = step * group, step * cache
    scaling = hd ** (-0.5)
    same = iota((many, cols), 0) // group == iota((many, cols), 1) // cache
    col_row = iota((1, cols), 1) // cache
    col_pos = iota((1, cols), 1) % cache + tensor_pos * cache
    new_here = iota((many, 2 * step), 1) == iota((many, 2 * step), 0) // group
    new_here = new_here & (tensor_pos == 0)
    empty = jnp.zeros((step, hd), F32)

    def rows_of(ref, b, size):
        return ref[b * step : (b + 1) * step].reshape(size, hd)

    def with_empty(value, b):
        return jnp.concatenate([value[b * step : (b + 1) * step], empty]).astype(BF)

    queries = []
    for b in range(blocks):
        query = rows_of(q_ref, b, many).astype(F32)
        queries.append(rms_scale(query, query_gain).astype(BF))
    for b in range(blocks):
        limit = jnp.zeros((1, cols), I32)
        for i in range(step):
            limit = jnp.where(col_row == i, lengths[b * step + i], limit)
        included = same & (col_pos < limit)
        scores = matmul_t(queries[b], rows_of(k_ref, b, cols)) * scaling
        score[b, :, :cols] = jnp.where(included, scores, -1e30)
        scores = matmul_t(queries[b], with_empty(key_norm, b)) * scaling
        score[b, :, cols:] = jnp.where(new_here, scores, -1e30)
    for b in range(blocks):
        top = jnp.maximum(jnp.max(score[b], axis=1, keepdims=True), -1e29).astype(BF).astype(F32)
        tops[b * many : (b + 1) * many, :] = jnp.broadcast_to(top, (many, LANES))
    for b in range(blocks):
        top = tops[b * many : (b + 1) * many, 0:1]
        weights = jnp.exp(score[b] - top).astype(BF)
        weight[b] = weights
        total = jnp.sum(weights.astype(F32), axis=1, keepdims=True)
        totals[b * many : (b + 1) * many, :] = jnp.broadcast_to(total, (many, LANES))
    for b in range(blocks):
        num[b * many : (b + 1) * many, :] = matmul(
            weight[b, :, :cols], rows_of(v_ref, b, cols)
        ) + matmul(weight[b, :, cols:], with_empty(new_value, b))

    lane = iota((rows, LANES), 1)
    for t in range(parts):
        slot = (tensor_pos % parts) ^ t
        side = jnp.zeros((rows, LANES), F32)
        for h in range(heads_own):
            own = pl.ds(t * heads_own + h, rows, stride=group)
            out_ref[slot, :, h * hd : (h + 1) * hd] = num[own, :].astype(BF)
            total = totals[own, :]
            high = total.astype(BF).astype(F32)
            side = jnp.where(lane == h, tops[own, :], side)
            side = jnp.where(lane == heads_own + h, high, side)
            side = jnp.where(lane == 2 * heads_own + h, total - high, side)
        out_ref[slot, :, heads_own * hd :] = side.astype(BF)


WEIGHT_COPIES = 4


def weight_copies(w_hbm, w_ref, half, sem):
    rows = w_ref.shape[0]
    size = rows // WEIGHT_COPIES
    return [
        pltpu.make_async_copy(
            w_hbm.at[pl.ds(half * rows + i * size, size)], w_ref.at[pl.ds(i * size, size)], sem.at[i]
        )
        for i in range(WEIGHT_COPIES)
    ]


def other_kernel(
    len_hbm,
    nk_hbm,
    nv_hbm,
    qg_hbm,
    kg_hbm,
    q_hbm,
    k_hbm,
    v_hbm,
    w_hbm,
    out_ref,
    w_ref,
    q_own,
    k_own,
    v_own,
    nk_scr,
    nv_scr,
    qg_ref,
    lengths,
    nk_ref,
    nv_ref,
    kg_ref,
    q_ref,
    k_ref,
    v_ref,
    *refs,
):
    scratch, (sem, wsem) = refs[:5], refs[5:]
    tensor_pos = lax.axis_index("tensor")
    rows, group, _ = q_ref.shape
    kvh = k_hbm.shape[1]
    mine = tensor_pos // out_ref.shape[0]
    which = mine ^ 1

    def heads(index):
        return pl.ds(pl.multiple_of(index * group, group), group)

    pairs = [
        (len_hbm, lengths),
        (nk_hbm, nk_ref),
        (nv_hbm, nv_ref),
        (qg_hbm, qg_ref),
        (kg_hbm, kg_ref),
        (q_hbm.at[:, heads(which)], q_ref),
        (k_hbm.at[:, which], k_ref),
        (v_hbm.at[:, which], v_ref),
        (q_hbm.at[:, heads(mine)], q_own),
        (k_hbm.at[:, mine], k_own),
        (v_hbm.at[:, mine], v_own),
    ]
    copies = [pltpu.make_async_copy(src, dst, sem.at[i]) for i, (src, dst) in enumerate(pairs)]
    weights = weight_copies(w_hbm, w_ref, 0, wsem)
    for c in copies:
        c.start()
    for c in copies[:5]:
        c.wait()
    for r in range(rows):
        nk_scr[r * kvh : (r + 1) * kvh, :] = nk_ref[r].astype(F32)
        nv_scr[r * kvh : (r + 1) * kvh, :] = nv_ref[r].astype(F32)
    nk_scr[...] = rms_scale(nk_scr[...], kg_ref[...])
    for c in copies[5:8]:
        c.wait()
    for c in weights:
        c.start()
    new_rows = pl.ds(which, rows, stride=kvh)
    attend(
        lengths,
        q_ref,
        k_ref,
        v_ref,
        nk_scr[new_rows, :],
        nv_scr[new_rows, :],
        qg_ref[...],
        out_ref,
        scratch,
    )
    for c in copies[8:] + weights:
        c.wait()


def own_kernel(
    len_hbm,
    ids_hbm,
    gates_hbm,
    w_hbm,
    q_ref,
    k_ref,
    v_ref,
    nk_scr,
    nv_scr,
    qg_ref,
    out_ref,
    w_ref,
    table_ref,
    lengths,
    ids_ref,
    gates_ref,
    *refs,
):
    scratch, (sem, wsem) = refs[:5], refs[5:]
    pairs = [(len_hbm, lengths), (ids_hbm, ids_ref), (gates_hbm, gates_ref)]
    copies = [pltpu.make_async_copy(src, dst, sem.at[i]) for i, (src, dst) in enumerate(pairs)]
    copies += weight_copies(w_hbm, w_ref, 1, wsem)
    for c in copies:
        c.start()
    rows = q_ref.shape[0]
    kvh = nk_scr.shape[0] // rows
    new_rows = pl.ds(lax.axis_index("tensor") // out_ref.shape[0], rows, stride=kvh)
    copies[0].wait()
    attend(
        lengths,
        q_ref,
        k_ref,
        v_ref,
        nk_scr[new_rows, :],
        nv_scr[new_rows, :],
        qg_ref[...],
        out_ref,
        scratch,
    )
    for c in copies[1:]:
        c.wait()
    gates = gates_ref[...]
    route = (gates / jnp.sum(gates, axis=1, keepdims=True)).astype(BF).astype(F32)
    expert = iota(table_ref.shape, 1)
    table = jnp.zeros(table_ref.shape, F32)
    for k in range(gates.shape[1]):
        table = jnp.where(expert == ids_ref[:, k : k + 1], route[:, k : k + 1], table)
    table_ref[...] = table.astype(BF)


def attention(
    lengths,
    queries,
    new_keys,
    new_values,
    key_cache,
    value_cache,
    query_gain,
    key_gain,
    expert_ids,
    gate_weights,
    out_proj,
    parts,
    lanes,
):
    rows, heads, hd = queries.shape
    kvh, cache = key_cache.shape[1:3]
    group = heads // kvh
    blocks = rows // 8
    hbm = pl.BlockSpec(memory_space=pltpu.HBM)
    vmem = pl.BlockSpec(memory_space=pltpu.VMEM)
    sums = jax.ShapeDtypeStruct((parts // kvh, rows, heads // parts * hd + LANES), BF)
    half = pltpu.VMEM((out_proj.shape[0] // 2, out_proj.shape[1]), BF)
    operands = [pltpu.VMEM((rows, group, hd), BF)] + [pltpu.VMEM((rows, cache, hd), BF)] * 2
    news = [pltpu.VMEM((rows * kvh, hd), F32)] * 2
    gain = pltpu.VMEM((1, hd), F32)
    scratch = [
        pltpu.VMEM((rows * group, hd), F32),
        pltpu.VMEM((rows * group, LANES), F32),
        pltpu.VMEM((rows * group, LANES), F32),
        pltpu.VMEM((blocks, 8 * group, 8 * (cache + 2)), F32),
        pltpu.VMEM((blocks, 8 * group, 8 * (cache + 2)), BF),
        pltpu.SemaphoreType.DMA((11,)),
        pltpu.SemaphoreType.DMA((WEIGHT_COPIES,)),
    ]
    size = out_proj.size
    settings = dict(
        compiler_params=pltpu.CompilerParams(vmem_limit_bytes=16 * MIB),
        cost_estimate=pl.CostEstimate(flops=size, bytes_accessed=size, transcendentals=0),
    )
    args = (lengths, new_keys, new_values, query_gain.reshape(1, -1), key_gain.reshape(1, -1))
    args = args + (queries, key_cache, value_cache, out_proj)
    other, first, *held = pl.pallas_call(
        other_kernel,
        out_shape=(sums, half, *operands, *news, gain),
        in_specs=[hbm] * len(args),
        out_specs=(vmem,) * 8,
        scratch_shapes=[
            pltpu.SMEM((rows,), I32),
            pltpu.VMEM(new_keys.shape, BF),
            pltpu.VMEM(new_values.shape, BF),
            gain,
            *operands,
            *scratch,
        ],
        name="attention_other",
        **settings,
    )(*[in_hbm(a) for a in args])
    args = (lengths, expert_ids, gate_weights, out_proj)
    own, second, table = pl.pallas_call(
        own_kernel,
        out_shape=(sums, half, jax.ShapeDtypeStruct((expert_ids.shape[0], lanes), BF)),
        in_specs=[hbm] * len(args) + [vmem] * len(held),
        out_specs=(vmem,) * 3,
        scratch_shapes=[
            pltpu.SMEM((rows,), I32),
            pltpu.VMEM(expert_ids.shape, I32),
            pltpu.VMEM(gate_weights.shape, F32),
            *scratch,
        ],
        name="attention_own",
        **settings,
    )(*[in_hbm(a) for a in args], *held)
    return (other, own), (first, second), table


def projection_kernel(parts, cuts, *refs):
    got = refs[:parts]
    w_refs, refs = refs[parts : parts + cuts], refs[parts + cuts :]
    ahead_hbm, out_ref, ahead_ref, attn, sem = refs
    ahead = pltpu.make_async_copy(ahead_hbm, ahead_ref, sem)
    ahead.start()
    tensor_pos = lax.axis_index("tensor")
    width = w_refs[0].shape[1]
    depth = attn.shape[1]
    share = out_ref.shape[2]
    hd = LANES
    heads_own = depth // hd
    size = 512
    sides = [g[:, depth:].astype(F32) for g in got]
    tops = [s[:, :heads_own] for s in sides]
    top = functools.reduce(jnp.maximum, tops)
    factors = [jnp.exp(t - top) for t in tops]
    totals = [
        f * (s[:, heads_own : 2 * heads_own] + s[:, 2 * heads_own : 3 * heads_own])
        for f, s in zip(factors, sides)
    ]
    total = functools.reduce(jnp.add, totals)
    factors = [f / total for f in factors]
    for h in range(heads_own):
        cols = slice(h * hd, (h + 1) * hd)
        terms = [g[:, cols].astype(F32) * f[:, h : h + 1] for g, f in zip(got, factors)]
        attn[:, cols] = functools.reduce(jnp.add, terms).astype(BF)
    part = depth // cuts
    for start in range(0, width, size):
        cols = slice(start, start + size)
        result = functools.reduce(
            jnp.add,
            [
                matmul(attn[:, k * part : (k + 1) * part], w_ref[:, cols])
                for k, w_ref in enumerate(w_refs)
            ],
        )
        for t in range(parts):
            slot = tensor_pos ^ t
            block = result[t * share : (t + 1) * share].astype(BF)
            out_ref[slot & 1, slot >> 1, :, cols] = block
    ahead.wait()


def projection(got, weights, share, later):
    parts = len(got)
    rows = got[0].shape[0]
    depth = sum(w.shape[0] for w in weights)
    width = weights[0].shape[1]
    vmem = pl.BlockSpec(memory_space=pltpu.VMEM)
    return pl.pallas_call(
        functools.partial(projection_kernel, parts, len(weights)),
        out_shape=(
            jax.ShapeDtypeStruct((2, parts // 2, share, width), BF),
            pltpu.VMEM(later.shape, later.dtype),
        ),
        in_specs=[vmem] * (parts + len(weights)) + [pl.BlockSpec(memory_space=pltpu.HBM)],
        out_specs=(vmem, vmem),
        scratch_shapes=[pltpu.VMEM((rows, depth), BF), pltpu.SemaphoreType.DMA],
        compiler_params=pltpu.CompilerParams(vmem_limit_bytes=12 * MIB),
        name="projection",
    )(*got, *weights, in_hbm(later))


def expert_kernel(slots, x_ref, gate, up, down_hbm, out_ref, down, xc, act, res, sem):
    own = lax.axis_index("dp") * lax.axis_size("tensor") + lax.axis_index("tensor")
    rows = x_ref.shape[0]
    _, width, hidden = gate.shape
    padded = res.shape[0]
    fsize = 384
    dsize = 1024
    chunks = width // dsize

    def down_copy(i):
        cols = pl.ds(i * dsize, dsize)
        return pltpu.make_async_copy(down_hbm.at[0, :, cols], down.at[:, cols], sem.at[i])

    for i in range(chunks):
        down_copy(i).start()
    table = x_ref[:, width:]
    pick = (iota((16, table.shape[1]), 1) == own).astype(F32).astype(BF)
    named = matmul_t(pick, table) != 0.0
    before = (iota((rows, rows), 0) < iota((rows, rows), 1)).astype(F32).astype(BF)
    place = matmul(named.astype(F32).astype(BF), before)
    place = jnp.where(named, place, -1.0)[:1]
    take = (iota((slots, rows), 0).astype(F32) == place).astype(F32).astype(BF)
    for i in range(chunks):
        cols = slice(i * dsize, (i + 1) * dsize)
        xc[:, cols] = matmul(take, x_ref[:, cols]).astype(BF)

    lane = iota(table.shape, 1)
    weight = jnp.sum(jnp.where(lane == own, table.astype(F32), 0.0), axis=1, keepdims=True)
    named = jnp.broadcast_to((weight != 0.0).astype(F32), (rows, LANES)).astype(BF)
    after = (iota((rows, rows), 1) < iota((rows, rows), 0)).astype(F32).astype(BF)
    place = matmul(after, named)[:, :1]
    spread = jnp.where(iota((rows, padded), 1).astype(F32) == place, weight, 0.0).astype(BF)
    if padded > slots:
        res[slots:, :] = jnp.zeros((padded - slots, dsize), BF)

    for i in range(hidden // fsize):
        cols = slice(i * fsize, (i + 1) * fsize)
        g = matmul(xc[...], gate[0, :, cols])
        u = matmul(xc[...], up[0, :, cols])
        act[:, cols] = (g / (1.0 + jnp.exp(-g)) * u).astype(BF)
    for i in range(chunks):
        down_copy(i).wait()
        cols = slice(i * dsize, (i + 1) * dsize)
        res[:slots, :] = matmul(act[...], down[:, cols]).astype(BF)
        out_ref[:, cols] = matmul(spread, res[...]).astype(BF)


def experts(x, expert_gate, expert_up, expert_down, share):
    rows = x.shape[0]
    _, width, hidden = expert_gate.shape
    slots = rows // share * CAP
    vmem = pl.BlockSpec(memory_space=pltpu.VMEM)
    return pl.pallas_call(
        functools.partial(expert_kernel, slots),
        out_shape=jax.ShapeDtypeStruct((rows, width), BF),
        in_specs=[vmem] * 3 + [pl.BlockSpec(memory_space=pltpu.HBM)],
        out_specs=vmem,
        scratch_shapes=[
            pltpu.VMEM((hidden, width), BF),
            pltpu.VMEM((slots, width), BF),
            pltpu.VMEM((slots, hidden), BF),
            pltpu.VMEM((-(-slots // LANES) * LANES, 1024), BF),
            pltpu.SemaphoreType.DMA((width // 1024,)),
        ],
        compiler_params=pltpu.CompilerParams(vmem_limit_bytes=(16 + rows // 32) * MIB),
        name="experts",
    )(x, expert_gate, expert_up, in_hbm(expert_down))


class Plan:
    def __init__(self, dp, tensor):
        self.zlen = min(4, dp)
        xlen, ylen = dp // self.zlen, tensor // 2
        self.count = dp * tensor
        self.core = 1
        self.y = [2 * j for j in range(1, ylen)]
        self.z = [tensor * xlen * j for j in range(1, self.zlen)]
        self.plane = [
            tensor * jx + 2 * jy for jx in range(xlen) for jy in range(ylen) if jx or jy
        ]

    def swap(self, value, flip):
        return lax.ppermute(value, ("dp", "tensor"), [(i, i ^ flip) for i in range(self.count)])

    def swaps(self, values, flips):
        pairs = list(zip(values, flips))[::-1]
        return [self.swap(value.astype(BF), flip) for value, flip in pairs][::-1]

    def spread(self, value, flips):
        return self.swaps([value] * len(flips), flips)


def total_of(values):
    return functools.reduce(jnp.add, [v.astype(F32) for v in values])


def shards(
    queries,
    new_keys,
    new_values,
    key_cache,
    value_cache,
    lengths,
    residual_in,
    query_gain,
    key_gain,
    out_proj,
    norm_gain,
    expert_ids,
    gate_weights,
    expert_gate,
    expert_up,
    expert_down,
):
    tensor = lax.axis_size("tensor")
    dp = lax.axis_size("dp")
    plan = Plan(dp, tensor)
    share, width = residual_in.shape
    lanes = -(-dp * tensor // LANES) * LANES

    sums, weights, table = attention(
        lengths,
        queries,
        new_keys,
        new_values,
        key_cache,
        value_cache,
        query_gain,
        key_gain,
        expert_ids,
        gate_weights,
        out_proj,
        tensor,
        lanes,
    )
    got = []
    for flip, local in zip((1, 0), sums):
        for j in range(0, local.shape[0], 2):
            far = flip * local.shape[0] + j
            pair = local[j : j + 2]
            if far:
                pair = plan.swap(pair, far)
            got += [pair[0], plan.swap(pair[1], plan.core)]
    partial, expert_gate = projection(got, weights, share, expert_gate)
    pair = total_of([partial[0], plan.swap(partial[1], plan.core)])
    projected = total_of([pair[0]] + plan.swaps(list(pair[1:]), plan.y))
    hidden = residual_in.astype(F32) + projected
    normed = rms_scale(hidden, norm_gain).astype(BF)

    mine = jnp.concatenate([normed, table], axis=1)
    others = plan.spread(mine, plan.z)
    near = plan.spread(mine + others[0][:, :1] * 0, plan.plane)
    far = plan.spread(jnp.concatenate(others), plan.plane)
    pieces = [jnp.concatenate([mine] + others + near)] + far
    x = jnp.concatenate(pieces + [plan.swap(piece, plan.core) for piece in pieces])

    result = experts(x, expert_gate, expert_up, expert_down, share)

    sizes = [piece.shape[0] for piece in pieces]
    starts = [sum(sizes[:i]) for i in range(len(sizes) + 1)]
    every = starts[-1]
    sums = [
        total_of(
            [
                result[starts[i] : starts[i + 1]],
                plan.swap(result[every + starts[i] : every + starts[i + 1]], plan.core),
            ]
        )
        for i in reversed(range(len(sizes)))
    ][::-1]
    blocks = sums[0].reshape(-1, share, width)
    far = plan.swaps(sums[1:], plan.plane)
    others = total_of([sums[0][share : plan.zlen * share]] + far).reshape(-1, share, width)
    near = plan.swaps(list(blocks[plan.zlen :]), plan.plane)
    moe_sum = total_of([blocks[0]] + near + plan.swaps(list(others), plan.z))
    return (hidden + moe_sum).astype(BF)


def solution(mesh):
    return jax.shard_map(
        shards,
        mesh=mesh,
        in_specs=(
            P("dp", None, None),
            P("dp", None, None),
            P("dp", None, None),
            P("dp", None, "tensor", None),
            P("dp", None, "tensor", None),
            P("dp"),
            P(("dp", "tensor"), None),
            P(),
            P(),
            P("tensor", None),
            P(),
            P(("dp", "tensor"), None),
            P(("dp", "tensor"), None),
            P(("dp", "tensor"), None, None),
            P(("dp", "tensor"), None, None),
            P(("dp", "tensor"), None, None),
        ),
        out_specs=P(("dp", "tensor"), None),
        check_vma=False,
    )
```

```python
import functools

import jax
import jax.numpy as jnp
from jax import lax
from jax.experimental import pallas as pl
from jax.experimental.pallas import tpu as pltpu
from jax.sharding import PartitionSpec as P

BF = jnp.bfloat16
F32 = jnp.float32
I32 = jnp.int32
MIB = 1 << 20
LANES = 128


def rms_scale(values, gain):
    mean_sq = jnp.mean(values * values, axis=-1, keepdims=True)
    return values * lax.rsqrt(mean_sq + 1e-06) * gain


def matmul(a, b):
    return jnp.dot(a, b, preferred_element_type=F32)


def matmul_t(a, b):
    return lax.dot_general(a, b, (((1,), (1,)), ((), ())), preferred_element_type=F32)


def iota(shape, dim):
    return lax.broadcasted_iota(I32, shape, dim)


def in_hbm(value):
    return pltpu.with_memory_space_constraint(value, pltpu.HBM)


def attention_kernel(flip, *refs):
    sources, refs = refs[:8], refs[8:]
    if flip == 0:
        ids_hbm, gates_hbm, w_hbm, _, out_ref, table_ref, *w_refs = refs[:8]
        refs = refs[8:]
    else:
        out_ref, refs = refs[0], refs[1:]
    len_hbm, q_hbm, nk_hbm, nv_hbm, k_hbm, v_hbm, qg_hbm, kg_hbm = sources
    lengths, q_ref, nk_ref, nv_ref, k_ref, v_ref, qg_ref, kg_ref = refs[:8]
    nk_scr, nv_scr, num, tops, totals, score, weight, sem = refs[8:16]
    tensor_pos = lax.axis_index("tensor")
    rows, group, hd = q_ref.shape
    kvh, cache = k_hbm.shape[1], k_ref.shape[1]
    heads_own = q_hbm.shape[1] // lax.axis_size("tensor")
    parts = group // heads_own
    which = (tensor_pos // parts) ^ flip
    heads = pl.ds(pl.multiple_of(which * group, group), group)
    pairs = [
        (len_hbm, lengths),
        (nk_hbm, nk_ref),
        (nv_hbm, nv_ref),
        (qg_hbm, qg_ref),
        (kg_hbm, kg_ref),
        (q_hbm.at[:, heads], q_ref),
        (k_hbm.at[:, which], k_ref),
        (v_hbm.at[:, which], v_ref),
    ]
    if flip == 0:
        ids_ref, gates_ref = refs[16:]
        pairs = [(ids_hbm, ids_ref), (gates_hbm, gates_ref)] + pairs
        size = w_refs[0].shape[0]
        pairs += [(w_hbm.at[pl.ds(i * size, size)], ref) for i, ref in enumerate(w_refs)]
    copies = [pltpu.make_async_copy(src, dst, sem.at[i]) for i, (src, dst) in enumerate(pairs)]
    for c in copies:
        c.start()
    if flip == 0:
        for c in copies[:2]:
            c.wait()
        ahead = copies[-2:]
        copies = copies[2:-2]
        gates = gates_ref[...]
        route = (gates / jnp.sum(gates, axis=1, keepdims=True)).astype(BF).astype(F32)
        expert = iota(table_ref.shape, 1)
        table = jnp.zeros(table_ref.shape, F32)
        for k in range(gates.shape[1]):
            table = jnp.where(expert == ids_ref[:, k : k + 1], route[:, k : k + 1], table)
        table_ref[...] = table.astype(BF)

    step = 8
    blocks = rows // step
    many, cols = step * group, step * cache
    scaling = hd ** (-0.5)
    same = iota((many, cols), 0) // group == iota((many, cols), 1) // cache
    col_row = iota((1, cols), 1) // cache
    col_pos = iota((1, cols), 1) % cache + tensor_pos * cache
    new_here = iota((many, 2 * step), 1) == iota((many, 2 * step), 0) // group
    new_here = new_here & (tensor_pos == 0)

    for c in copies[:5]:
        c.wait()
    for r in range(rows):
        nk_scr[r * kvh : (r + 1) * kvh, :] = nk_ref[r].astype(F32)
        nv_scr[r * kvh : (r + 1) * kvh, :] = nv_ref[r].astype(F32)
    query_gain = qg_ref[...]
    new_rows = pl.ds(which, rows, stride=kvh)
    key_norm = rms_scale(nk_scr[new_rows, :], kg_ref[...])
    new_value = nv_scr[new_rows, :]
    empty = jnp.zeros((step, hd), F32)
    for c in copies[5:]:
        c.wait()

    def rows_of(ref, b, size):
        return ref[b * step : (b + 1) * step].reshape(size, hd)

    def with_empty(value, b):
        return jnp.concatenate([value[b * step : (b + 1) * step], empty]).astype(BF)

    queries = []
    for b in range(blocks):
        query = rows_of(q_ref, b, many).astype(F32)
        queries.append(rms_scale(query, query_gain).astype(BF))
    for b in range(blocks):
        limit = jnp.zeros((1, cols), I32)
        for i in range(step):
            limit = jnp.where(col_row == i, lengths[b * step + i], limit)
        included = same & (col_pos < limit)
        scores = matmul_t(queries[b], rows_of(k_ref, b, cols)) * scaling
        score[b, :, :cols] = jnp.where(included, scores, -1e30)
        scores = matmul_t(queries[b], with_empty(key_norm, b)) * scaling
        score[b, :, cols:] = jnp.where(new_here, scores, -1e30)
    for b in range(blocks):
        top = jnp.maximum(jnp.max(score[b], axis=1, keepdims=True), -1e29).astype(BF).astype(F32)
        tops[b * many : (b + 1) * many, :] = jnp.broadcast_to(top, (many, LANES))
    for b in range(blocks):
        top = tops[b * many : (b + 1) * many, 0:1]
        weights = jnp.exp(score[b] - top).astype(BF)
        weight[b] = weights
        total = jnp.sum(weights.astype(F32), axis=1, keepdims=True)
        totals[b * many : (b + 1) * many, :] = jnp.broadcast_to(total, (many, LANES))
    for b in range(blocks):
        num[b * many : (b + 1) * many, :] = matmul(
            weight[b, :, :cols], rows_of(v_ref, b, cols)
        ) + matmul(weight[b, :, cols:], with_empty(new_value, b))

    lane = iota((rows, LANES), 1)
    for t in range(parts):
        slot = (tensor_pos % parts) ^ t
        side = jnp.zeros((rows, LANES), F32)
        for h in range(heads_own):
            own = pl.ds(t * heads_own + h, rows, stride=group)
            out_ref[slot, :, h * hd : (h + 1) * hd] = num[own, :].astype(BF)
            total = totals[own, :]
            high = total.astype(BF).astype(F32)
            side = jnp.where(lane == h, tops[own, :], side)
            side = jnp.where(lane == heads_own + h, high, side)
            side = jnp.where(lane == 2 * heads_own + h, total - high, side)
        out_ref[slot, :, heads_own * hd :] = side.astype(BF)
    if flip == 0:
        for c in ahead:
            c.wait()


def attention(
    flip, lengths, queries, new_keys, new_values, key_cache, value_cache, qg, kg, parts, more
):
    rows, heads, hd = queries.shape
    kvh, cache = key_cache.shape[1:3]
    group = heads // kvh
    blocks = rows // 8
    args = [lengths, queries, new_keys, new_values, key_cache, value_cache]
    args = [in_hbm(a) for a in (*args, qg.reshape(1, -1), kg.reshape(1, -1))]
    outs = [jax.ShapeDtypeStruct((parts // kvh, rows, heads // parts * hd + LANES), BF)]
    scratch = [
        pltpu.SMEM((rows,), I32),
        pltpu.VMEM((rows, group, hd), BF),
        pltpu.VMEM(new_keys.shape, BF),
        pltpu.VMEM(new_values.shape, BF),
        pltpu.VMEM((rows, cache, hd), BF),
        pltpu.VMEM((rows, cache, hd), BF),
        pltpu.VMEM((1, hd), F32),
        pltpu.VMEM((1, hd), F32),
        pltpu.VMEM((rows * kvh, hd), F32),
        pltpu.VMEM((rows * kvh, hd), F32),
        pltpu.VMEM((rows * group, hd), F32),
        pltpu.VMEM((rows * group, LANES), F32),
        pltpu.VMEM((rows * group, LANES), F32),
        pltpu.VMEM((blocks, 8 * group, 8 * (cache + 2)), F32),
        pltpu.VMEM((blocks, 8 * group, 8 * (cache + 2)), BF),
        pltpu.SemaphoreType.DMA((12,)),
    ]
    specs = [pl.BlockSpec(memory_space=pltpu.HBM)] * len(args)
    size = 2 * rows * group * hd * 8
    if flip == 0:
        expert_ids, gate_weights, lanes, later, earlier = more
        args += [in_hbm(a) for a in (expert_ids, gate_weights, later)] + [earlier]
        specs += [pl.BlockSpec(memory_space=pltpu.HBM)] * 3 + [pl.BlockSpec(memory_space=pl.ANY)]
        outs.append(jax.ShapeDtypeStruct((expert_ids.shape[0], lanes), BF))
        outs += [pltpu.VMEM((later.shape[0] // 2, later.shape[1]), later.dtype)] * 2
        scratch += [pltpu.VMEM(expert_ids.shape, I32), pltpu.VMEM(gate_weights.shape, F32)]
        size = size + 2 * later.size
    return pl.pallas_call(
        functools.partial(attention_kernel, flip),
        out_shape=tuple(outs),
        in_specs=specs,
        out_specs=(pl.BlockSpec(memory_space=pltpu.VMEM),) * len(outs),
        scratch_shapes=scratch,
        compiler_params=pltpu.CompilerParams(vmem_limit_bytes=16 * MIB),
        cost_estimate=pl.CostEstimate(flops=size, bytes_accessed=size, transcendentals=0),
        name="attention",
    )(*args)


def projection_kernel(parts, cuts, *refs):
    got = refs[:parts]
    w_refs, refs = refs[parts : parts + cuts], refs[parts + cuts :]
    ahead_hbm, out_ref, ahead_ref, attn, sem = refs
    ahead = pltpu.make_async_copy(ahead_hbm, ahead_ref, sem)
    ahead.start()
    tensor_pos = lax.axis_index("tensor")
    width = w_refs[0].shape[1]
    depth = attn.shape[1]
    share = out_ref.shape[2]
    hd = LANES
    heads_own = depth // hd
    size = 512
    sides = [g[:, depth:].astype(F32) for g in got]
    tops = [s[:, :heads_own] for s in sides]
    top = functools.reduce(jnp.maximum, tops)
    factors = [jnp.exp(t - top) for t in tops]
    totals = [
        f * (s[:, heads_own : 2 * heads_own] + s[:, 2 * heads_own : 3 * heads_own])
        for f, s in zip(factors, sides)
    ]
    total = functools.reduce(jnp.add, totals)
    factors = [f / total for f in factors]
    for h in range(heads_own):
        cols = slice(h * hd, (h + 1) * hd)
        terms = [g[:, cols].astype(F32) * f[:, h : h + 1] for g, f in zip(got, factors)]
        attn[:, cols] = functools.reduce(jnp.add, terms).astype(BF)
    part = depth // cuts
    for start in range(0, width, size):
        cols = slice(start, start + size)
        result = functools.reduce(
            jnp.add,
            [
                matmul(attn[:, k * part : (k + 1) * part], w_ref[:, cols])
                for k, w_ref in enumerate(w_refs)
            ],
        )
        for t in range(parts):
            slot = tensor_pos ^ t
            block = result[t * share : (t + 1) * share].astype(BF)
            out_ref[slot & 1, slot >> 1, :, cols] = block
    ahead.wait()


def projection(got, weights, share, later):
    parts = len(got)
    rows = got[0].shape[0]
    depth = sum(w.shape[0] for w in weights)
    width = weights[0].shape[1]
    vmem = pl.BlockSpec(memory_space=pltpu.VMEM)
    return pl.pallas_call(
        functools.partial(projection_kernel, parts, len(weights)),
        out_shape=(
            jax.ShapeDtypeStruct((2, parts // 2, share, width), BF),
            pltpu.VMEM(later.shape, later.dtype),
        ),
        in_specs=[vmem] * (parts + len(weights)) + [pl.BlockSpec(memory_space=pltpu.HBM)],
        out_specs=(vmem, vmem),
        scratch_shapes=[pltpu.VMEM((rows, depth), BF), pltpu.SemaphoreType.DMA],
        compiler_params=pltpu.CompilerParams(vmem_limit_bytes=12 * MIB),
        name="projection",
    )(*got, *weights, in_hbm(later))


def expert_kernel(x_ref, gate, up, down_hbm, out_ref, down, act, sem):
    own = lax.axis_index("dp") * lax.axis_size("tensor") + lax.axis_index("tensor")
    _, width, hidden = gate.shape
    fsize = 384
    dsize = 1024
    chunks = width // dsize

    def down_copy(i):
        cols = pl.ds(i * dsize, dsize)
        return pltpu.make_async_copy(down_hbm.at[0, :, cols], down.at[:, cols], sem.at[i])

    for i in range(chunks):
        down_copy(i).start()
    for i in range(hidden // fsize):
        cols = slice(i * fsize, (i + 1) * fsize)
        g = matmul(x_ref[:, :width], gate[0, :, cols])
        u = matmul(x_ref[:, :width], up[0, :, cols])
        act[:, cols] = (g / (1.0 + jnp.exp(-g)) * u).astype(BF)
    table = x_ref[:, width:].astype(F32)
    named = iota(table.shape, 1) == own
    weight = jnp.sum(jnp.where(named, table, 0.0), axis=1, keepdims=True)
    for i in range(chunks):
        down_copy(i).wait()
        cols = slice(i * dsize, (i + 1) * dsize)
        out_ref[:, cols] = (matmul(act[...], down[:, cols]) * weight).astype(BF)


def experts(x, expert_gate, expert_up, expert_down):
    rows = x.shape[0]
    _, width, hidden = expert_gate.shape
    vmem = pl.BlockSpec(memory_space=pltpu.VMEM)
    return pl.pallas_call(
        expert_kernel,
        out_shape=jax.ShapeDtypeStruct((rows, width), BF),
        in_specs=[vmem] * 3 + [pl.BlockSpec(memory_space=pltpu.HBM)],
        out_specs=vmem,
        scratch_shapes=[
            pltpu.VMEM((hidden, width), BF),
            pltpu.VMEM((rows, hidden), BF),
            pltpu.SemaphoreType.DMA((width // 1024,)),
        ],
        compiler_params=pltpu.CompilerParams(vmem_limit_bytes=(16 + rows // 32) * MIB),
        name="experts",
    )(x, expert_gate, expert_up, in_hbm(expert_down))


class Plan:
    def __init__(self, dp, tensor):
        self.zlen = min(4, dp)
        xlen, ylen = dp // self.zlen, tensor // 2
        self.count = dp * tensor
        self.core = 1
        self.y = [2 * j for j in range(1, ylen)]
        self.z = [tensor * xlen * j for j in range(1, self.zlen)]
        self.plane = [
            tensor * jx + 2 * jy for jx in range(xlen) for jy in range(ylen) if jx or jy
        ]

    def swap(self, value, flip):
        return lax.ppermute(value, ("dp", "tensor"), [(i, i ^ flip) for i in range(self.count)])

    def swaps(self, values, flips):
        pairs = list(zip(values, flips))[::-1]
        return [self.swap(value.astype(BF), flip) for value, flip in pairs][::-1]

    def spread(self, value, flips):
        return self.swaps([value] * len(flips), flips)


def total_of(values):
    return functools.reduce(jnp.add, [v.astype(F32) for v in values])


def shards(
    queries,
    new_keys,
    new_values,
    key_cache,
    value_cache,
    lengths,
    residual_in,
    query_gain,
    key_gain,
    out_proj,
    norm_gain,
    expert_ids,
    gate_weights,
    expert_gate,
    expert_up,
    expert_down,
):
    tensor = lax.axis_size("tensor")
    dp = lax.axis_size("dp")
    plan = Plan(dp, tensor)
    share, width = residual_in.shape
    lanes = -(-dp * tensor // LANES) * LANES

    inputs = (lengths, queries, new_keys, new_values, key_cache, value_cache, query_gain, key_gain)
    groups = key_cache.shape[1]
    got, local = [], None
    for flip in reversed(range(groups)):
        more = (expert_ids, gate_weights, lanes, out_proj, local)
        results = attention(flip, *inputs, tensor, more)
        local = results[0]
        for j in range(0, tensor // groups, 2):
            far = flip * (tensor // groups) + j
            pair = local[j : j + 2]
            if far:
                pair = plan.swap(pair, far)
            got += [pair[0], plan.swap(pair[1], plan.core)]
    _, table, *weights = results
    partial, expert_gate = projection(got, weights, share, expert_gate)
    pair = total_of([partial[0], plan.swap(partial[1], plan.core)])
    projected = total_of([pair[0]] + plan.swaps(list(pair[1:]), plan.y))
    hidden = residual_in.astype(F32) + projected
    normed = rms_scale(hidden, norm_gain).astype(BF)

    mine = jnp.concatenate([normed, table], axis=1)
    others = plan.spread(mine, plan.z)
    near = plan.spread(mine + others[0][:, :1] * 0, plan.plane)
    far = plan.spread(jnp.concatenate(others), plan.plane)
    pieces = [jnp.concatenate([mine] + others + near)] + far
    x = jnp.concatenate(pieces + [plan.swap(piece, plan.core) for piece in pieces])

    result = experts(x, expert_gate, expert_up, expert_down)

    sizes = [piece.shape[0] for piece in pieces]
    starts = [sum(sizes[:i]) for i in range(len(sizes) + 1)]
    every = starts[-1]
    sums = [
        total_of(
            [
                result[starts[i] : starts[i + 1]],
                plan.swap(result[every + starts[i] : every + starts[i + 1]], plan.core),
            ]
        )
        for i in reversed(range(len(sizes)))
    ][::-1]
    blocks = sums[0].reshape(-1, share, width)
    far = plan.swaps(sums[1:], plan.plane)
    others = total_of([sums[0][share : plan.zlen * share]] + far).reshape(-1, share, width)
    near = plan.swaps(list(blocks[plan.zlen :]), plan.plane)
    moe_sum = total_of([blocks[0]] + near + plan.swaps(list(others), plan.z))
    return (hidden + moe_sum).astype(BF)


def solution(mesh):
    return jax.shard_map(
        shards,
        mesh=mesh,
        in_specs=(
            P("dp", None, None),
            P("dp", None, None),
            P("dp", None, None),
            P("dp", None, "tensor", None),
            P("dp", None, "tensor", None),
            P("dp"),
            P(("dp", "tensor"), None),
            P(),
            P(),
            P("tensor", None),
            P(),
            P(("dp", "tensor"), None),
            P(("dp", "tensor"), None),
            P(("dp", "tensor"), None, None),
            P(("dp", "tensor"), None, None),
            P(("dp", "tensor"), None, None),
        ),
        out_specs=P(("dp", "tensor"), None),
        check_vma=False,
    )
```

```python
import functools

import jax
import jax.numpy as jnp
from jax import lax
from jax.experimental import pallas as pl
from jax.experimental.pallas import tpu as pltpu
from jax.sharding import PartitionSpec as P

BF = jnp.bfloat16
F32 = jnp.float32
I32 = jnp.int32
MIB = 1 << 20
LANES = 128
CAP = 3


def rms_scale(values, gain):
    mean_sq = jnp.mean(values * values, axis=-1, keepdims=True)
    return values * lax.rsqrt(mean_sq + 1e-06) * gain


def matmul(a, b):
    return jnp.dot(a, b, preferred_element_type=F32)


def matmul_t(a, b):
    return lax.dot_general(a, b, (((1,), (1,)), ((), ())), preferred_element_type=F32)


def iota(shape, dim):
    return lax.broadcasted_iota(I32, shape, dim)


def in_hbm(value):
    return pltpu.with_memory_space_constraint(value, pltpu.HBM)


def attention_kernel(flip, *refs):
    sources, refs = refs[:8], refs[8:]
    if flip == 0:
        ids_hbm, gates_hbm, w_hbm, _, out_ref, table_ref, *w_refs = refs[:8]
        refs = refs[8:]
    else:
        out_ref, refs = refs[0], refs[1:]
    len_hbm, q_hbm, nk_hbm, nv_hbm, k_hbm, v_hbm, qg_hbm, kg_hbm = sources
    lengths, q_ref, nk_ref, nv_ref, k_ref, v_ref, qg_ref, kg_ref = refs[:8]
    nk_scr, nv_scr, num, tops, totals, score, weight, sem = refs[8:16]
    tensor_pos = lax.axis_index("tensor")
    rows, group, hd = q_ref.shape
    kvh, cache = k_hbm.shape[1], k_ref.shape[1]
    heads_own = q_hbm.shape[1] // lax.axis_size("tensor")
    parts = group // heads_own
    which = (tensor_pos // parts) ^ flip
    heads = pl.ds(pl.multiple_of(which * group, group), group)
    pairs = [
        (len_hbm, lengths),
        (nk_hbm, nk_ref),
        (nv_hbm, nv_ref),
        (qg_hbm, qg_ref),
        (kg_hbm, kg_ref),
        (q_hbm.at[:, heads], q_ref),
        (k_hbm.at[:, which], k_ref),
        (v_hbm.at[:, which], v_ref),
    ]
    if flip == 0:
        ids_ref, gates_ref = refs[16:]
        pairs = [(ids_hbm, ids_ref), (gates_hbm, gates_ref)] + pairs
        size = w_refs[0].shape[0]
        pairs += [(w_hbm.at[pl.ds(i * size, size)], ref) for i, ref in enumerate(w_refs)]
    copies = [pltpu.make_async_copy(src, dst, sem.at[i]) for i, (src, dst) in enumerate(pairs)]
    for c in copies:
        c.start()
    if flip == 0:
        for c in copies[:2]:
            c.wait()
        ahead = copies[-2:]
        copies = copies[2:-2]
        gates = gates_ref[...]
        route = (gates / jnp.sum(gates, axis=1, keepdims=True)).astype(BF).astype(F32)
        expert = iota(table_ref.shape, 1)
        table = jnp.zeros(table_ref.shape, F32)
        for k in range(gates.shape[1]):
            table = jnp.where(expert == ids_ref[:, k : k + 1], route[:, k : k + 1], table)
        table_ref[...] = table.astype(BF)

    step = 8
    blocks = rows // step
    many, cols = step * group, step * cache
    scaling = hd ** (-0.5)
    same = iota((many, cols), 0) // group == iota((many, cols), 1) // cache
    col_row = iota((1, cols), 1) // cache
    col_pos = iota((1, cols), 1) % cache + tensor_pos * cache
    new_here = iota((many, 2 * step), 1) == iota((many, 2 * step), 0) // group
    new_here = new_here & (tensor_pos == 0)

    for c in copies[:5]:
        c.wait()
    for r in range(rows):
        nk_scr[r * kvh : (r + 1) * kvh, :] = nk_ref[r].astype(F32)
        nv_scr[r * kvh : (r + 1) * kvh, :] = nv_ref[r].astype(F32)
    query_gain = qg_ref[...]
    new_rows = pl.ds(which, rows, stride=kvh)
    key_norm = rms_scale(nk_scr[new_rows, :], kg_ref[...])
    new_value = nv_scr[new_rows, :]
    empty = jnp.zeros((step, hd), F32)
    for c in copies[5:]:
        c.wait()

    def rows_of(ref, b, size):
        return ref[b * step : (b + 1) * step].reshape(size, hd)

    def with_empty(value, b):
        return jnp.concatenate([value[b * step : (b + 1) * step], empty]).astype(BF)

    queries = []
    for b in range(blocks):
        query = rows_of(q_ref, b, many).astype(F32)
        queries.append(rms_scale(query, query_gain).astype(BF))
    for b in range(blocks):
        limit = jnp.zeros((1, cols), I32)
        for i in range(step):
            limit = jnp.where(col_row == i, lengths[b * step + i], limit)
        included = same & (col_pos < limit)
        scores = matmul_t(queries[b], rows_of(k_ref, b, cols)) * scaling
        score[b, :, :cols] = jnp.where(included, scores, -1e30)
        scores = matmul_t(queries[b], with_empty(key_norm, b)) * scaling
        score[b, :, cols:] = jnp.where(new_here, scores, -1e30)
    for b in range(blocks):
        top = jnp.maximum(jnp.max(score[b], axis=1, keepdims=True), -1e29).astype(BF).astype(F32)
        tops[b * many : (b + 1) * many, :] = jnp.broadcast_to(top, (many, LANES))
    for b in range(blocks):
        top = tops[b * many : (b + 1) * many, 0:1]
        weights = jnp.exp(score[b] - top).astype(BF)
        weight[b] = weights
        total = jnp.sum(weights.astype(F32), axis=1, keepdims=True)
        totals[b * many : (b + 1) * many, :] = jnp.broadcast_to(total, (many, LANES))
    for b in range(blocks):
        num[b * many : (b + 1) * many, :] = matmul(
            weight[b, :, :cols], rows_of(v_ref, b, cols)
        ) + matmul(weight[b, :, cols:], with_empty(new_value, b))

    lane = iota((rows, LANES), 1)
    for t in range(parts):
        slot = (tensor_pos % parts) ^ t
        side = jnp.zeros((rows, LANES), F32)
        for h in range(heads_own):
            own = pl.ds(t * heads_own + h, rows, stride=group)
            out_ref[slot, :, h * hd : (h + 1) * hd] = num[own, :].astype(BF)
            total = totals[own, :]
            high = total.astype(BF).astype(F32)
            side = jnp.where(lane == h, tops[own, :], side)
            side = jnp.where(lane == heads_own + h, high, side)
            side = jnp.where(lane == 2 * heads_own + h, total - high, side)
        out_ref[slot, :, heads_own * hd :] = side.astype(BF)
    if flip == 0:
        for c in ahead:
            c.wait()


def attention(
    flip, lengths, queries, new_keys, new_values, key_cache, value_cache, qg, kg, parts, more
):
    rows, heads, hd = queries.shape
    kvh, cache = key_cache.shape[1:3]
    group = heads // kvh
    blocks = rows // 8
    args = [lengths, queries, new_keys, new_values, key_cache, value_cache]
    args = [in_hbm(a) for a in (*args, qg.reshape(1, -1), kg.reshape(1, -1))]
    outs = [jax.ShapeDtypeStruct((parts // kvh, rows, heads // parts * hd + LANES), BF)]
    scratch = [
        pltpu.SMEM((rows,), I32),
        pltpu.VMEM((rows, group, hd), BF),
        pltpu.VMEM(new_keys.shape, BF),
        pltpu.VMEM(new_values.shape, BF),
        pltpu.VMEM((rows, cache, hd), BF),
        pltpu.VMEM((rows, cache, hd), BF),
        pltpu.VMEM((1, hd), F32),
        pltpu.VMEM((1, hd), F32),
        pltpu.VMEM((rows * kvh, hd), F32),
        pltpu.VMEM((rows * kvh, hd), F32),
        pltpu.VMEM((rows * group, hd), F32),
        pltpu.VMEM((rows * group, LANES), F32),
        pltpu.VMEM((rows * group, LANES), F32),
        pltpu.VMEM((blocks, 8 * group, 8 * (cache + 2)), F32),
        pltpu.VMEM((blocks, 8 * group, 8 * (cache + 2)), BF),
        pltpu.SemaphoreType.DMA((12,)),
    ]
    specs = [pl.BlockSpec(memory_space=pltpu.HBM)] * len(args)
    size = 2 * rows * group * hd * 8
    if flip == 0:
        expert_ids, gate_weights, lanes, later, earlier = more
        args += [in_hbm(a) for a in (expert_ids, gate_weights, later)] + [earlier]
        specs += [pl.BlockSpec(memory_space=pltpu.HBM)] * 3 + [pl.BlockSpec(memory_space=pl.ANY)]
        outs.append(jax.ShapeDtypeStruct((expert_ids.shape[0], lanes), BF))
        outs += [pltpu.VMEM((later.shape[0] // 2, later.shape[1]), later.dtype)] * 2
        scratch += [pltpu.VMEM(expert_ids.shape, I32), pltpu.VMEM(gate_weights.shape, F32)]
        size = size + 2 * later.size
    return pl.pallas_call(
        functools.partial(attention_kernel, flip),
        out_shape=tuple(outs),
        in_specs=specs,
        out_specs=(pl.BlockSpec(memory_space=pltpu.VMEM),) * len(outs),
        scratch_shapes=scratch,
        compiler_params=pltpu.CompilerParams(vmem_limit_bytes=16 * MIB),
        cost_estimate=pl.CostEstimate(flops=size, bytes_accessed=size, transcendentals=0),
        name="attention",
    )(*args)


def projection_kernel(parts, cuts, *refs):
    got = refs[:parts]
    w_refs, refs = refs[parts : parts + cuts], refs[parts + cuts :]
    ahead_hbm, out_ref, ahead_ref, attn, sem = refs
    ahead = pltpu.make_async_copy(ahead_hbm, ahead_ref, sem)
    ahead.start()
    tensor_pos = lax.axis_index("tensor")
    width = w_refs[0].shape[1]
    depth = attn.shape[1]
    share = out_ref.shape[2]
    hd = LANES
    heads_own = depth // hd
    size = 512
    sides = [g[:, depth:].astype(F32) for g in got]
    tops = [s[:, :heads_own] for s in sides]
    top = functools.reduce(jnp.maximum, tops)
    factors = [jnp.exp(t - top) for t in tops]
    totals = [
        f * (s[:, heads_own : 2 * heads_own] + s[:, 2 * heads_own : 3 * heads_own])
        for f, s in zip(factors, sides)
    ]
    total = functools.reduce(jnp.add, totals)
    factors = [f / total for f in factors]
    for h in range(heads_own):
        cols = slice(h * hd, (h + 1) * hd)
        terms = [g[:, cols].astype(F32) * f[:, h : h + 1] for g, f in zip(got, factors)]
        attn[:, cols] = functools.reduce(jnp.add, terms).astype(BF)
    part = depth // cuts
    for start in range(0, width, size):
        cols = slice(start, start + size)
        result = functools.reduce(
            jnp.add,
            [
                matmul(attn[:, k * part : (k + 1) * part], w_ref[:, cols])
                for k, w_ref in enumerate(w_refs)
            ],
        )
        for t in range(parts):
            slot = tensor_pos ^ t
            block = result[t * share : (t + 1) * share].astype(BF)
            out_ref[slot & 1, slot >> 1, :, cols] = block
    ahead.wait()


def projection(got, weights, share, later):
    parts = len(got)
    rows = got[0].shape[0]
    depth = sum(w.shape[0] for w in weights)
    width = weights[0].shape[1]
    vmem = pl.BlockSpec(memory_space=pltpu.VMEM)
    return pl.pallas_call(
        functools.partial(projection_kernel, parts, len(weights)),
        out_shape=(
            jax.ShapeDtypeStruct((2, parts // 2, share, width), BF),
            pltpu.VMEM(later.shape, later.dtype),
        ),
        in_specs=[vmem] * (parts + len(weights)) + [pl.BlockSpec(memory_space=pltpu.HBM)],
        out_specs=(vmem, vmem),
        scratch_shapes=[pltpu.VMEM((rows, depth), BF), pltpu.SemaphoreType.DMA],
        compiler_params=pltpu.CompilerParams(vmem_limit_bytes=12 * MIB),
        name="projection",
    )(*got, *weights, in_hbm(later))


def expert_kernel(slots, x_ref, gate, up, down_hbm, out_ref, down, xc, act, res, sem):
    own = lax.axis_index("dp") * lax.axis_size("tensor") + lax.axis_index("tensor")
    rows = x_ref.shape[0]
    _, width, hidden = gate.shape
    padded = res.shape[0]
    fsize = 384
    dsize = 1024
    chunks = width // dsize

    def down_copy(i):
        cols = pl.ds(i * dsize, dsize)
        return pltpu.make_async_copy(down_hbm.at[0, :, cols], down.at[:, cols], sem.at[i])

    for i in range(chunks):
        down_copy(i).start()
    table = x_ref[:, width:]
    pick = (iota((16, table.shape[1]), 1) == own).astype(F32).astype(BF)
    named = matmul_t(pick, table) != 0.0
    before = (iota((rows, rows), 0) < iota((rows, rows), 1)).astype(F32).astype(BF)
    place = matmul(named.astype(F32).astype(BF), before)
    place = jnp.where(named, place, -1.0)[:1]
    take = (iota((slots, rows), 0).astype(F32) == place).astype(F32).astype(BF)
    for i in range(chunks):
        cols = slice(i * dsize, (i + 1) * dsize)
        xc[:, cols] = matmul(take, x_ref[:, cols]).astype(BF)

    lane = iota(table.shape, 1)
    weight = jnp.sum(jnp.where(lane == own, table.astype(F32), 0.0), axis=1, keepdims=True)
    named = jnp.broadcast_to((weight != 0.0).astype(F32), (rows, LANES)).astype(BF)
    after = (iota((rows, rows), 1) < iota((rows, rows), 0)).astype(F32).astype(BF)
    place = matmul(after, named)[:, :1]
    spread = jnp.where(iota((rows, padded), 1).astype(F32) == place, weight, 0.0).astype(BF)
    if padded > slots:
        res[slots:, :] = jnp.zeros((padded - slots, dsize), BF)

    for i in range(hidden // fsize):
        cols = slice(i * fsize, (i + 1) * fsize)
        g = matmul(xc[...], gate[0, :, cols])
        u = matmul(xc[...], up[0, :, cols])
        act[:, cols] = (g / (1.0 + jnp.exp(-g)) * u).astype(BF)
    for i in range(chunks):
        down_copy(i).wait()
        cols = slice(i * dsize, (i + 1) * dsize)
        res[:slots, :] = matmul(act[...], down[:, cols]).astype(BF)
        out_ref[:, cols] = matmul(spread, res[...]).astype(BF)


def experts(x, expert_gate, expert_up, expert_down, share):
    rows = x.shape[0]
    _, width, hidden = expert_gate.shape
    slots = rows // share * CAP
    vmem = pl.BlockSpec(memory_space=pltpu.VMEM)
    return pl.pallas_call(
        functools.partial(expert_kernel, slots),
        out_shape=jax.ShapeDtypeStruct((rows, width), BF),
        in_specs=[vmem] * 3 + [pl.BlockSpec(memory_space=pltpu.HBM)],
        out_specs=vmem,
        scratch_shapes=[
            pltpu.VMEM((hidden, width), BF),
            pltpu.VMEM((slots, width), BF),
            pltpu.VMEM((slots, hidden), BF),
            pltpu.VMEM((-(-slots // LANES) * LANES, 1024), BF),
            pltpu.SemaphoreType.DMA((width // 1024,)),
        ],
        compiler_params=pltpu.CompilerParams(vmem_limit_bytes=(16 + rows // 32) * MIB),
        name="experts",
    )(x, expert_gate, expert_up, in_hbm(expert_down))


class Plan:
    def __init__(self, dp, tensor):
        self.zlen = min(4, dp)
        xlen, ylen = dp // self.zlen, tensor // 2
        self.count = dp * tensor
        self.core = 1
        self.y = [2 * j for j in range(1, ylen)]
        self.z = [tensor * xlen * j for j in range(1, self.zlen)]
        self.x = [tensor * j for j in range(1, xlen)]
        self.diagonal = [jx + jy for jx in self.x for jy in self.y]

    def swap(self, value, flip):
        return lax.ppermute(value, ("dp", "tensor"), [(i, i ^ flip) for i in range(self.count)])

    def swaps(self, values, flips):
        pairs = list(zip(values, flips))[::-1]
        return [self.swap(value.astype(BF), flip) for value, flip in pairs][::-1]

    def spread(self, value, flips):
        return self.swaps([value] * len(flips), flips)


def total_of(values):
    return functools.reduce(jnp.add, [v.astype(F32) for v in values])


def shards(
    queries,
    new_keys,
    new_values,
    key_cache,
    value_cache,
    lengths,
    residual_in,
    query_gain,
    key_gain,
    out_proj,
    norm_gain,
    expert_ids,
    gate_weights,
    expert_gate,
    expert_up,
    expert_down,
):
    tensor = lax.axis_size("tensor")
    dp = lax.axis_size("dp")
    plan = Plan(dp, tensor)
    share, width = residual_in.shape
    lanes = -(-dp * tensor // LANES) * LANES

    inputs = (lengths, queries, new_keys, new_values, key_cache, value_cache, query_gain, key_gain)
    groups = key_cache.shape[1]
    got, local = [], None
    for flip in reversed(range(groups)):
        more = (expert_ids, gate_weights, lanes, out_proj, local)
        results = attention(flip, *inputs, tensor, more)
        local = results[0]
        for j in range(0, tensor // groups, 2):
            far = flip * (tensor // groups) + j
            pair = local[j : j + 2]
            if far:
                pair = plan.swap(pair, far)
            got += [pair[0], plan.swap(pair[1], plan.core)]
    _, table, *weights = results
    partial, expert_gate = projection(got, weights, share, expert_gate)
    pair = total_of([partial[0], plan.swap(partial[1], plan.core)])
    projected = total_of([pair[0]] + plan.swaps(list(pair[1:]), plan.y))
    hidden = residual_in.astype(F32) + projected
    normed = rms_scale(hidden, norm_gain).astype(BF)

    mine = jnp.concatenate([normed, table], axis=1)
    others = plan.spread(mine, plan.z)
    first = mine + others[0][:, :1] * 0
    near_x = plan.spread(first, plan.x)
    near_y = plan.spread(first, plan.y)
    rest = jnp.concatenate(others)
    far_diagonal = plan.spread(rest, plan.diagonal)
    far_y = plan.spread(rest, plan.y)
    far_x = plan.spread(jnp.concatenate(others + near_y), plan.x)
    pieces = [jnp.concatenate([mine] + others + near_x + near_y)] + far_y + far_x + far_diagonal
    x = jnp.concatenate(pieces + [plan.swap(piece, plan.core) for piece in pieces])

    result = experts(x, expert_gate, expert_up, expert_down, share)

    sizes = [piece.shape[0] for piece in pieces]
    starts = [sum(sizes[:i]) for i in range(len(sizes) + 1)]
    every = starts[-1]
    sums = [
        total_of(
            [
                result[starts[i] : starts[i + 1]],
                plan.swap(result[every + starts[i] : every + starts[i + 1]], plan.core),
            ]
        )
        for i in reversed(range(len(sizes)))
    ][::-1]
    back = plan.swaps(sums[1:], plan.y + plan.x + plan.diagonal)
    height, x_end = rest.shape[0], len(plan.y) + len(plan.x)
    column = sums[0][: share + height]
    near = sums[0][share + height :].reshape(-1, share, width)
    through = [v[height:] for v in back[len(plan.y) : x_end]]
    through = total_of([near[len(plan.x) :].reshape(-1, width)] + through)
    others = total_of([column[share:]] + [v[:height] for v in back])
    others = plan.swaps(list(others.reshape(-1, share, width)), plan.z)
    near_x = plan.swaps(list(near[: len(plan.x)]), plan.x)
    near_y = plan.swaps(list(through.reshape(-1, share, width)), plan.y)
    moe_sum = total_of([column[:share]] + near_x + near_y + others)
    return (hidden + moe_sum).astype(BF)


def solution(mesh):
    return jax.shard_map(
        shards,
        mesh=mesh,
        in_specs=(
            P("dp", None, None),
            P("dp", None, None),
            P("dp", None, None),
            P("dp", None, "tensor", None),
            P("dp", None, "tensor", None),
            P("dp"),
            P(("dp", "tensor"), None),
            P(),
            P(),
            P("tensor", None),
            P(),
            P(("dp", "tensor"), None),
            P(("dp", "tensor"), None),
            P(("dp", "tensor"), None, None),
            P(("dp", "tensor"), None, None),
            P(("dp", "tensor"), None, None),
        ),
        out_specs=P(("dp", "tensor"), None),
        check_vma=False,
    )
```

```python
import functools

import jax
import jax.numpy as jnp
from jax import lax
from jax.experimental import pallas as pl
from jax.experimental.pallas import tpu as pltpu
from jax.sharding import PartitionSpec as P

BF = jnp.bfloat16
F32 = jnp.float32
I32 = jnp.int32
MIB = 1 << 20
LANES = 128
CAP = 3


def rms_scale(values, gain):
    mean_sq = jnp.mean(values * values, axis=-1, keepdims=True)
    return values * lax.rsqrt(mean_sq + 1e-06) * gain


def matmul(a, b):
    return jnp.dot(a, b, preferred_element_type=F32)


def matmul_t(a, b):
    return lax.dot_general(a, b, (((1,), (1,)), ((), ())), preferred_element_type=F32)


def iota(shape, dim):
    return lax.broadcasted_iota(I32, shape, dim)


def in_hbm(value):
    return pltpu.with_memory_space_constraint(value, pltpu.HBM)


def attention_kernel(flip, *refs):
    sources, refs = refs[:8], refs[8:]
    if flip == 0:
        ids_hbm, gates_hbm, w_hbm, _, out_ref, table_ref, *w_refs = refs[:8]
        refs = refs[8:]
    else:
        out_ref, refs = refs[0], refs[1:]
    len_hbm, q_hbm, nk_hbm, nv_hbm, k_hbm, v_hbm, qg_hbm, kg_hbm = sources
    lengths, q_ref, nk_ref, nv_ref, k_ref, v_ref, qg_ref, kg_ref = refs[:8]
    nk_scr, nv_scr, num, tops, totals, score, weight, sem = refs[8:16]
    tensor_pos = lax.axis_index("tensor")
    rows, group, hd = q_ref.shape
    kvh, cache = k_hbm.shape[1], k_ref.shape[1]
    heads_own = q_hbm.shape[1] // lax.axis_size("tensor")
    parts = group // heads_own
    which = (tensor_pos // parts) ^ flip
    heads = pl.ds(pl.multiple_of(which * group, group), group)
    pairs = [
        (len_hbm, lengths),
        (nk_hbm, nk_ref),
        (nv_hbm, nv_ref),
        (qg_hbm, qg_ref),
        (kg_hbm, kg_ref),
        (q_hbm.at[:, heads], q_ref),
        (k_hbm.at[:, which], k_ref),
        (v_hbm.at[:, which], v_ref),
    ]
    if flip == 0:
        ids_ref, gates_ref = refs[16:]
        pairs = [(ids_hbm, ids_ref), (gates_hbm, gates_ref)] + pairs
        size = w_refs[0].shape[0]
        pairs += [(w_hbm.at[pl.ds(i * size, size)], ref) for i, ref in enumerate(w_refs)]
    copies = [pltpu.make_async_copy(src, dst, sem.at[i]) for i, (src, dst) in enumerate(pairs)]
    for c in copies:
        c.start()
    if flip == 0:
        for c in copies[:2]:
            c.wait()
        ahead = copies[-2:]
        copies = copies[2:-2]
        gates = gates_ref[...]
        route = (gates / jnp.sum(gates, axis=1, keepdims=True)).astype(BF).astype(F32)
        expert = iota(table_ref.shape, 1)
        table = jnp.zeros(table_ref.shape, F32)
        for k in range(gates.shape[1]):
            table = jnp.where(expert == ids_ref[:, k : k + 1], route[:, k : k + 1], table)
        table_ref[...] = table.astype(BF)

    step = 8
    blocks = rows // step
    many, cols = step * group, step * cache
    scaling = hd ** (-0.5)
    same = iota((many, cols), 0) // group == iota((many, cols), 1) // cache
    col_row = iota((1, cols), 1) // cache
    col_pos = iota((1, cols), 1) % cache + tensor_pos * cache
    new_here = iota((many, 2 * step), 1) == iota((many, 2 * step), 0) // group
    new_here = new_here & (tensor_pos == 0)

    for c in copies[:5]:
        c.wait()
    for r in range(rows):
        nk_scr[r * kvh : (r + 1) * kvh, :] = nk_ref[r].astype(F32)
        nv_scr[r * kvh : (r + 1) * kvh, :] = nv_ref[r].astype(F32)
    query_gain = qg_ref[...]
    new_rows = pl.ds(which, rows, stride=kvh)
    key_norm = rms_scale(nk_scr[new_rows, :], kg_ref[...])
    new_value = nv_scr[new_rows, :]
    empty = jnp.zeros((step, hd), F32)
    for c in copies[5:]:
        c.wait()

    def rows_of(ref, b, size):
        return ref[b * step : (b + 1) * step].reshape(size, hd)

    def with_empty(value, b):
        return jnp.concatenate([value[b * step : (b + 1) * step], empty]).astype(BF)

    queries = []
    for b in range(blocks):
        query = rows_of(q_ref, b, many).astype(F32)
        queries.append(rms_scale(query, query_gain).astype(BF))
    for b in range(blocks):
        limit = jnp.zeros((1, cols), I32)
        for i in range(step):
            limit = jnp.where(col_row == i, lengths[b * step + i], limit)
        included = same & (col_pos < limit)
        scores = matmul_t(queries[b], rows_of(k_ref, b, cols)) * scaling
        score[b, :, :cols] = jnp.where(included, scores, -1e30)
        scores = matmul_t(queries[b], with_empty(key_norm, b)) * scaling
        score[b, :, cols:] = jnp.where(new_here, scores, -1e30)
    for b in range(blocks):
        top = jnp.maximum(jnp.max(score[b], axis=1, keepdims=True), -1e29).astype(BF).astype(F32)
        tops[b * many : (b + 1) * many, :] = jnp.broadcast_to(top, (many, LANES))
    for b in range(blocks):
        top = tops[b * many : (b + 1) * many, 0:1]
        weights = jnp.exp(score[b] - top).astype(BF)
        weight[b] = weights
        total = jnp.sum(weights.astype(F32), axis=1, keepdims=True)
        totals[b * many : (b + 1) * many, :] = jnp.broadcast_to(total, (many, LANES))
    for b in range(blocks):
        num[b * many : (b + 1) * many, :] = matmul(
            weight[b, :, :cols], rows_of(v_ref, b, cols)
        ) + matmul(weight[b, :, cols:], with_empty(new_value, b))

    lane = iota((rows, LANES), 1)
    for t in range(parts):
        slot = (tensor_pos % parts) ^ t
        side = jnp.zeros((rows, LANES), F32)
        for h in range(heads_own):
            own = pl.ds(t * heads_own + h, rows, stride=group)
            out_ref[slot, :, h * hd : (h + 1) * hd] = num[own, :].astype(BF)
            total = totals[own, :]
            high = total.astype(BF).astype(F32)
            side = jnp.where(lane == h, tops[own, :], side)
            side = jnp.where(lane == heads_own + h, high, side)
            side = jnp.where(lane == 2 * heads_own + h, total - high, side)
        out_ref[slot, :, heads_own * hd :] = side.astype(BF)
    if flip == 0:
        for c in ahead:
            c.wait()


def attention(
    flip, lengths, queries, new_keys, new_values, key_cache, value_cache, qg, kg, parts, more
):
    rows, heads, hd = queries.shape
    kvh, cache = key_cache.shape[1:3]
    group = heads // kvh
    blocks = rows // 8
    args = [lengths, queries, new_keys, new_values, key_cache, value_cache]
    args = [in_hbm(a) for a in (*args, qg.reshape(1, -1), kg.reshape(1, -1))]
    outs = [jax.ShapeDtypeStruct((parts // kvh, rows, heads // parts * hd + LANES), BF)]
    scratch = [
        pltpu.SMEM((rows,), I32),
        pltpu.VMEM((rows, group, hd), BF),
        pltpu.VMEM(new_keys.shape, BF),
        pltpu.VMEM(new_values.shape, BF),
        pltpu.VMEM((rows, cache, hd), BF),
        pltpu.VMEM((rows, cache, hd), BF),
        pltpu.VMEM((1, hd), F32),
        pltpu.VMEM((1, hd), F32),
        pltpu.VMEM((rows * kvh, hd), F32),
        pltpu.VMEM((rows * kvh, hd), F32),
        pltpu.VMEM((rows * group, hd), F32),
        pltpu.VMEM((rows * group, LANES), F32),
        pltpu.VMEM((rows * group, LANES), F32),
        pltpu.VMEM((blocks, 8 * group, 8 * (cache + 2)), F32),
        pltpu.VMEM((blocks, 8 * group, 8 * (cache + 2)), BF),
        pltpu.SemaphoreType.DMA((12,)),
    ]
    specs = [pl.BlockSpec(memory_space=pltpu.HBM)] * len(args)
    size = 2 * rows * group * hd * 8
    if flip == 0:
        expert_ids, gate_weights, lanes, later, earlier = more
        args += [in_hbm(a) for a in (expert_ids, gate_weights, later)] + [earlier]
        specs += [pl.BlockSpec(memory_space=pltpu.HBM)] * 3 + [pl.BlockSpec(memory_space=pl.ANY)]
        outs.append(jax.ShapeDtypeStruct((expert_ids.shape[0], lanes), BF))
        outs += [pltpu.VMEM((later.shape[0] // 2, later.shape[1]), later.dtype)] * 2
        scratch += [pltpu.VMEM(expert_ids.shape, I32), pltpu.VMEM(gate_weights.shape, F32)]
        size = size + 2 * later.size
    return pl.pallas_call(
        functools.partial(attention_kernel, flip),
        out_shape=tuple(outs),
        in_specs=specs,
        out_specs=(pl.BlockSpec(memory_space=pltpu.VMEM),) * len(outs),
        scratch_shapes=scratch,
        compiler_params=pltpu.CompilerParams(vmem_limit_bytes=16 * MIB),
        cost_estimate=pl.CostEstimate(flops=size, bytes_accessed=size, transcendentals=0),
        name="attention",
    )(*args)


def projection_kernel(parts, cuts, *refs):
    got = refs[:parts]
    w_refs, refs = refs[parts : parts + cuts], refs[parts + cuts :]
    ahead_hbm, out_ref, ahead_ref, attn, sem = refs
    ahead = pltpu.make_async_copy(ahead_hbm, ahead_ref, sem)
    ahead.start()
    tensor_pos = lax.axis_index("tensor")
    width = w_refs[0].shape[1]
    depth = attn.shape[1]
    share = out_ref.shape[2]
    hd = LANES
    heads_own = depth // hd
    size = 512
    sides = [g[:, depth:].astype(F32) for g in got]
    tops = [s[:, :heads_own] for s in sides]
    top = functools.reduce(jnp.maximum, tops)
    factors = [jnp.exp(t - top) for t in tops]
    totals = [
        f * (s[:, heads_own : 2 * heads_own] + s[:, 2 * heads_own : 3 * heads_own])
        for f, s in zip(factors, sides)
    ]
    total = functools.reduce(jnp.add, totals)
    factors = [f / total for f in factors]
    for h in range(heads_own):
        cols = slice(h * hd, (h + 1) * hd)
        terms = [g[:, cols].astype(F32) * f[:, h : h + 1] for g, f in zip(got, factors)]
        attn[:, cols] = functools.reduce(jnp.add, terms).astype(BF)
    part = depth // cuts
    for start in range(0, width, size):
        cols = slice(start, start + size)
        result = functools.reduce(
            jnp.add,
            [
                matmul(attn[:, k * part : (k + 1) * part], w_ref[:, cols])
                for k, w_ref in enumerate(w_refs)
            ],
        )
        for t in range(parts):
            slot = tensor_pos ^ t
            block = result[t * share : (t + 1) * share].astype(BF)
            out_ref[slot & 1, slot >> 1, :, cols] = block
    ahead.wait()


def projection(got, weights, share, later):
    parts = len(got)
    rows = got[0].shape[0]
    depth = sum(w.shape[0] for w in weights)
    width = weights[0].shape[1]
    vmem = pl.BlockSpec(memory_space=pltpu.VMEM)
    return pl.pallas_call(
        functools.partial(projection_kernel, parts, len(weights)),
        out_shape=(
            jax.ShapeDtypeStruct((2, parts // 2, share, width), BF),
            pltpu.VMEM(later.shape, later.dtype),
        ),
        in_specs=[vmem] * (parts + len(weights)) + [pl.BlockSpec(memory_space=pltpu.HBM)],
        out_specs=(vmem, vmem),
        scratch_shapes=[pltpu.VMEM((rows, depth), BF), pltpu.SemaphoreType.DMA],
        compiler_params=pltpu.CompilerParams(vmem_limit_bytes=12 * MIB),
        name="projection",
    )(*got, *weights, in_hbm(later))


def expert_kernel(slots, x_ref, gate, up, down_hbm, out_ref, down, xc, act, res, sem):
    own = lax.axis_index("dp") * lax.axis_size("tensor") + lax.axis_index("tensor")
    rows = x_ref.shape[0]
    _, width, hidden = gate.shape
    padded = res.shape[0]
    fsize = 384
    dsize = 1024
    chunks = width // dsize

    def down_copy(i):
        cols = pl.ds(i * dsize, dsize)
        return pltpu.make_async_copy(down_hbm.at[0, :, cols], down.at[:, cols], sem.at[i])

    for i in range(chunks):
        down_copy(i).start()
    table = x_ref[:, width:]
    pick = (iota((16, table.shape[1]), 1) == own).astype(F32).astype(BF)
    named = matmul_t(pick, table) != 0.0
    before = (iota((rows, rows), 0) < iota((rows, rows), 1)).astype(F32).astype(BF)
    place = matmul(named.astype(F32).astype(BF), before)
    place = jnp.where(named, place, -1.0)[:1]
    take = (iota((slots, rows), 0).astype(F32) == place).astype(F32).astype(BF)
    for i in range(chunks):
        cols = slice(i * dsize, (i + 1) * dsize)
        xc[:, cols] = matmul(take, x_ref[:, cols]).astype(BF)

    lane = iota(table.shape, 1)
    weight = jnp.sum(jnp.where(lane == own, table.astype(F32), 0.0), axis=1, keepdims=True)
    named = jnp.broadcast_to((weight != 0.0).astype(F32), (rows, LANES)).astype(BF)
    after = (iota((rows, rows), 1) < iota((rows, rows), 0)).astype(F32).astype(BF)
    place = matmul(after, named)[:, :1]
    spread = jnp.where(iota((rows, padded), 1).astype(F32) == place, weight, 0.0).astype(BF)
    if padded > slots:
        res[slots:, :] = jnp.zeros((padded - slots, dsize), BF)

    for i in range(hidden // fsize):
        cols = slice(i * fsize, (i + 1) * fsize)
        g = matmul(xc[...], gate[0, :, cols])
        u = matmul(xc[...], up[0, :, cols])
        act[:, cols] = (g / (1.0 + jnp.exp(-g)) * u).astype(BF)
    for i in range(chunks):
        down_copy(i).wait()
        cols = slice(i * dsize, (i + 1) * dsize)
        res[:slots, :] = matmul(act[...], down[:, cols]).astype(BF)
        out_ref[:, cols] = matmul(spread, res[...]).astype(BF)


def experts(x, expert_gate, expert_up, expert_down, share):
    rows = x.shape[0]
    _, width, hidden = expert_gate.shape
    slots = rows // share * CAP
    vmem = pl.BlockSpec(memory_space=pltpu.VMEM)
    return pl.pallas_call(
        functools.partial(expert_kernel, slots),
        out_shape=jax.ShapeDtypeStruct((rows, width), BF),
        in_specs=[vmem] * 3 + [pl.BlockSpec(memory_space=pltpu.HBM)],
        out_specs=vmem,
        scratch_shapes=[
            pltpu.VMEM((hidden, width), BF),
            pltpu.VMEM((slots, width), BF),
            pltpu.VMEM((slots, hidden), BF),
            pltpu.VMEM((-(-slots // LANES) * LANES, 1024), BF),
            pltpu.SemaphoreType.DMA((width // 1024,)),
        ],
        compiler_params=pltpu.CompilerParams(vmem_limit_bytes=(16 + rows // 32) * MIB),
        name="experts",
    )(x, expert_gate, expert_up, in_hbm(expert_down))


class Plan:
    def __init__(self, dp, tensor):
        self.zlen = min(4, dp)
        xlen, ylen = dp // self.zlen, tensor // 2
        self.count = dp * tensor
        self.core = 1
        self.y = [2 * j for j in range(1, ylen)]
        self.z = [tensor * xlen * j for j in range(1, self.zlen)]
        self.x = [tensor * j for j in range(1, xlen)]
        self.diagonal = [jx + jy for jx in self.x for jy in self.y]

    def swap(self, value, flip):
        return lax.ppermute(value, ("dp", "tensor"), [(i, i ^ flip) for i in range(self.count)])

    def swaps(self, values, flips):
        pairs = list(zip(values, flips))[::-1]
        return [self.swap(value.astype(BF), flip) for value, flip in pairs][::-1]

    def spread(self, value, flips):
        return self.swaps([value] * len(flips), flips)


def total_of(values):
    return functools.reduce(jnp.add, [v.astype(F32) for v in values])


def shards(
    queries,
    new_keys,
    new_values,
    key_cache,
    value_cache,
    lengths,
    residual_in,
    query_gain,
    key_gain,
    out_proj,
    norm_gain,
    expert_ids,
    gate_weights,
    expert_gate,
    expert_up,
    expert_down,
):
    tensor = lax.axis_size("tensor")
    dp = lax.axis_size("dp")
    plan = Plan(dp, tensor)
    share, width = residual_in.shape
    lanes = -(-dp * tensor // LANES) * LANES

    inputs = (lengths, queries, new_keys, new_values, key_cache, value_cache, query_gain, key_gain)
    groups = key_cache.shape[1]
    got, local = [], None
    for flip in reversed(range(groups)):
        more = (expert_ids, gate_weights, lanes, out_proj, local)
        results = attention(flip, *inputs, tensor, more)
        local = results[0]
        for j in range(0, tensor // groups, 2):
            far = flip * (tensor // groups) + j
            pair = local[j : j + 2]
            if far:
                pair = plan.swap(pair, far)
            got += [pair[0], plan.swap(pair[1], plan.core)]
    _, table, *weights = results
    partial, expert_gate = projection(got, weights, share, expert_gate)
    pair = total_of([partial[0], plan.swap(partial[1], plan.core)])
    projected = total_of([pair[0]] + plan.swaps(list(pair[1:]), plan.y))
    hidden = residual_in.astype(F32) + projected
    normed = rms_scale(hidden, norm_gain).astype(BF)

    mine = jnp.concatenate([normed, table], axis=1)
    others = plan.spread(mine, plan.z)
    first = mine + others[0][:, :1] * 0
    near_x = plan.spread(first, plan.x)
    near_y = plan.spread(first, plan.y)
    rest = jnp.concatenate(others)
    far_diagonal = plan.spread(rest, plan.diagonal)
    far_y = plan.spread(rest, plan.y)
    far_x = plan.spread(jnp.concatenate(others + near_y), plan.x)
    pieces = [jnp.concatenate([mine] + others + near_x + near_y)] + far_y + far_x + far_diagonal
    x = jnp.concatenate(pieces + [plan.swap(piece, plan.core) for piece in pieces])

    result = experts(x, expert_gate, expert_up, expert_down, share)

    sizes = [piece.shape[0] for piece in pieces]
    starts = [sum(sizes[:i]) for i in range(len(sizes) + 1)]
    every = starts[-1]
    sums = [
        total_of(
            [
                result[starts[i] : starts[i + 1]],
                plan.swap(result[every + starts[i] : every + starts[i + 1]], plan.core),
            ]
        )
        for i in reversed(range(len(sizes)))
    ][::-1]
    back = plan.swaps(sums[1:], plan.y + plan.x + plan.diagonal)
    height, x_end = rest.shape[0], len(plan.y) + len(plan.x)
    column = sums[0][: share + height]
    near = sums[0][share + height :].reshape(-1, share, width)
    through = [v[height:] for v in back[len(plan.y) : x_end]]
    through = total_of([near[len(plan.x) :].reshape(-1, width)] + through)
    others = total_of([v[:height] for v in back[::-1]] + [column[share:]])
    others = plan.swaps(list(others.reshape(-1, share, width)), plan.z)
    wait = back[len(plan.y)][:share, :1] * 0
    near_x = plan.swaps([value + wait for value in near[: len(plan.x)]], plan.x)
    near_y = plan.swaps(list(through.reshape(-1, share, width)), plan.y)
    moe_sum = total_of([column[:share]] + near_x + near_y + others)
    return (hidden + moe_sum).astype(BF)


def solution(mesh):
    return jax.shard_map(
        shards,
        mesh=mesh,
        in_specs=(
            P("dp", None, None),
            P("dp", None, None),
            P("dp", None, None),
            P("dp", None, "tensor", None),
            P("dp", None, "tensor", None),
            P("dp"),
            P(("dp", "tensor"), None),
            P(),
            P(),
            P("tensor", None),
            P(),
            P(("dp", "tensor"), None),
            P(("dp", "tensor"), None),
            P(("dp", "tensor"), None, None),
            P(("dp", "tensor"), None, None),
            P(("dp", "tensor"), None, None),
        ),
        out_specs=P(("dp", "tensor"), None),
        check_vma=False,
    )
```

```python
import functools

import jax
import jax.numpy as jnp
from jax import lax
from jax.experimental import pallas as pl
from jax.experimental.pallas import tpu as pltpu
from jax.sharding import PartitionSpec as P

BF = jnp.bfloat16
F32 = jnp.float32
I32 = jnp.int32
MIB = 1 << 20
LANES = 128
CAP = 3


def rms_scale(values, gain):
    mean_sq = jnp.mean(values * values, axis=-1, keepdims=True)
    return values * lax.rsqrt(mean_sq + 1e-06) * gain


def matmul(a, b):
    return jnp.dot(a, b, preferred_element_type=F32)


def matmul_t(a, b):
    return lax.dot_general(a, b, (((1,), (1,)), ((), ())), preferred_element_type=F32)


def iota(shape, dim):
    return lax.broadcasted_iota(I32, shape, dim)


def in_hbm(value):
    return pltpu.with_memory_space_constraint(value, pltpu.HBM)


def attention_kernel(flip, *refs):
    sources, refs = refs[:8], refs[8:]
    if flip == 0:
        ids_hbm, gates_hbm, w_hbm, _, out_ref, table_ref, *w_refs = refs[:8]
        refs = refs[8:]
    else:
        out_ref, refs = refs[0], refs[1:]
    len_hbm, q_hbm, nk_hbm, nv_hbm, k_hbm, v_hbm, qg_hbm, kg_hbm = sources
    lengths, q_ref, nk_ref, nv_ref, k_ref, v_ref, qg_ref, kg_ref = refs[:8]
    nk_scr, nv_scr, num, tops, totals, score, weight, sem = refs[8:16]
    tensor_pos = lax.axis_index("tensor")
    rows, group, hd = q_ref.shape
    kvh, cache = k_hbm.shape[1], k_ref.shape[1]
    heads_own = q_hbm.shape[1] // lax.axis_size("tensor")
    parts = group // heads_own
    which = (tensor_pos // parts) ^ flip
    heads = pl.ds(pl.multiple_of(which * group, group), group)
    pairs = [
        (len_hbm, lengths),
        (nk_hbm, nk_ref),
        (nv_hbm, nv_ref),
        (qg_hbm, qg_ref),
        (kg_hbm, kg_ref),
        (q_hbm.at[:, heads], q_ref),
        (k_hbm.at[:, which], k_ref),
        (v_hbm.at[:, which], v_ref),
    ]
    if flip == 0:
        ids_ref, gates_ref = refs[16:]
        pairs = [(ids_hbm, ids_ref), (gates_hbm, gates_ref)] + pairs
        size = w_refs[0].shape[0]
        pairs += [(w_hbm.at[pl.ds(i * size, size)], ref) for i, ref in enumerate(w_refs)]
    copies = [pltpu.make_async_copy(src, dst, sem.at[i]) for i, (src, dst) in enumerate(pairs)]
    for c in copies:
        c.start()
    if flip == 0:
        for c in copies[:2]:
            c.wait()
        ahead = copies[-2:]
        copies = copies[2:-2]
        gates = gates_ref[...]
        route = (gates / jnp.sum(gates, axis=1, keepdims=True)).astype(BF).astype(F32)
        expert = iota(table_ref.shape, 1)
        table = jnp.zeros(table_ref.shape, F32)
        for k in range(gates.shape[1]):
            table = jnp.where(expert == ids_ref[:, k : k + 1], route[:, k : k + 1], table)
        table_ref[...] = table.astype(BF)

    step = 8
    blocks = rows // step
    many, cols = step * group, step * cache
    scaling = hd ** (-0.5)
    same = iota((many, cols), 0) // group == iota((many, cols), 1) // cache
    col_row = iota((1, cols), 1) // cache
    col_pos = iota((1, cols), 1) % cache + tensor_pos * cache
    new_here = iota((many, 2 * step), 1) == iota((many, 2 * step), 0) // group
    new_here = new_here & (tensor_pos == 0)

    for c in copies[:5]:
        c.wait()
    for r in range(rows):
        nk_scr[r * kvh : (r + 1) * kvh, :] = nk_ref[r].astype(F32)
        nv_scr[r * kvh : (r + 1) * kvh, :] = nv_ref[r].astype(F32)
    query_gain = qg_ref[...]
    new_rows = pl.ds(which, rows, stride=kvh)
    key_norm = rms_scale(nk_scr[new_rows, :], kg_ref[...])
    new_value = nv_scr[new_rows, :]
    empty = jnp.zeros((step, hd), F32)
    for c in copies[5:]:
        c.wait()

    def rows_of(ref, b, size):
        return ref[b * step : (b + 1) * step].reshape(size, hd)

    def with_empty(value, b):
        return jnp.concatenate([value[b * step : (b + 1) * step], empty]).astype(BF)

    queries = []
    for b in range(blocks):
        query = rows_of(q_ref, b, many).astype(F32)
        queries.append(rms_scale(query, query_gain).astype(BF))
    for b in range(blocks):
        limit = jnp.zeros((1, cols), I32)
        for i in range(step):
            limit = jnp.where(col_row == i, lengths[b * step + i], limit)
        included = same & (col_pos < limit)
        scores = matmul_t(queries[b], rows_of(k_ref, b, cols)) * scaling
        score[b, :, :cols] = jnp.where(included, scores, -1e30)
        scores = matmul_t(queries[b], with_empty(key_norm, b)) * scaling
        score[b, :, cols:] = jnp.where(new_here, scores, -1e30)
    for b in range(blocks):
        top = jnp.maximum(jnp.max(score[b], axis=1, keepdims=True), -1e29).astype(BF).astype(F32)
        tops[b * many : (b + 1) * many, :] = jnp.broadcast_to(top, (many, LANES))
    for b in range(blocks):
        top = tops[b * many : (b + 1) * many, 0:1]
        weights = jnp.exp(score[b] - top).astype(BF)
        weight[b] = weights
        total = jnp.sum(weights.astype(F32), axis=1, keepdims=True)
        totals[b * many : (b + 1) * many, :] = jnp.broadcast_to(total, (many, LANES))
    for b in range(blocks):
        num[b * many : (b + 1) * many, :] = matmul(
            weight[b, :, :cols], rows_of(v_ref, b, cols)
        ) + matmul(weight[b, :, cols:], with_empty(new_value, b))

    lane = iota((rows, LANES), 1)
    for t in range(parts):
        slot = (tensor_pos % parts) ^ t
        side = jnp.zeros((rows, LANES), F32)
        for h in range(heads_own):
            own = pl.ds(t * heads_own + h, rows, stride=group)
            out_ref[slot, :, h * hd : (h + 1) * hd] = num[own, :].astype(BF)
            total = totals[own, :]
            high = total.astype(BF).astype(F32)
            side = jnp.where(lane == h, tops[own, :], side)
            side = jnp.where(lane == heads_own + h, high, side)
            side = jnp.where(lane == 2 * heads_own + h, total - high, side)
        out_ref[slot, :, heads_own * hd :] = side.astype(BF)
    if flip == 0:
        for c in ahead:
            c.wait()


def attention(
    flip, lengths, queries, new_keys, new_values, key_cache, value_cache, qg, kg, parts, more
):
    rows, heads, hd = queries.shape
    kvh, cache = key_cache.shape[1:3]
    group = heads // kvh
    blocks = rows // 8
    args = [lengths, queries, new_keys, new_values, key_cache, value_cache]
    args = [in_hbm(a) for a in (*args, qg.reshape(1, -1), kg.reshape(1, -1))]
    outs = [jax.ShapeDtypeStruct((parts // kvh, rows, heads // parts * hd + LANES), BF)]
    scratch = [
        pltpu.SMEM((rows,), I32),
        pltpu.VMEM((rows, group, hd), BF),
        pltpu.VMEM(new_keys.shape, BF),
        pltpu.VMEM(new_values.shape, BF),
        pltpu.VMEM((rows, cache, hd), BF),
        pltpu.VMEM((rows, cache, hd), BF),
        pltpu.VMEM((1, hd), F32),
        pltpu.VMEM((1, hd), F32),
        pltpu.VMEM((rows * kvh, hd), F32),
        pltpu.VMEM((rows * kvh, hd), F32),
        pltpu.VMEM((rows * group, hd), F32),
        pltpu.VMEM((rows * group, LANES), F32),
        pltpu.VMEM((rows * group, LANES), F32),
        pltpu.VMEM((blocks, 8 * group, 8 * (cache + 2)), F32),
        pltpu.VMEM((blocks, 8 * group, 8 * (cache + 2)), BF),
        pltpu.SemaphoreType.DMA((12,)),
    ]
    specs = [pl.BlockSpec(memory_space=pltpu.HBM)] * len(args)
    size = 2 * rows * group * hd * 8
    if flip == 0:
        expert_ids, gate_weights, lanes, later, earlier = more
        args += [in_hbm(a) for a in (expert_ids, gate_weights, later)] + [earlier]
        specs += [pl.BlockSpec(memory_space=pltpu.HBM)] * 3 + [pl.BlockSpec(memory_space=pl.ANY)]
        outs.append(jax.ShapeDtypeStruct((expert_ids.shape[0], lanes), BF))
        outs += [pltpu.VMEM((later.shape[0] // 2, later.shape[1]), later.dtype)] * 2
        scratch += [pltpu.VMEM(expert_ids.shape, I32), pltpu.VMEM(gate_weights.shape, F32)]
        size = size + 2 * later.size
    return pl.pallas_call(
        functools.partial(attention_kernel, flip),
        out_shape=tuple(outs),
        in_specs=specs,
        out_specs=(pl.BlockSpec(memory_space=pltpu.VMEM),) * len(outs),
        scratch_shapes=scratch,
        compiler_params=pltpu.CompilerParams(vmem_limit_bytes=16 * MIB),
        cost_estimate=pl.CostEstimate(flops=size, bytes_accessed=size, transcendentals=0),
        name="attention",
    )(*args)


def projection_kernel(parts, cuts, *refs):
    got = refs[:parts]
    w_refs, refs = refs[parts : parts + cuts], refs[parts + cuts :]
    out_ref, attn = refs
    tensor_pos = lax.axis_index("tensor")
    width = w_refs[0].shape[1]
    depth = attn.shape[1]
    share = out_ref.shape[2]
    hd = LANES
    heads_own = depth // hd
    size = 512
    sides = [g[:, depth:].astype(F32) for g in got]
    tops = [s[:, :heads_own] for s in sides]
    top = functools.reduce(jnp.maximum, tops)
    factors = [jnp.exp(t - top) for t in tops]
    totals = [
        f * (s[:, heads_own : 2 * heads_own] + s[:, 2 * heads_own : 3 * heads_own])
        for f, s in zip(factors, sides)
    ]
    total = functools.reduce(jnp.add, totals)
    factors = [f / total for f in factors]
    for h in range(heads_own):
        cols = slice(h * hd, (h + 1) * hd)
        terms = [g[:, cols].astype(F32) * f[:, h : h + 1] for g, f in zip(got, factors)]
        attn[:, cols] = functools.reduce(jnp.add, terms).astype(BF)
    part = depth // cuts
    for start in range(0, width, size):
        cols = slice(start, start + size)
        result = functools.reduce(
            jnp.add,
            [
                matmul(attn[:, k * part : (k + 1) * part], w_ref[:, cols])
                for k, w_ref in enumerate(w_refs)
            ],
        )
        for t in range(parts):
            slot = tensor_pos ^ t
            block = result[t * share : (t + 1) * share].astype(BF)
            out_ref[slot & 1, slot >> 1, :, cols] = block


def projection(got, weights, share):
    parts = len(got)
    rows = got[0].shape[0]
    depth = sum(w.shape[0] for w in weights)
    width = weights[0].shape[1]
    vmem = pl.BlockSpec(memory_space=pltpu.VMEM)
    return pl.pallas_call(
        functools.partial(projection_kernel, parts, len(weights)),
        out_shape=jax.ShapeDtypeStruct((2, parts // 2, share, width), BF),
        in_specs=[vmem] * (parts + len(weights)),
        out_specs=vmem,
        scratch_shapes=[pltpu.VMEM((rows, depth), BF)],
        compiler_params=pltpu.CompilerParams(vmem_limit_bytes=12 * MIB),
        name="projection",
    )(*got, *weights)


def expert_kernel(slots, sizes, *refs):
    x_ref, gate, up, down_hbm = refs[:4]
    outs = refs[4 : 4 + len(sizes)]
    down, xc, act, res, sem = refs[4 + len(sizes) :]
    own = lax.axis_index("dp") * lax.axis_size("tensor") + lax.axis_index("tensor")
    rows = x_ref.shape[0]
    _, width, hidden = gate.shape
    padded = res.shape[0]
    fsize = 384
    dsize = 1024
    chunks = width // dsize

    def down_copy(i):
        cols = pl.ds(i * dsize, dsize)
        return pltpu.make_async_copy(down_hbm.at[0, :, cols], down.at[:, cols], sem.at[i])

    for i in range(chunks):
        down_copy(i).start()
    table = x_ref[:, width:]
    pick = (iota((16, table.shape[1]), 1) == own).astype(F32).astype(BF)
    named = matmul_t(pick, table) != 0.0
    before = (iota((rows, rows), 0) < iota((rows, rows), 1)).astype(F32).astype(BF)
    place = matmul(named.astype(F32).astype(BF), before)
    place = jnp.where(named, place, -1.0)[:1]
    take = (iota((slots, rows), 0).astype(F32) == place).astype(F32).astype(BF)
    for i in range(chunks):
        cols = slice(i * dsize, (i + 1) * dsize)
        xc[:, cols] = matmul(take, x_ref[:, cols]).astype(BF)

    lane = iota(table.shape, 1)
    weight = jnp.sum(jnp.where(lane == own, table.astype(F32), 0.0), axis=1, keepdims=True)
    named = jnp.broadcast_to((weight != 0.0).astype(F32), (rows, LANES)).astype(BF)
    after = (iota((rows, rows), 1) < iota((rows, rows), 0)).astype(F32).astype(BF)
    place = matmul(after, named)[:, :1]
    spread = jnp.where(iota((rows, padded), 1).astype(F32) == place, weight, 0.0).astype(BF)
    if padded > slots:
        res[slots:, :] = jnp.zeros((padded - slots, dsize), BF)

    for i in range(hidden // fsize):
        cols = slice(i * fsize, (i + 1) * fsize)
        g = matmul(xc[...], gate[0, :, cols])
        u = matmul(xc[...], up[0, :, cols])
        act[:, cols] = (g / (1.0 + jnp.exp(-g)) * u).astype(BF)
    for i in range(chunks):
        down_copy(i).wait()
        cols = slice(i * dsize, (i + 1) * dsize)
        res[:slots, :] = matmul(act[...], down[:, cols]).astype(BF)
        result, start = matmul(spread, res[...]), 0
        for size, out in zip(sizes, outs):
            out[:, cols] = result[start : start + size].astype(BF)
            start += size


def experts(x, expert_gate, expert_up, expert_down, share, sizes):
    rows = x.shape[0]
    _, width, hidden = expert_gate.shape
    slots = rows // share * CAP
    vmem = pl.BlockSpec(memory_space=pltpu.VMEM)
    return pl.pallas_call(
        functools.partial(expert_kernel, slots, sizes),
        out_shape=tuple(jax.ShapeDtypeStruct((size, width), BF) for size in sizes),
        in_specs=[vmem] * 3 + [pl.BlockSpec(memory_space=pltpu.HBM)],
        out_specs=(vmem,) * len(sizes),
        scratch_shapes=[
            pltpu.VMEM((hidden, width), BF),
            pltpu.VMEM((slots, width), BF),
            pltpu.VMEM((slots, hidden), BF),
            pltpu.VMEM((-(-slots // LANES) * LANES, 1024), BF),
            pltpu.SemaphoreType.DMA((width // 1024,)),
        ],
        compiler_params=pltpu.CompilerParams(vmem_limit_bytes=(16 + rows // 32) * MIB),
        name="experts",
    )(x, expert_gate, expert_up, in_hbm(expert_down))


class Plan:
    def __init__(self, dp, tensor):
        self.zlen = min(4, dp)
        xlen, ylen = dp // self.zlen, tensor // 2
        self.count = dp * tensor
        self.core = 1
        self.y = [2 * j for j in range(1, ylen)]
        self.z = [tensor * xlen * j for j in range(1, self.zlen)]
        self.x = [tensor * j for j in range(1, xlen)]
        self.diagonal = [jx + jy for jx in self.x for jy in self.y]

    def swap(self, value, flip):
        return lax.ppermute(value, ("dp", "tensor"), [(i, i ^ flip) for i in range(self.count)])

    def swaps(self, values, flips):
        pairs = list(zip(values, flips))[::-1]
        return [self.swap(value.astype(BF), flip) for value, flip in pairs][::-1]

    def spread(self, value, flips):
        return self.swaps([value] * len(flips), flips)


def total_of(values):
    return functools.reduce(jnp.add, [v.astype(F32) for v in values])


def shards(
    queries,
    new_keys,
    new_values,
    key_cache,
    value_cache,
    lengths,
    residual_in,
    query_gain,
    key_gain,
    out_proj,
    norm_gain,
    expert_ids,
    gate_weights,
    expert_gate,
    expert_up,
    expert_down,
):
    tensor = lax.axis_size("tensor")
    dp = lax.axis_size("dp")
    plan = Plan(dp, tensor)
    share, width = residual_in.shape
    lanes = -(-dp * tensor // LANES) * LANES

    inputs = (lengths, queries, new_keys, new_values, key_cache, value_cache, query_gain, key_gain)
    groups = key_cache.shape[1]
    got, local = [], None
    for flip in reversed(range(groups)):
        more = (expert_ids, gate_weights, lanes, out_proj, local)
        results = attention(flip, *inputs, tensor, more)
        local = results[0]
        for j in range(0, tensor // groups, 2):
            far = flip * (tensor // groups) + j
            pair = local[j : j + 2]
            if far:
                pair = plan.swap(pair, far)
            got += [pair[0], plan.swap(pair[1], plan.core)]
    _, table, *weights = results
    partial = projection(got, weights, share)
    pair = total_of([partial[0], plan.swap(partial[1], plan.core)])
    projected = total_of([pair[0]] + plan.swaps(list(pair[1:]), plan.y))
    hidden = residual_in.astype(F32) + projected
    normed = rms_scale(hidden, norm_gain).astype(BF)

    mine = jnp.concatenate([normed, table], axis=1)
    others = plan.spread(mine, plan.z)
    first = mine + others[0][:, :1] * 0
    near_x = plan.spread(first, plan.x)
    near_y = plan.spread(first, plan.y)
    rest = jnp.concatenate(others)
    far_diagonal = plan.spread(rest, plan.diagonal)
    far_y = plan.spread(rest, plan.y)
    far_x = plan.spread(jnp.concatenate(others + near_y), plan.x)
    pieces = [jnp.concatenate([mine] + others + near_x + near_y)] + far_y + far_x + far_diagonal
    x = jnp.concatenate(pieces + [plan.swap(piece, plan.core) for piece in pieces])

    sizes = [piece.shape[0] for piece in pieces] * 2
    results = experts(x, expert_gate, expert_up, expert_down, share, sizes)

    half = len(pieces)
    sums = [
        total_of([results[i], plan.swap(results[half + i], plan.core)])
        for i in reversed(range(half))
    ][::-1]
    back = plan.swaps(sums[1:], plan.y + plan.x + plan.diagonal)
    height, x_end = rest.shape[0], len(plan.y) + len(plan.x)
    column = sums[0][: share + height]
    near = sums[0][share + height :].reshape(-1, share, width)
    through = [v[height:] for v in back[len(plan.y) : x_end]]
    through = total_of([near[len(plan.x) :].reshape(-1, width)] + through)
    others = total_of([v[:height] for v in back[::-1]] + [column[share:]])
    others = plan.swaps(list(others.reshape(-1, share, width)), plan.z)
    wait = back[len(plan.y)][:share, :1] * 0
    near_x = plan.swaps([value + wait for value in near[: len(plan.x)]], plan.x)
    near_y = plan.swaps(list(through.reshape(-1, share, width)), plan.y)
    moe_sum = total_of([column[:share]] + near_x + near_y + others)
    return (hidden + moe_sum).astype(BF)


def solution(mesh):
    return jax.shard_map(
        shards,
        mesh=mesh,
        in_specs=(
            P("dp", None, None),
            P("dp", None, None),
            P("dp", None, None),
            P("dp", None, "tensor", None),
            P("dp", None, "tensor", None),
            P("dp"),
            P(("dp", "tensor"), None),
            P(),
            P(),
            P("tensor", None),
            P(),
            P(("dp", "tensor"), None),
            P(("dp", "tensor"), None),
            P(("dp", "tensor"), None, None),
            P(("dp", "tensor"), None, None),
            P(("dp", "tensor"), None, None),
        ),
        out_specs=P(("dp", "tensor"), None),
        check_vma=False,
    )
```

```python
import functools

import jax
import jax.numpy as jnp
from jax import lax
from jax.experimental import pallas as pl
from jax.experimental.pallas import tpu as pltpu
from jax.sharding import PartitionSpec as P

BF = jnp.bfloat16
F32 = jnp.float32
I32 = jnp.int32
MIB = 1 << 20
LANES = 128
CAP = 3


def rms_scale(values, gain):
    mean_sq = jnp.mean(values * values, axis=-1, keepdims=True)
    return values * lax.rsqrt(mean_sq + 1e-06) * gain


def matmul(a, b):
    return jnp.dot(a, b, preferred_element_type=F32)


def matmul_t(a, b):
    return lax.dot_general(a, b, (((1,), (1,)), ((), ())), preferred_element_type=F32)


def iota(shape, dim):
    return lax.broadcasted_iota(I32, shape, dim)


def in_hbm(value):
    return pltpu.with_memory_space_constraint(value, pltpu.HBM)


def attention_kernel(flip, *refs):
    sources, refs = refs[:8], refs[8:]
    if flip == 0:
        ids_hbm, gates_hbm, w_hbm, _, out_ref, table_ref, *w_refs = refs[:8]
        refs = refs[8:]
    else:
        out_ref, refs = refs[0], refs[1:]
    len_hbm, q_hbm, nk_hbm, nv_hbm, k_hbm, v_hbm, qg_hbm, kg_hbm = sources
    lengths, q_ref, nk_ref, nv_ref, k_ref, v_ref, qg_ref, kg_ref = refs[:8]
    nk_scr, nv_scr, num, tops, totals, score, weight, sem = refs[8:16]
    tensor_pos = lax.axis_index("tensor")
    rows, group, hd = q_ref.shape
    kvh, cache = k_hbm.shape[1], k_ref.shape[1]
    heads_own = q_hbm.shape[1] // lax.axis_size("tensor")
    parts = group // heads_own
    which = (tensor_pos // parts) ^ flip
    heads = pl.ds(pl.multiple_of(which * group, group), group)
    pairs = [
        (len_hbm, lengths),
        (nk_hbm, nk_ref),
        (nv_hbm, nv_ref),
        (qg_hbm, qg_ref),
        (kg_hbm, kg_ref),
        (q_hbm.at[:, heads], q_ref),
        (k_hbm.at[:, which], k_ref),
        (v_hbm.at[:, which], v_ref),
    ]
    if flip == 0:
        ids_ref, gates_ref = refs[16:]
        pairs = [(ids_hbm, ids_ref), (gates_hbm, gates_ref)] + pairs
        size = w_refs[0].shape[0]
        pairs += [(w_hbm.at[pl.ds(i * size, size)], ref) for i, ref in enumerate(w_refs)]
    copies = [pltpu.make_async_copy(src, dst, sem.at[i]) for i, (src, dst) in enumerate(pairs)]
    for c in copies:
        c.start()
    if flip == 0:
        for c in copies[:2]:
            c.wait()
        ahead = copies[-2:]
        copies = copies[2:-2]
        gates = gates_ref[...]
        route = (gates / jnp.sum(gates, axis=1, keepdims=True)).astype(BF).astype(F32)
        expert = iota(table_ref.shape, 1)
        table = jnp.zeros(table_ref.shape, F32)
        for k in range(gates.shape[1]):
            table = jnp.where(expert == ids_ref[:, k : k + 1], route[:, k : k + 1], table)
        table_ref[...] = table.astype(BF)

    step = 8
    blocks = rows // step
    many, cols = step * group, step * cache
    scaling = hd ** (-0.5)
    same = iota((many, cols), 0) // group == iota((many, cols), 1) // cache
    col_row = iota((1, cols), 1) // cache
    col_pos = iota((1, cols), 1) % cache + tensor_pos * cache
    new_here = iota((many, 2 * step), 1) == iota((many, 2 * step), 0) // group
    new_here = new_here & (tensor_pos == 0)

    for c in copies[:5]:
        c.wait()
    for r in range(rows):
        nk_scr[r * kvh : (r + 1) * kvh, :] = nk_ref[r].astype(F32)
        nv_scr[r * kvh : (r + 1) * kvh, :] = nv_ref[r].astype(F32)
    query_gain = qg_ref[...]
    new_rows = pl.ds(which, rows, stride=kvh)
    key_norm = rms_scale(nk_scr[new_rows, :], kg_ref[...])
    new_value = nv_scr[new_rows, :]
    empty = jnp.zeros((step, hd), F32)
    for c in copies[5:]:
        c.wait()

    def rows_of(ref, b, size):
        return ref[b * step : (b + 1) * step].reshape(size, hd)

    def with_empty(value, b):
        return jnp.concatenate([value[b * step : (b + 1) * step], empty]).astype(BF)

    queries = []
    for b in range(blocks):
        query = rows_of(q_ref, b, many).astype(F32)
        queries.append(rms_scale(query, query_gain).astype(BF))
    for b in range(blocks):
        limit = jnp.zeros((1, cols), I32)
        for i in range(step):
            limit = jnp.where(col_row == i, lengths[b * step + i], limit)
        included = same & (col_pos < limit)
        scores = matmul_t(queries[b], rows_of(k_ref, b, cols)) * scaling
        score[b, :, :cols] = jnp.where(included, scores, -1e30)
        scores = matmul_t(queries[b], with_empty(key_norm, b)) * scaling
        score[b, :, cols:] = jnp.where(new_here, scores, -1e30)
    for b in range(blocks):
        top = jnp.maximum(jnp.max(score[b], axis=1, keepdims=True), -1e29).astype(BF).astype(F32)
        tops[b * many : (b + 1) * many, :] = jnp.broadcast_to(top, (many, LANES))
    for b in range(blocks):
        top = tops[b * many : (b + 1) * many, 0:1]
        weights = jnp.exp(score[b] - top).astype(BF)
        weight[b] = weights
        total = jnp.sum(weights.astype(F32), axis=1, keepdims=True)
        totals[b * many : (b + 1) * many, :] = jnp.broadcast_to(total, (many, LANES))
    for b in range(blocks):
        num[b * many : (b + 1) * many, :] = matmul(
            weight[b, :, :cols], rows_of(v_ref, b, cols)
        ) + matmul(weight[b, :, cols:], with_empty(new_value, b))

    lane = iota((rows, LANES), 1)
    for t in range(parts):
        slot = (tensor_pos % parts) ^ t
        side = jnp.zeros((rows, LANES), F32)
        for h in range(heads_own):
            own = pl.ds(t * heads_own + h, rows, stride=group)
            out_ref[slot, :, h * hd : (h + 1) * hd] = num[own, :].astype(BF)
            total = totals[own, :]
            high = total.astype(BF).astype(F32)
            side = jnp.where(lane == h, tops[own, :], side)
            side = jnp.where(lane == heads_own + h, high, side)
            side = jnp.where(lane == 2 * heads_own + h, total - high, side)
        out_ref[slot, :, heads_own * hd :] = side.astype(BF)
    if flip == 0:
        for c in ahead:
            c.wait()


def attention(
    flip, lengths, queries, new_keys, new_values, key_cache, value_cache, qg, kg, parts, more
):
    rows, heads, hd = queries.shape
    kvh, cache = key_cache.shape[1:3]
    group = heads // kvh
    blocks = rows // 8
    args = [lengths, queries, new_keys, new_values, key_cache, value_cache]
    args = [in_hbm(a) for a in (*args, qg.reshape(1, -1), kg.reshape(1, -1))]
    outs = [jax.ShapeDtypeStruct((parts // kvh, rows, heads // parts * hd + LANES), BF)]
    scratch = [
        pltpu.SMEM((rows,), I32),
        pltpu.VMEM((rows, group, hd), BF),
        pltpu.VMEM(new_keys.shape, BF),
        pltpu.VMEM(new_values.shape, BF),
        pltpu.VMEM((rows, cache, hd), BF),
        pltpu.VMEM((rows, cache, hd), BF),
        pltpu.VMEM((1, hd), F32),
        pltpu.VMEM((1, hd), F32),
        pltpu.VMEM((rows * kvh, hd), F32),
        pltpu.VMEM((rows * kvh, hd), F32),
        pltpu.VMEM((rows * group, hd), F32),
        pltpu.VMEM((rows * group, LANES), F32),
        pltpu.VMEM((rows * group, LANES), F32),
        pltpu.VMEM((blocks, 8 * group, 8 * (cache + 2)), F32),
        pltpu.VMEM((blocks, 8 * group, 8 * (cache + 2)), BF),
        pltpu.SemaphoreType.DMA((12,)),
    ]
    specs = [pl.BlockSpec(memory_space=pltpu.HBM)] * len(args)
    size = 2 * rows * group * hd * 8
    if flip == 0:
        expert_ids, gate_weights, lanes, later, earlier = more
        args += [in_hbm(a) for a in (expert_ids, gate_weights, later)] + [earlier]
        specs += [pl.BlockSpec(memory_space=pltpu.HBM)] * 3 + [pl.BlockSpec(memory_space=pl.ANY)]
        outs.append(jax.ShapeDtypeStruct((expert_ids.shape[0], lanes), BF))
        outs += [pltpu.VMEM((later.shape[0] // 2, later.shape[1]), later.dtype)] * 2
        scratch += [pltpu.VMEM(expert_ids.shape, I32), pltpu.VMEM(gate_weights.shape, F32)]
        size = size + 2 * later.size
    return pl.pallas_call(
        functools.partial(attention_kernel, flip),
        out_shape=tuple(outs),
        in_specs=specs,
        out_specs=(pl.BlockSpec(memory_space=pltpu.VMEM),) * len(outs),
        scratch_shapes=scratch,
        compiler_params=pltpu.CompilerParams(vmem_limit_bytes=16 * MIB),
        cost_estimate=pl.CostEstimate(flops=size, bytes_accessed=size, transcendentals=0),
        name="attention",
    )(*args)


def projection_kernel(parts, cuts, *refs):
    got = refs[:parts]
    w_refs, refs = refs[parts : parts + cuts], refs[parts + cuts :]
    out_ref, attn = refs
    tensor_pos = lax.axis_index("tensor")
    width = w_refs[0].shape[1]
    depth = attn.shape[1]
    share = out_ref.shape[2]
    hd = LANES
    heads_own = depth // hd
    size = 512
    sides = [g[:, depth:].astype(F32) for g in got]
    tops = [s[:, :heads_own] for s in sides]
    top = functools.reduce(jnp.maximum, tops)
    factors = [jnp.exp(t - top) for t in tops]
    totals = [
        f * (s[:, heads_own : 2 * heads_own] + s[:, 2 * heads_own : 3 * heads_own])
        for f, s in zip(factors, sides)
    ]
    total = functools.reduce(jnp.add, totals)
    factors = [f / total for f in factors]
    for h in range(heads_own):
        cols = slice(h * hd, (h + 1) * hd)
        terms = [g[:, cols].astype(F32) * f[:, h : h + 1] for g, f in zip(got, factors)]
        attn[:, cols] = functools.reduce(jnp.add, terms).astype(BF)
    part = depth // cuts
    for start in range(0, width, size):
        cols = slice(start, start + size)
        result = functools.reduce(
            jnp.add,
            [
                matmul(attn[:, k * part : (k + 1) * part], w_ref[:, cols])
                for k, w_ref in enumerate(w_refs)
            ],
        )
        for t in range(parts):
            slot = tensor_pos ^ t
            block = result[t * share : (t + 1) * share].astype(BF)
            out_ref[slot & 1, slot >> 1, :, cols] = block


def projection(got, weights, share):
    parts = len(got)
    rows = got[0].shape[0]
    depth = sum(w.shape[0] for w in weights)
    width = weights[0].shape[1]
    vmem = pl.BlockSpec(memory_space=pltpu.VMEM)
    return pl.pallas_call(
        functools.partial(projection_kernel, parts, len(weights)),
        out_shape=jax.ShapeDtypeStruct((2, parts // 2, share, width), BF),
        in_specs=[vmem] * (parts + len(weights)),
        out_specs=vmem,
        scratch_shapes=[pltpu.VMEM((rows, depth), BF)],
        compiler_params=pltpu.CompilerParams(vmem_limit_bytes=12 * MIB),
        name="projection",
    )(*got, *weights)


def expert_kernel(slots, sizes, *refs):
    x_ref, gate, up, down_hbm = refs[:4]
    outs = refs[4 : 4 + len(sizes)]
    down, xc, act, res, sem = refs[4 + len(sizes) :]
    own = lax.axis_index("dp") * lax.axis_size("tensor") + lax.axis_index("tensor")
    rows = x_ref.shape[0]
    _, width, hidden = gate.shape
    padded = res.shape[0]
    fsize = 384
    dsize = 1024
    chunks = width // dsize

    def down_copy(i):
        cols = pl.ds(i * dsize, dsize)
        return pltpu.make_async_copy(down_hbm.at[0, :, cols], down.at[:, cols], sem.at[i])

    for i in range(chunks):
        down_copy(i).start()
    table = x_ref[:, width:]
    pick = (iota((16, table.shape[1]), 1) == own).astype(F32).astype(BF)
    named = matmul_t(pick, table) != 0.0
    before = (iota((rows, rows), 0) < iota((rows, rows), 1)).astype(F32).astype(BF)
    place = matmul(named.astype(F32).astype(BF), before)
    place = jnp.where(named, place, -1.0)[:1]
    take = (iota((slots, rows), 0).astype(F32) == place).astype(F32).astype(BF)
    for i in range(chunks):
        cols = slice(i * dsize, (i + 1) * dsize)
        xc[:, cols] = matmul(take, x_ref[:, cols]).astype(BF)

    lane = iota(table.shape, 1)
    weight = jnp.sum(jnp.where(lane == own, table.astype(F32), 0.0), axis=1, keepdims=True)
    named = jnp.broadcast_to((weight != 0.0).astype(F32), (rows, LANES)).astype(BF)
    after = (iota((rows, rows), 1) < iota((rows, rows), 0)).astype(F32).astype(BF)
    place = matmul(after, named)[:, :1]
    spread = jnp.where(iota((rows, padded), 1).astype(F32) == place, weight, 0.0).astype(BF)
    if padded > slots:
        res[slots:, :] = jnp.zeros((padded - slots, dsize), BF)

    for i in range(hidden // fsize):
        cols = slice(i * fsize, (i + 1) * fsize)
        g = matmul(xc[...], gate[0, :, cols])
        u = matmul(xc[...], up[0, :, cols])
        act[:, cols] = (g / (1.0 + jnp.exp(-g)) * u).astype(BF)
    for i in range(chunks):
        down_copy(i).wait()
        cols = slice(i * dsize, (i + 1) * dsize)
        res[:slots, :] = matmul(act[...], down[:, cols]).astype(BF)
        result, start = matmul(spread, res[...]), 0
        for size, out in zip(sizes, outs):
            out[:, cols] = result[start : start + size].astype(BF)
            start += size


def experts(x, expert_gate, expert_up, expert_down, share, sizes):
    rows = x.shape[0]
    _, width, hidden = expert_gate.shape
    slots = rows // share * CAP
    vmem = pl.BlockSpec(memory_space=pltpu.VMEM)
    return pl.pallas_call(
        functools.partial(expert_kernel, slots, sizes),
        out_shape=tuple(jax.ShapeDtypeStruct((size, width), BF) for size in sizes),
        in_specs=[vmem] * 3 + [pl.BlockSpec(memory_space=pltpu.HBM)],
        out_specs=(vmem,) * len(sizes),
        scratch_shapes=[
            pltpu.VMEM((hidden, width), BF),
            pltpu.VMEM((slots, width), BF),
            pltpu.VMEM((slots, hidden), BF),
            pltpu.VMEM((-(-slots // LANES) * LANES, 1024), BF),
            pltpu.SemaphoreType.DMA((width // 1024,)),
        ],
        compiler_params=pltpu.CompilerParams(vmem_limit_bytes=(16 + rows // 32) * MIB),
        name="experts",
    )(x, expert_gate, expert_up, in_hbm(expert_down))


class Plan:
    def __init__(self, dp, tensor):
        self.zlen = min(4, dp)
        xlen, ylen = dp // self.zlen, tensor // 2
        self.count = dp * tensor
        self.core = 1
        self.y = [2 * j for j in range(1, ylen)]
        self.z = [tensor * xlen * j for j in range(1, self.zlen)]
        self.x = [tensor * j for j in range(1, xlen)]
        self.diagonal = [jx + jy for jx in self.x for jy in self.y]

    def swap(self, value, flip):
        return lax.ppermute(value, ("dp", "tensor"), [(i, i ^ flip) for i in range(self.count)])

    def swaps(self, values, flips):
        pairs = list(zip(values, flips))[::-1]
        return [self.swap(value.astype(BF), flip) for value, flip in pairs][::-1]

    def spread(self, value, flips):
        return self.swaps([value] * len(flips), flips)


def total_of(values):
    return functools.reduce(jnp.add, [v.astype(F32) for v in values])


def shards(
    queries,
    new_keys,
    new_values,
    key_cache,
    value_cache,
    lengths,
    residual_in,
    query_gain,
    key_gain,
    out_proj,
    norm_gain,
    expert_ids,
    gate_weights,
    expert_gate,
    expert_up,
    expert_down,
):
    tensor = lax.axis_size("tensor")
    dp = lax.axis_size("dp")
    plan = Plan(dp, tensor)
    share, width = residual_in.shape
    lanes = -(-dp * tensor // LANES) * LANES

    inputs = (lengths, queries, new_keys, new_values, key_cache, value_cache, query_gain, key_gain)
    groups = key_cache.shape[1]
    got, local = [], None
    for flip in reversed(range(groups)):
        more = (expert_ids, gate_weights, lanes, out_proj, local)
        results = attention(flip, *inputs, tensor, more)
        local = results[0]
        for j in range(0, tensor // groups, 2):
            far = flip * (tensor // groups) + j
            pair = local[j : j + 2]
            if far:
                pair = plan.swap(pair, far)
            got += [pair[0], plan.swap(pair[1], plan.core)]
    _, table, *weights = results
    partial = projection(got, weights, share)
    pair = total_of([partial[0], plan.swap(partial[1], plan.core)])
    projected = total_of([pair[0]] + plan.swaps(list(pair[1:]), plan.y))
    hidden = residual_in.astype(F32) + projected
    normed = rms_scale(hidden, norm_gain).astype(BF)

    mine = jnp.concatenate([normed, table], axis=1)
    others = plan.spread(mine, plan.z)
    cut = plan.zlen // 2
    first = jnp.concatenate([mine + others[0][:, :1] * 0] + others[: cut - 1])
    rest = jnp.concatenate(others[cut - 1 :])
    near_x = plan.spread(first, plan.x)
    near_y = plan.spread(first, plan.y)
    far_diagonal = plan.spread(rest, plan.diagonal)
    far_y = plan.spread(rest, plan.y)
    far_x = plan.spread(jnp.concatenate([rest] + near_y), plan.x)

    def ordered(column, near_x, near_y, far_x, far_y, far_diagonal):
        size, height = first.shape[0], rest.shape[0]
        own = [column] + [v[:share] for v in near_x] + [v[:share] for v in near_y]
        along_y = [[near[share:], far] for near, far in zip(near_y, far_y)]
        through = [
            [v[height + k * size : height + (k + 1) * size] for k in range(len(plan.y))]
            for v in far_x
        ]
        along_x = [
            [near[share:], far[:height]] + [v[:share] for v in more]
            for near, far, more in zip(near_x, far_x, through)
        ]
        more = [v for row in through for v in row]
        diagonal = [[near[share:], far] for near, far in zip(more, far_diagonal)]
        return [own] + along_y + along_x + diagonal

    lists = [[jnp.concatenate([mine] + others)], near_x, near_y, far_x, far_y, far_diagonal]
    pieces = ordered(lists[0][0], *lists[1:])
    lists = [[plan.swap(v, plan.core) for v in values] for values in lists]
    there = ordered(lists[0][0], *lists[1:])
    x = jnp.concatenate([v for piece in pieces + there for v in piece])

    sizes = [sum(v.shape[0] for v in piece) for piece in pieces] * 2
    results = experts(x, expert_gate, expert_up, expert_down, share, sizes)

    half = len(pieces)
    sums = [
        total_of([results[i], plan.swap(results[half + i], plan.core)])
        for i in reversed(range(half))
    ][::-1]
    back = plan.swaps(sums[1:], plan.y + plan.x + plan.diagonal)
    height, x_end = (plan.zlen - 1) * share, len(plan.y) + len(plan.x)
    column = sums[0][: share + height]
    near = sums[0][share + height :].reshape(-1, share, width)
    through = [v[height:] for v in back[len(plan.y) : x_end]]
    through = total_of([near[len(plan.x) :].reshape(-1, width)] + through)
    others = total_of([v[:height] for v in back[::-1]] + [column[share:]])
    others = plan.swaps(list(others.reshape(-1, share, width)), plan.z)
    wait = back[len(plan.y)][:share, :1] * 0
    near_x = plan.swaps([value + wait for value in near[: len(plan.x)]], plan.x)
    near_y = plan.swaps(list(through.reshape(-1, share, width)), plan.y)
    moe_sum = total_of([column[:share]] + near_x + near_y + others)
    return (hidden + moe_sum).astype(BF)


def solution(mesh):
    return jax.shard_map(
        shards,
        mesh=mesh,
        in_specs=(
            P("dp", None, None),
            P("dp", None, None),
            P("dp", None, None),
            P("dp", None, "tensor", None),
            P("dp", None, "tensor", None),
            P("dp"),
            P(("dp", "tensor"), None),
            P(),
            P(),
            P("tensor", None),
            P(),
            P(("dp", "tensor"), None),
            P(("dp", "tensor"), None),
            P(("dp", "tensor"), None, None),
            P(("dp", "tensor"), None, None),
            P(("dp", "tensor"), None, None),
        ),
        out_specs=P(("dp", "tensor"), None),
        check_vma=False,
    )
```

```python
import functools

import jax
import jax.numpy as jnp
from jax import lax
from jax.experimental import pallas as pl
from jax.experimental.pallas import tpu as pltpu
from jax.sharding import PartitionSpec as P

BF = jnp.bfloat16
F32 = jnp.float32
I32 = jnp.int32
MIB = 1 << 20
LANES = 128
CAP = 3


def rms_scale(values, gain):
    mean_sq = jnp.mean(values * values, axis=-1, keepdims=True)
    return values * lax.rsqrt(mean_sq + 1e-06) * gain


def matmul(a, b):
    return jnp.dot(a, b, preferred_element_type=F32)


def matmul_t(a, b):
    return lax.dot_general(a, b, (((1,), (1,)), ((), ())), preferred_element_type=F32)


def iota(shape, dim):
    return lax.broadcasted_iota(I32, shape, dim)


def in_hbm(value):
    return pltpu.with_memory_space_constraint(value, pltpu.HBM)


def attention_kernel(flip, *refs):
    sources, refs = refs[:8], refs[8:]
    if flip == 0:
        ids_hbm, gates_hbm, w_hbm, _, out_ref, table_ref, *w_refs = refs[:8]
        refs = refs[8:]
    else:
        out_ref, refs = refs[0], refs[1:]
    len_hbm, q_hbm, nk_hbm, nv_hbm, k_hbm, v_hbm, qg_hbm, kg_hbm = sources
    lengths, q_ref, nk_ref, nv_ref, k_ref, v_ref, qg_ref, kg_ref = refs[:8]
    nk_scr, nv_scr, num, tops, totals, score, weight, sem = refs[8:16]
    tensor_pos = lax.axis_index("tensor")
    rows, group, hd = q_ref.shape
    kvh, cache = k_hbm.shape[1], k_ref.shape[1]
    heads_own = q_hbm.shape[1] // lax.axis_size("tensor")
    parts = group // heads_own
    which = (tensor_pos // parts) ^ flip
    heads = pl.ds(pl.multiple_of(which * group, group), group)
    pairs = [
        (len_hbm, lengths),
        (nk_hbm, nk_ref),
        (nv_hbm, nv_ref),
        (qg_hbm, qg_ref),
        (kg_hbm, kg_ref),
        (q_hbm.at[:, heads], q_ref),
        (k_hbm.at[:, which], k_ref),
        (v_hbm.at[:, which], v_ref),
    ]
    if flip == 0:
        ids_ref, gates_ref = refs[16:]
        pairs = [(ids_hbm, ids_ref), (gates_hbm, gates_ref)] + pairs
        size = w_refs[0].shape[0]
        pairs += [(w_hbm.at[pl.ds(i * size, size)], ref) for i, ref in enumerate(w_refs)]
    copies = [pltpu.make_async_copy(src, dst, sem.at[i]) for i, (src, dst) in enumerate(pairs)]
    for c in copies:
        c.start()
    if flip == 0:
        for c in copies[:2]:
            c.wait()
        ahead = copies[-2:]
        copies = copies[2:-2]
        gates = gates_ref[...]
        route = (gates / jnp.sum(gates, axis=1, keepdims=True)).astype(BF).astype(F32)
        expert = iota(table_ref.shape, 1)
        table = jnp.zeros(table_ref.shape, F32)
        for k in range(gates.shape[1]):
            table = jnp.where(expert == ids_ref[:, k : k + 1], route[:, k : k + 1], table)
        table_ref[...] = table.astype(BF)

    step = 8
    blocks = rows // step
    many, cols = step * group, step * cache
    scaling = hd ** (-0.5)
    same = iota((many, cols), 0) // group == iota((many, cols), 1) // cache
    col_row = iota((1, cols), 1) // cache
    col_pos = iota((1, cols), 1) % cache + tensor_pos * cache
    new_here = iota((many, 2 * step), 1) == iota((many, 2 * step), 0) // group
    new_here = new_here & (tensor_pos == 0)

    for c in copies[:5]:
        c.wait()
    for r in range(rows):
        nk_scr[r * kvh : (r + 1) * kvh, :] = nk_ref[r].astype(F32)
        nv_scr[r * kvh : (r + 1) * kvh, :] = nv_ref[r].astype(F32)
    query_gain = qg_ref[...]
    new_rows = pl.ds(which, rows, stride=kvh)
    key_norm = rms_scale(nk_scr[new_rows, :], kg_ref[...])
    new_value = nv_scr[new_rows, :]
    empty = jnp.zeros((step, hd), F32)
    for c in copies[5:]:
        c.wait()

    def rows_of(ref, b, size):
        return ref[b * step : (b + 1) * step].reshape(size, hd)

    def with_empty(value, b):
        return jnp.concatenate([value[b * step : (b + 1) * step], empty]).astype(BF)

    queries = []
    for b in range(blocks):
        query = rows_of(q_ref, b, many).astype(F32)
        queries.append(rms_scale(query, query_gain).astype(BF))
    for b in range(blocks):
        limit = jnp.zeros((1, cols), I32)
        for i in range(step):
            limit = jnp.where(col_row == i, lengths[b * step + i], limit)
        included = same & (col_pos < limit)
        scores = matmul_t(queries[b], rows_of(k_ref, b, cols)) * scaling
        score[b, :, :cols] = jnp.where(included, scores, -1e30)
        scores = matmul_t(queries[b], with_empty(key_norm, b)) * scaling
        score[b, :, cols:] = jnp.where(new_here, scores, -1e30)
    for b in range(blocks):
        top = jnp.maximum(jnp.max(score[b], axis=1, keepdims=True), -1e29).astype(BF).astype(F32)
        tops[b * many : (b + 1) * many, :] = jnp.broadcast_to(top, (many, LANES))
    for b in range(blocks):
        top = tops[b * many : (b + 1) * many, 0:1]
        weights = jnp.exp(score[b] - top).astype(BF)
        weight[b] = weights
        total = jnp.sum(weights.astype(F32), axis=1, keepdims=True)
        totals[b * many : (b + 1) * many, :] = jnp.broadcast_to(total, (many, LANES))
    for b in range(blocks):
        num[b * many : (b + 1) * many, :] = matmul(
            weight[b, :, :cols], rows_of(v_ref, b, cols)
        ) + matmul(weight[b, :, cols:], with_empty(new_value, b))

    lane = iota((rows, LANES), 1)
    for t in range(parts):
        slot = (tensor_pos % parts) ^ t
        side = jnp.zeros((rows, LANES), F32)
        for h in range(heads_own):
            own = pl.ds(t * heads_own + h, rows, stride=group)
            out_ref[slot, :, h * hd : (h + 1) * hd] = num[own, :].astype(BF)
            total = totals[own, :]
            high = total.astype(BF).astype(F32)
            side = jnp.where(lane == h, tops[own, :], side)
            side = jnp.where(lane == heads_own + h, high, side)
            side = jnp.where(lane == 2 * heads_own + h, total - high, side)
        out_ref[slot, :, heads_own * hd :] = side.astype(BF)
    if flip == 0:
        for c in ahead:
            c.wait()


def attention(
    flip, lengths, queries, new_keys, new_values, key_cache, value_cache, qg, kg, parts, more
):
    rows, heads, hd = queries.shape
    kvh, cache = key_cache.shape[1:3]
    group = heads // kvh
    blocks = rows // 8
    args = [lengths, queries, new_keys, new_values, key_cache, value_cache]
    args = [in_hbm(a) for a in (*args, qg.reshape(1, -1), kg.reshape(1, -1))]
    outs = [jax.ShapeDtypeStruct((parts // kvh, rows, heads // parts * hd + LANES), BF)]
    scratch = [
        pltpu.SMEM((rows,), I32),
        pltpu.VMEM((rows, group, hd), BF),
        pltpu.VMEM(new_keys.shape, BF),
        pltpu.VMEM(new_values.shape, BF),
        pltpu.VMEM((rows, cache, hd), BF),
        pltpu.VMEM((rows, cache, hd), BF),
        pltpu.VMEM((1, hd), F32),
        pltpu.VMEM((1, hd), F32),
        pltpu.VMEM((rows * kvh, hd), F32),
        pltpu.VMEM((rows * kvh, hd), F32),
        pltpu.VMEM((rows * group, hd), F32),
        pltpu.VMEM((rows * group, LANES), F32),
        pltpu.VMEM((rows * group, LANES), F32),
        pltpu.VMEM((blocks, 8 * group, 8 * (cache + 2)), F32),
        pltpu.VMEM((blocks, 8 * group, 8 * (cache + 2)), BF),
        pltpu.SemaphoreType.DMA((12,)),
    ]
    specs = [pl.BlockSpec(memory_space=pltpu.HBM)] * len(args)
    size = 2 * rows * group * hd * 8
    if flip == 0:
        expert_ids, gate_weights, lanes, later, earlier = more
        args += [in_hbm(a) for a in (expert_ids, gate_weights, later)] + [earlier]
        specs += [pl.BlockSpec(memory_space=pltpu.HBM)] * 3 + [pl.BlockSpec(memory_space=pl.ANY)]
        outs.append(jax.ShapeDtypeStruct((expert_ids.shape[0], lanes), BF))
        outs += [pltpu.VMEM((later.shape[0] // 2, later.shape[1]), later.dtype)] * 2
        scratch += [pltpu.VMEM(expert_ids.shape, I32), pltpu.VMEM(gate_weights.shape, F32)]
        size = size + 2 * later.size
    return pl.pallas_call(
        functools.partial(attention_kernel, flip),
        out_shape=tuple(outs),
        in_specs=specs,
        out_specs=(pl.BlockSpec(memory_space=pltpu.VMEM),) * len(outs),
        scratch_shapes=scratch,
        compiler_params=pltpu.CompilerParams(vmem_limit_bytes=16 * MIB),
        cost_estimate=pl.CostEstimate(flops=size, bytes_accessed=size, transcendentals=0),
        name="attention",
    )(*args)


def projection_kernel(parts, cuts, *refs):
    got = refs[:parts]
    w_refs, refs = refs[parts : parts + cuts], refs[parts + cuts :]
    out_ref, attn = refs
    tensor_pos = lax.axis_index("tensor")
    width = w_refs[0].shape[1]
    depth = attn.shape[1]
    share = out_ref.shape[2]
    hd = LANES
    heads_own = depth // hd
    size = 512
    sides = [g[:, depth:].astype(F32) for g in got]
    tops = [s[:, :heads_own] for s in sides]
    top = functools.reduce(jnp.maximum, tops)
    factors = [jnp.exp(t - top) for t in tops]
    totals = [
        f * (s[:, heads_own : 2 * heads_own] + s[:, 2 * heads_own : 3 * heads_own])
        for f, s in zip(factors, sides)
    ]
    total = functools.reduce(jnp.add, totals)
    factors = [f / total for f in factors]
    for h in range(heads_own):
        cols = slice(h * hd, (h + 1) * hd)
        terms = [g[:, cols].astype(F32) * f[:, h : h + 1] for g, f in zip(got, factors)]
        attn[:, cols] = functools.reduce(jnp.add, terms).astype(BF)
    part = depth // cuts
    for start in range(0, width, size):
        cols = slice(start, start + size)
        result = functools.reduce(
            jnp.add,
            [
                matmul(attn[:, k * part : (k + 1) * part], w_ref[:, cols])
                for k, w_ref in enumerate(w_refs)
            ],
        )
        for t in range(parts):
            slot = tensor_pos ^ t
            block = result[t * share : (t + 1) * share].astype(BF)
            out_ref[slot & 1, slot >> 1, :, cols] = block


def projection(got, weights, share):
    parts = len(got)
    rows = got[0].shape[0]
    depth = sum(w.shape[0] for w in weights)
    width = weights[0].shape[1]
    vmem = pl.BlockSpec(memory_space=pltpu.VMEM)
    return pl.pallas_call(
        functools.partial(projection_kernel, parts, len(weights)),
        out_shape=jax.ShapeDtypeStruct((2, parts // 2, share, width), BF),
        in_specs=[vmem] * (parts + len(weights)),
        out_specs=vmem,
        scratch_shapes=[pltpu.VMEM((rows, depth), BF)],
        compiler_params=pltpu.CompilerParams(vmem_limit_bytes=12 * MIB),
        name="projection",
    )(*got, *weights)


def expert_kernel(slots, sizes, *refs):
    x_ref, gate, up, down_hbm = refs[:4]
    outs = refs[4 : 4 + len(sizes)]
    down, xc, act, res, sem = refs[4 + len(sizes) :]
    own = lax.axis_index("dp") * lax.axis_size("tensor") + lax.axis_index("tensor")
    rows = x_ref.shape[0]
    _, width, hidden = gate.shape
    padded = res.shape[0]
    fsize = 384
    dsize = 1024
    chunks = width // dsize

    def down_copy(i):
        cols = pl.ds(i * dsize, dsize)
        return pltpu.make_async_copy(down_hbm.at[0, :, cols], down.at[:, cols], sem.at[i])

    for i in range(chunks):
        down_copy(i).start()
    table = x_ref[:, width:]
    pick = (iota((16, table.shape[1]), 1) == own).astype(F32).astype(BF)
    named = matmul_t(pick, table) != 0.0
    before = (iota((rows, rows), 0) < iota((rows, rows), 1)).astype(F32).astype(BF)
    place = matmul(named.astype(F32).astype(BF), before)
    place = jnp.where(named, place, -1.0)[:1]
    take = (iota((slots, rows), 0).astype(F32) == place).astype(F32).astype(BF)
    for i in range(chunks):
        cols = slice(i * dsize, (i + 1) * dsize)
        xc[:, cols] = matmul(take, x_ref[:, cols]).astype(BF)

    lane = iota(table.shape, 1)
    weight = jnp.sum(jnp.where(lane == own, table.astype(F32), 0.0), axis=1, keepdims=True)
    named = jnp.broadcast_to((weight != 0.0).astype(F32), (rows, LANES)).astype(BF)
    after = (iota((rows, rows), 1) < iota((rows, rows), 0)).astype(F32).astype(BF)
    place = matmul(after, named)[:, :1]
    spread = jnp.where(iota((rows, padded), 1).astype(F32) == place, weight, 0.0).astype(BF)
    if padded > slots:
        res[slots:, :] = jnp.zeros((padded - slots, dsize), BF)

    for i in range(hidden // fsize):
        cols = slice(i * fsize, (i + 1) * fsize)
        g = matmul(xc[...], gate[0, :, cols])
        u = matmul(xc[...], up[0, :, cols])
        act[:, cols] = (g / (1.0 + jnp.exp(-g)) * u).astype(BF)
    for i in range(chunks):
        down_copy(i).wait()
        cols = slice(i * dsize, (i + 1) * dsize)
        res[:slots, :] = matmul(act[...], down[:, cols]).astype(BF)
        result, start = matmul(spread, res[...]), 0
        for size, out in zip(sizes, outs):
            out[:, cols] = result[start : start + size].astype(BF)
            start += size


def experts(x, expert_gate, expert_up, expert_down, share, sizes):
    rows = x.shape[0]
    _, width, hidden = expert_gate.shape
    slots = rows // share * CAP
    vmem = pl.BlockSpec(memory_space=pltpu.VMEM)
    return pl.pallas_call(
        functools.partial(expert_kernel, slots, sizes),
        out_shape=tuple(jax.ShapeDtypeStruct((size, width), BF) for size in sizes),
        in_specs=[vmem] * 3 + [pl.BlockSpec(memory_space=pltpu.HBM)],
        out_specs=(vmem,) * len(sizes),
        scratch_shapes=[
            pltpu.VMEM((hidden, width), BF),
            pltpu.VMEM((slots, width), BF),
            pltpu.VMEM((slots, hidden), BF),
            pltpu.VMEM((-(-slots // LANES) * LANES, 1024), BF),
            pltpu.SemaphoreType.DMA((width // 1024,)),
        ],
        compiler_params=pltpu.CompilerParams(vmem_limit_bytes=(16 + rows // 32) * MIB),
        name="experts",
    )(x, expert_gate, expert_up, in_hbm(expert_down))


class Plan:
    def __init__(self, dp, tensor):
        self.zlen = min(4, dp)
        xlen, ylen = dp // self.zlen, tensor // 2
        self.count = dp * tensor
        self.core = 1
        self.y = [2 * j for j in range(1, ylen)]
        self.z = [tensor * xlen * j for j in range(1, self.zlen)]
        self.x = [tensor * j for j in range(1, xlen)]
        self.diagonal = [jx + jy for jx in self.x for jy in self.y]

    def swap(self, value, flip):
        return lax.ppermute(value, ("dp", "tensor"), [(i, i ^ flip) for i in range(self.count)])

    def swaps(self, values, flips):
        pairs = list(zip(values, flips))[::-1]
        return [self.swap(value.astype(BF), flip) for value, flip in pairs][::-1]

    def spread(self, value, flips):
        return self.swaps([value] * len(flips), flips)


def total_of(values):
    return functools.reduce(jnp.add, [v.astype(F32) for v in values])


def shards(
    queries,
    new_keys,
    new_values,
    key_cache,
    value_cache,
    lengths,
    residual_in,
    query_gain,
    key_gain,
    out_proj,
    norm_gain,
    expert_ids,
    gate_weights,
    expert_gate,
    expert_up,
    expert_down,
):
    tensor = lax.axis_size("tensor")
    dp = lax.axis_size("dp")
    plan = Plan(dp, tensor)
    share, width = residual_in.shape
    lanes = -(-dp * tensor // LANES) * LANES

    inputs = (lengths, queries, new_keys, new_values, key_cache, value_cache, query_gain, key_gain)
    groups = key_cache.shape[1]
    got, local = [], None
    for flip in reversed(range(groups)):
        more = (expert_ids, gate_weights, lanes, out_proj, local)
        results = attention(flip, *inputs, tensor, more)
        local = results[0]
        for j in range(0, tensor // groups, 2):
            far = flip * (tensor // groups) + j
            pair = local[j : j + 2]
            if far:
                pair = plan.swap(pair, far)
            got += [pair[0], plan.swap(pair[1], plan.core)]
    _, table, *weights = results
    partial = projection(got, weights, share)
    pair = total_of([partial[0], plan.swap(partial[1], plan.core)])
    projected = total_of([pair[0]] + plan.swaps(list(pair[1:]), plan.y))
    hidden = residual_in.astype(F32) + projected
    normed = rms_scale(hidden, norm_gain).astype(BF)

    mine = jnp.concatenate([normed, table], axis=1)
    others = plan.spread(mine, plan.z)
    first = mine + others[0][:, :1] * 0
    near_x = plan.spread(first, plan.x)
    near_y = plan.spread(first, plan.y)
    rest = jnp.concatenate(others)
    far_diagonal = plan.spread(rest, plan.diagonal)
    far_y = plan.spread(rest, plan.y)
    far_x = plan.spread(jnp.concatenate(others + near_y), plan.x)
    pieces = [jnp.concatenate([mine] + others + near_x + near_y)] + far_y + far_x + far_diagonal
    x = jnp.concatenate(pieces + [plan.swap(piece, plan.core) for piece in pieces])

    sizes = [piece.shape[0] for piece in pieces] * 2
    results = experts(x, expert_gate, expert_up, expert_down, share, sizes)

    half = len(pieces)
    sums = [
        total_of([results[i], plan.swap(results[half + i], plan.core)])
        for i in reversed(range(half))
    ][::-1]
    back = plan.swaps(sums[1:], plan.y + plan.x + plan.diagonal)
    height, x_end = rest.shape[0], len(plan.y) + len(plan.x)
    column = sums[0][: share + height]
    near = sums[0][share + height :].reshape(-1, share, width)
    through = [v[height:] for v in back[len(plan.y) : x_end]]
    through = total_of([near[len(plan.x) :].reshape(-1, width)] + through)
    others = total_of([v[:height] for v in back[::-1]] + [column[share:]])
    others = plan.swaps(list(others.reshape(-1, share, width)), plan.z)
    wait = back[len(plan.y)][:share, :1] * 0
    near_x = plan.swaps([value + wait for value in near[: len(plan.x)]], plan.x)
    near_y = plan.swaps(list(through.reshape(-1, share, width)), plan.y)
    moe_sum = total_of([column[:share]] + near_x + near_y + others[-1:] + others[:-1])
    return (hidden + moe_sum).astype(BF)


def solution(mesh):
    return jax.shard_map(
        shards,
        mesh=mesh,
        in_specs=(
            P("dp", None, None),
            P("dp", None, None),
            P("dp", None, None),
            P("dp", None, "tensor", None),
            P("dp", None, "tensor", None),
            P("dp"),
            P(("dp", "tensor"), None),
            P(),
            P(),
            P("tensor", None),
            P(),
            P(("dp", "tensor"), None),
            P(("dp", "tensor"), None),
            P(("dp", "tensor"), None, None),
            P(("dp", "tensor"), None, None),
            P(("dp", "tensor"), None, None),
        ),
        out_specs=P(("dp", "tensor"), None),
        check_vma=False,
    )
```

```python
import functools

import jax
import jax.numpy as jnp
from jax import lax
from jax.experimental import pallas as pl
from jax.experimental.pallas import tpu as pltpu
from jax.sharding import PartitionSpec as P

BF = jnp.bfloat16
F32 = jnp.float32
I32 = jnp.int32
MIB = 1 << 20
LANES = 128
CAP = 3


def rms_scale(values, gain):
    mean_sq = jnp.mean(values * values, axis=-1, keepdims=True)
    return values * lax.rsqrt(mean_sq + 1e-06) * gain


def matmul(a, b):
    return jnp.dot(a, b, preferred_element_type=F32)


def matmul_t(a, b):
    return lax.dot_general(a, b, (((1,), (1,)), ((), ())), preferred_element_type=F32)


def iota(shape, dim):
    return lax.broadcasted_iota(I32, shape, dim)


def in_hbm(value):
    return pltpu.with_memory_space_constraint(value, pltpu.HBM)


def attention_kernel(flip, *refs):
    sources, refs = refs[:8], refs[8:]
    if flip == 0:
        ids_hbm, gates_hbm, w_hbm, _, out_ref, table_ref, *w_refs = refs[:8]
        refs = refs[8:]
    else:
        out_ref, refs = refs[0], refs[1:]
    len_hbm, q_hbm, nk_hbm, nv_hbm, k_hbm, v_hbm, qg_hbm, kg_hbm = sources
    lengths, q_ref, nk_ref, nv_ref, k_ref, v_ref, qg_ref, kg_ref = refs[:8]
    nk_scr, nv_scr, num, tops, totals, score, weight, sem = refs[8:16]
    tensor_pos = lax.axis_index("tensor")
    rows, group, hd = q_ref.shape
    kvh, cache = k_hbm.shape[1], k_ref.shape[1]
    heads_own = q_hbm.shape[1] // lax.axis_size("tensor")
    parts = group // heads_own
    which = (tensor_pos // parts) ^ flip
    heads = pl.ds(pl.multiple_of(which * group, group), group)
    pairs = [
        (len_hbm, lengths),
        (nk_hbm, nk_ref),
        (nv_hbm, nv_ref),
        (qg_hbm, qg_ref),
        (kg_hbm, kg_ref),
        (q_hbm.at[:, heads], q_ref),
        (k_hbm.at[:, which], k_ref),
        (v_hbm.at[:, which], v_ref),
    ]
    if flip == 0:
        ids_ref, gates_ref = refs[16:]
        pairs = [(ids_hbm, ids_ref), (gates_hbm, gates_ref)] + pairs
        size = w_refs[0].shape[0]
        pairs += [(w_hbm.at[pl.ds(i * size, size)], ref) for i, ref in enumerate(w_refs)]
    copies = [pltpu.make_async_copy(src, dst, sem.at[i]) for i, (src, dst) in enumerate(pairs)]
    for c in copies:
        c.start()
    if flip == 0:
        for c in copies[:2]:
            c.wait()
        ahead = copies[-2:]
        copies = copies[2:-2]
        gates = gates_ref[...]
        route = (gates / jnp.sum(gates, axis=1, keepdims=True)).astype(BF).astype(F32)
        expert = iota(table_ref.shape, 1)
        table = jnp.zeros(table_ref.shape, F32)
        for k in range(gates.shape[1]):
            table = jnp.where(expert == ids_ref[:, k : k + 1], route[:, k : k + 1], table)
        table_ref[...] = table.astype(BF)

    step = 8
    blocks = rows // step
    many, cols = step * group, step * cache
    scaling = hd ** (-0.5)
    same = iota((many, cols), 0) // group == iota((many, cols), 1) // cache
    col_row = iota((1, cols), 1) // cache
    col_pos = iota((1, cols), 1) % cache + tensor_pos * cache
    new_here = iota((many, 2 * step), 1) == iota((many, 2 * step), 0) // group
    new_here = new_here & (tensor_pos == 0)

    for c in copies[:5]:
        c.wait()
    for r in range(rows):
        nk_scr[r * kvh : (r + 1) * kvh, :] = nk_ref[r].astype(F32)
        nv_scr[r * kvh : (r + 1) * kvh, :] = nv_ref[r].astype(F32)
    query_gain = qg_ref[...]
    new_rows = pl.ds(which, rows, stride=kvh)
    key_norm = rms_scale(nk_scr[new_rows, :], kg_ref[...])
    new_value = nv_scr[new_rows, :]
    empty = jnp.zeros((step, hd), F32)
    for c in copies[5:]:
        c.wait()

    def rows_of(ref, b, size):
        return ref[b * step : (b + 1) * step].reshape(size, hd)

    def with_empty(value, b):
        return jnp.concatenate([value[b * step : (b + 1) * step], empty]).astype(BF)

    queries = []
    for b in range(blocks):
        query = rows_of(q_ref, b, many).astype(F32)
        queries.append(rms_scale(query, query_gain).astype(BF))
    for b in range(blocks):
        limit = jnp.zeros((1, cols), I32)
        for i in range(step):
            limit = jnp.where(col_row == i, lengths[b * step + i], limit)
        included = same & (col_pos < limit)
        scores = matmul_t(queries[b], rows_of(k_ref, b, cols)) * scaling
        score[b, :, :cols] = jnp.where(included, scores, -1e30)
        scores = matmul_t(queries[b], with_empty(key_norm, b)) * scaling
        score[b, :, cols:] = jnp.where(new_here, scores, -1e30)
    for b in range(blocks):
        top = jnp.maximum(jnp.max(score[b], axis=1, keepdims=True), -1e29).astype(BF).astype(F32)
        tops[b * many : (b + 1) * many, :] = jnp.broadcast_to(top, (many, LANES))
    for b in range(blocks):
        top = tops[b * many : (b + 1) * many, 0:1]
        weights = jnp.exp(score[b] - top).astype(BF)
        weight[b] = weights
        total = jnp.sum(weights.astype(F32), axis=1, keepdims=True)
        totals[b * many : (b + 1) * many, :] = jnp.broadcast_to(total, (many, LANES))
    for b in range(blocks):
        num[b * many : (b + 1) * many, :] = matmul(
            weight[b, :, :cols], rows_of(v_ref, b, cols)
        ) + matmul(weight[b, :, cols:], with_empty(new_value, b))

    lane = iota((rows, LANES), 1)
    for t in range(parts):
        slot = (tensor_pos % parts) ^ t
        side = jnp.zeros((rows, LANES), F32)
        for h in range(heads_own):
            own = pl.ds(t * heads_own + h, rows, stride=group)
            out_ref[slot, :, h * hd : (h + 1) * hd] = num[own, :].astype(BF)
            total = totals[own, :]
            high = total.astype(BF).astype(F32)
            side = jnp.where(lane == h, tops[own, :], side)
            side = jnp.where(lane == heads_own + h, high, side)
            side = jnp.where(lane == 2 * heads_own + h, total - high, side)
        out_ref[slot, :, heads_own * hd :] = side.astype(BF)
    if flip == 0:
        for c in ahead:
            c.wait()


def attention(
    flip, lengths, queries, new_keys, new_values, key_cache, value_cache, qg, kg, parts, more
):
    rows, heads, hd = queries.shape
    kvh, cache = key_cache.shape[1:3]
    group = heads // kvh
    blocks = rows // 8
    args = [lengths, queries, new_keys, new_values, key_cache, value_cache]
    args = [in_hbm(a) for a in (*args, qg.reshape(1, -1), kg.reshape(1, -1))]
    outs = [jax.ShapeDtypeStruct((parts // kvh, rows, heads // parts * hd + LANES), BF)]
    scratch = [
        pltpu.SMEM((rows,), I32),
        pltpu.VMEM((rows, group, hd), BF),
        pltpu.VMEM(new_keys.shape, BF),
        pltpu.VMEM(new_values.shape, BF),
        pltpu.VMEM((rows, cache, hd), BF),
        pltpu.VMEM((rows, cache, hd), BF),
        pltpu.VMEM((1, hd), F32),
        pltpu.VMEM((1, hd), F32),
        pltpu.VMEM((rows * kvh, hd), F32),
        pltpu.VMEM((rows * kvh, hd), F32),
        pltpu.VMEM((rows * group, hd), F32),
        pltpu.VMEM((rows * group, LANES), F32),
        pltpu.VMEM((rows * group, LANES), F32),
        pltpu.VMEM((blocks, 8 * group, 8 * (cache + 2)), F32),
        pltpu.VMEM((blocks, 8 * group, 8 * (cache + 2)), BF),
        pltpu.SemaphoreType.DMA((12,)),
    ]
    specs = [pl.BlockSpec(memory_space=pltpu.HBM)] * len(args)
    size = 2 * rows * group * hd * 8
    if flip == 0:
        expert_ids, gate_weights, lanes, later, earlier = more
        args += [in_hbm(a) for a in (expert_ids, gate_weights, later)] + [earlier]
        specs += [pl.BlockSpec(memory_space=pltpu.HBM)] * 3 + [pl.BlockSpec(memory_space=pl.ANY)]
        outs.append(jax.ShapeDtypeStruct((expert_ids.shape[0], lanes), BF))
        outs += [pltpu.VMEM((later.shape[0] // 2, later.shape[1]), later.dtype)] * 2
        scratch += [pltpu.VMEM(expert_ids.shape, I32), pltpu.VMEM(gate_weights.shape, F32)]
        size = size + 2 * later.size
    return pl.pallas_call(
        functools.partial(attention_kernel, flip),
        out_shape=tuple(outs),
        in_specs=specs,
        out_specs=(pl.BlockSpec(memory_space=pltpu.VMEM),) * len(outs),
        scratch_shapes=scratch,
        compiler_params=pltpu.CompilerParams(vmem_limit_bytes=16 * MIB),
        cost_estimate=pl.CostEstimate(flops=size, bytes_accessed=size, transcendentals=0),
        name="attention",
    )(*args)


def projection_kernel(parts, cuts, *refs):
    got = refs[:parts]
    w_refs, refs = refs[parts : parts + cuts], refs[parts + cuts :]
    out_ref, attn = refs
    tensor_pos = lax.axis_index("tensor")
    width = w_refs[0].shape[1]
    depth = attn.shape[1]
    share = out_ref.shape[2]
    hd = LANES
    heads_own = depth // hd
    size = 512
    sides = [g[:, depth:].astype(F32) for g in got]
    tops = [s[:, :heads_own] for s in sides]
    top = functools.reduce(jnp.maximum, tops)
    factors = [jnp.exp(t - top) for t in tops]
    totals = [
        f * (s[:, heads_own : 2 * heads_own] + s[:, 2 * heads_own : 3 * heads_own])
        for f, s in zip(factors, sides)
    ]
    total = functools.reduce(jnp.add, totals)
    factors = [f / total for f in factors]
    for h in range(heads_own):
        cols = slice(h * hd, (h + 1) * hd)
        terms = [g[:, cols].astype(F32) * f[:, h : h + 1] for g, f in zip(got, factors)]
        attn[:, cols] = functools.reduce(jnp.add, terms).astype(BF)
    part = depth // cuts
    for start in range(0, width, size):
        cols = slice(start, start + size)
        result = functools.reduce(
            jnp.add,
            [
                matmul(attn[:, k * part : (k + 1) * part], w_ref[:, cols])
                for k, w_ref in enumerate(w_refs)
            ],
        )
        for t in range(parts):
            slot = tensor_pos ^ t
            block = result[t * share : (t + 1) * share].astype(BF)
            out_ref[slot & 1, slot >> 1, :, cols] = block


def projection(got, weights, share):
    parts = len(got)
    rows = got[0].shape[0]
    depth = sum(w.shape[0] for w in weights)
    width = weights[0].shape[1]
    vmem = pl.BlockSpec(memory_space=pltpu.VMEM)
    return pl.pallas_call(
        functools.partial(projection_kernel, parts, len(weights)),
        out_shape=jax.ShapeDtypeStruct((2, parts // 2, share, width), BF),
        in_specs=[vmem] * (parts + len(weights)),
        out_specs=vmem,
        scratch_shapes=[pltpu.VMEM((rows, depth), BF)],
        compiler_params=pltpu.CompilerParams(vmem_limit_bytes=12 * MIB),
        name="projection",
    )(*got, *weights)


def expert_kernel(slots, sizes, *refs):
    x_ref, gate, up, down_hbm = refs[:4]
    outs = refs[4 : 4 + len(sizes)]
    down, xc, act, res, sem = refs[4 + len(sizes) :]
    own = lax.axis_index("dp") * lax.axis_size("tensor") + lax.axis_index("tensor")
    rows = x_ref.shape[0]
    _, width, hidden = gate.shape
    padded = res.shape[0]
    fsize = 384
    dsize = 1024
    chunks = width // dsize

    def down_copy(i):
        cols = pl.ds(i * dsize, dsize)
        return pltpu.make_async_copy(down_hbm.at[0, :, cols], down.at[:, cols], sem.at[i])

    for i in range(chunks):
        down_copy(i).start()
    table = x_ref[:, width:]
    pick = (iota((16, table.shape[1]), 1) == own).astype(F32).astype(BF)
    named = matmul_t(pick, table) != 0.0
    before = (iota((rows, rows), 0) < iota((rows, rows), 1)).astype(F32).astype(BF)
    place = matmul(named.astype(F32).astype(BF), before)
    place = jnp.where(named, place, -1.0)[:1]
    take = (iota((slots, rows), 0).astype(F32) == place).astype(F32).astype(BF)
    for i in range(chunks):
        cols = slice(i * dsize, (i + 1) * dsize)
        xc[:, cols] = matmul(take, x_ref[:, cols]).astype(BF)

    lane = iota(table.shape, 1)
    weight = jnp.sum(jnp.where(lane == own, table.astype(F32), 0.0), axis=1, keepdims=True)
    named = jnp.broadcast_to((weight != 0.0).astype(F32), (rows, LANES)).astype(BF)
    after = (iota((rows, rows), 1) < iota((rows, rows), 0)).astype(F32).astype(BF)
    place = matmul(after, named)[:, :1]
    spread = jnp.where(iota((rows, padded), 1).astype(F32) == place, weight, 0.0).astype(BF)
    if padded > slots:
        res[slots:, :] = jnp.zeros((padded - slots, dsize), BF)

    for i in range(hidden // fsize):
        cols = slice(i * fsize, (i + 1) * fsize)
        g = matmul(xc[...], gate[0, :, cols])
        u = matmul(xc[...], up[0, :, cols])
        act[:, cols] = (g / (1.0 + jnp.exp(-g)) * u).astype(BF)
    for i in range(chunks):
        down_copy(i).wait()
        cols = slice(i * dsize, (i + 1) * dsize)
        res[:slots, :] = matmul(act[...], down[:, cols]).astype(BF)
        result, start = matmul(spread, res[...]), 0
        for size, out in zip(sizes, outs):
            out[:, cols] = result[start : start + size].astype(BF)
            start += size


def experts(x, expert_gate, expert_up, expert_down, share, sizes):
    rows = x.shape[0]
    _, width, hidden = expert_gate.shape
    slots = rows // share * CAP
    vmem = pl.BlockSpec(memory_space=pltpu.VMEM)
    return pl.pallas_call(
        functools.partial(expert_kernel, slots, sizes),
        out_shape=tuple(jax.ShapeDtypeStruct((size, width), BF) for size in sizes),
        in_specs=[vmem] * 3 + [pl.BlockSpec(memory_space=pltpu.HBM)],
        out_specs=(vmem,) * len(sizes),
        scratch_shapes=[
            pltpu.VMEM((hidden, width), BF),
            pltpu.VMEM((slots, width), BF),
            pltpu.VMEM((slots, hidden), BF),
            pltpu.VMEM((-(-slots // LANES) * LANES, 1024), BF),
            pltpu.SemaphoreType.DMA((width // 1024,)),
        ],
        compiler_params=pltpu.CompilerParams(vmem_limit_bytes=(16 + rows // 32) * MIB),
        name="experts",
    )(x, expert_gate, expert_up, in_hbm(expert_down))


class Plan:
    def __init__(self, dp, tensor):
        self.zlen = min(4, dp)
        xlen, ylen = dp // self.zlen, tensor // 2
        self.count = dp * tensor
        self.core = 1
        self.y = [2 * j for j in range(1, ylen)]
        self.z = [tensor * xlen * j for j in range(1, self.zlen)]
        self.x = [tensor * j for j in range(1, xlen)]
        self.diagonal = [jx + jy for jx in self.x for jy in self.y]

    def swap(self, value, flip):
        return lax.ppermute(value, ("dp", "tensor"), [(i, i ^ flip) for i in range(self.count)])

    def swaps(self, values, flips):
        pairs = list(zip(values, flips))[::-1]
        return [self.swap(value.astype(BF), flip) for value, flip in pairs][::-1]

    def spread(self, value, flips):
        return self.swaps([value] * len(flips), flips)


def total_of(values):
    return functools.reduce(jnp.add, [v.astype(F32) for v in values])


def shards(
    queries,
    new_keys,
    new_values,
    key_cache,
    value_cache,
    lengths,
    residual_in,
    query_gain,
    key_gain,
    out_proj,
    norm_gain,
    expert_ids,
    gate_weights,
    expert_gate,
    expert_up,
    expert_down,
):
    tensor = lax.axis_size("tensor")
    dp = lax.axis_size("dp")
    plan = Plan(dp, tensor)
    share, width = residual_in.shape
    lanes = -(-dp * tensor // LANES) * LANES

    inputs = (lengths, queries, new_keys, new_values, key_cache, value_cache, query_gain, key_gain)
    groups = key_cache.shape[1]
    got, local = [], None
    for flip in reversed(range(groups)):
        more = (expert_ids, gate_weights, lanes, out_proj, local)
        results = attention(flip, *inputs, tensor, more)
        local = results[0]
        for j in range(0, tensor // groups, 2):
            far = flip * (tensor // groups) + j
            pair = local[j : j + 2]
            if far:
                pair = plan.swap(pair, far)
            got += [pair[0], plan.swap(pair[1], plan.core)]
    _, table, *weights = results
    partial = projection(got, weights, share)
    pair = total_of([partial[0], plan.swap(partial[1], plan.core)])
    projected = total_of([pair[0]] + plan.swaps(list(pair[1:]), plan.y))
    hidden = residual_in.astype(F32) + projected
    normed = rms_scale(hidden, norm_gain).astype(BF)

    mine = jnp.concatenate([normed, table], axis=1)
    others = plan.spread(mine, plan.z)
    first = mine + others[0][:, :1] * 0
    near_x = plan.spread(first, plan.x)
    near_y = plan.spread(first, plan.y)
    rest = jnp.concatenate(others)
    far_diagonal = plan.spread(rest, plan.diagonal)
    far_y = plan.spread(rest, plan.y)
    far_x = plan.spread(jnp.concatenate(others + near_y), plan.x)
    pieces = [jnp.concatenate([mine] + others + near_x + near_y)] + far_y + far_x + far_diagonal
    x = jnp.concatenate(pieces + [plan.swap(piece, plan.core) for piece in pieces])

    sizes = [piece.shape[0] for piece in pieces] * 2
    results = experts(x, expert_gate, expert_up, expert_down, share, sizes)

    half = len(pieces)
    sums = [
        total_of([results[i], plan.swap(results[half + i], plan.core)])
        for i in reversed(range(half))
    ][::-1]
    back = plan.swaps(sums[1:], plan.y + plan.x + plan.diagonal)
    height, x_end = rest.shape[0], len(plan.y) + len(plan.x)
    column = sums[0][: share + height]
    near = sums[0][share + height :].reshape(-1, share, width)
    through = [v[height:] for v in back[len(plan.y) : x_end]]
    through = total_of([near[len(plan.x) :].reshape(-1, width)] + through)
    others = total_of([v[:height] for v in back[::-1]] + [column[share:]])
    others = plan.swaps(list(others.reshape(-1, share, width)), plan.z)
    wait = back[len(plan.y)][:share, :1] * 0
    near_x = plan.swaps([value + wait for value in near[: len(plan.x)]], plan.x)
    near_y = plan.swaps(list(through.reshape(-1, share, width)), plan.y)
    moe_sum = total_of([column[:share]] + near_x + near_y + others[::-1])
    return (hidden + moe_sum).astype(BF)


def solution(mesh):
    return jax.shard_map(
        shards,
        mesh=mesh,
        in_specs=(
            P("dp", None, None),
            P("dp", None, None),
            P("dp", None, None),
            P("dp", None, "tensor", None),
            P("dp", None, "tensor", None),
            P("dp"),
            P(("dp", "tensor"), None),
            P(),
            P(),
            P("tensor", None),
            P(),
            P(("dp", "tensor"), None),
            P(("dp", "tensor"), None),
            P(("dp", "tensor"), None, None),
            P(("dp", "tensor"), None, None),
            P(("dp", "tensor"), None, None),
        ),
        out_specs=P(("dp", "tensor"), None),
        check_vma=False,
    )
```

```python
import functools

import jax
import jax.numpy as jnp
from jax import lax
from jax.experimental import pallas as pl
from jax.experimental.pallas import tpu as pltpu
from jax.sharding import PartitionSpec as P

BF = jnp.bfloat16
F32 = jnp.float32
I32 = jnp.int32
MIB = 1 << 20
LANES = 128
CAP = 3


def rms_scale(values, gain):
    mean_sq = jnp.mean(values * values, axis=-1, keepdims=True)
    return values * lax.rsqrt(mean_sq + 1e-06) * gain


def matmul(a, b):
    return jnp.dot(a, b, preferred_element_type=F32)


def matmul_t(a, b):
    return lax.dot_general(a, b, (((1,), (1,)), ((), ())), preferred_element_type=F32)


def iota(shape, dim):
    return lax.broadcasted_iota(I32, shape, dim)


def in_hbm(value):
    return pltpu.with_memory_space_constraint(value, pltpu.HBM)


def attention_kernel(flip, *refs):
    sources, refs = refs[:8], refs[8:]
    if flip == 0:
        w_hbm, ids_hbm, gates_hbm, _, out_ref, w_ref, table_ref = refs[:7]
        refs = refs[7:]
    else:
        w_hbm, out_ref, w_ref = refs[:3]
        refs = refs[3:]
    len_hbm, q_hbm, nk_hbm, nv_hbm, k_hbm, v_hbm, qg_hbm, kg_hbm = sources
    lengths, q_ref, nk_ref, nv_ref, k_ref, v_ref, qg_ref, kg_ref = refs[:8]
    nk_scr, nv_scr, num, tops, totals, score, weight, sem = refs[8:16]
    tensor_pos = lax.axis_index("tensor")
    rows, group, hd = q_ref.shape
    kvh, cache = k_hbm.shape[1], k_ref.shape[1]
    heads_own = q_hbm.shape[1] // lax.axis_size("tensor")
    parts = group // heads_own
    which = (tensor_pos // parts) ^ flip
    heads = pl.ds(pl.multiple_of(which * group, group), group)
    pairs = [
        (len_hbm, lengths),
        (nk_hbm, nk_ref),
        (nv_hbm, nv_ref),
        (qg_hbm, qg_ref),
        (kg_hbm, kg_ref),
        (q_hbm.at[:, heads], q_ref),
        (k_hbm.at[:, which], k_ref),
        (v_hbm.at[:, which], v_ref),
    ]
    if flip == 0:
        ids_ref, gates_ref = refs[16:]
        pairs = [(ids_hbm, ids_ref), (gates_hbm, gates_ref)] + pairs
    start = 0 if flip else w_hbm.shape[0] - w_ref.shape[0]
    pairs.append((w_hbm.at[pl.ds(start, w_ref.shape[0])], w_ref))
    copies = [pltpu.make_async_copy(src, dst, sem.at[i]) for i, (src, dst) in enumerate(pairs)]
    for c in copies:
        c.start()
    ahead, copies = copies[-1], copies[:-1]
    if flip == 0:
        for c in copies[:2]:
            c.wait()
        copies = copies[2:]
        gates = gates_ref[...]
        route = (gates / jnp.sum(gates, axis=1, keepdims=True)).astype(BF).astype(F32)
        expert = iota(table_ref.shape, 1)
        table = jnp.zeros(table_ref.shape, F32)
        for k in range(gates.shape[1]):
            table = jnp.where(expert == ids_ref[:, k : k + 1], route[:, k : k + 1], table)
        table_ref[...] = table.astype(BF)

    step = 8
    blocks = rows // step
    many, cols = step * group, step * cache
    scaling = hd ** (-0.5)
    same = iota((many, cols), 0) // group == iota((many, cols), 1) // cache
    col_row = iota((1, cols), 1) // cache
    col_pos = iota((1, cols), 1) % cache + tensor_pos * cache
    new_here = iota((many, 2 * step), 1) == iota((many, 2 * step), 0) // group
    new_here = new_here & (tensor_pos == 0)

    for c in copies[:5]:
        c.wait()
    for r in range(rows):
        nk_scr[r * kvh : (r + 1) * kvh, :] = nk_ref[r].astype(F32)
        nv_scr[r * kvh : (r + 1) * kvh, :] = nv_ref[r].astype(F32)
    query_gain = qg_ref[...]
    new_rows = pl.ds(which, rows, stride=kvh)
    key_norm = rms_scale(nk_scr[new_rows, :], kg_ref[...])
    new_value = nv_scr[new_rows, :]
    empty = jnp.zeros((step, hd), F32)
    for c in copies[5:]:
        c.wait()

    def rows_of(ref, b, size):
        return ref[b * step : (b + 1) * step].reshape(size, hd)

    def with_empty(value, b):
        return jnp.concatenate([value[b * step : (b + 1) * step], empty]).astype(BF)

    queries = []
    for b in range(blocks):
        query = rows_of(q_ref, b, many).astype(F32)
        queries.append(rms_scale(query, query_gain).astype(BF))
    for b in range(blocks):
        limit = jnp.zeros((1, cols), I32)
        for i in range(step):
            limit = jnp.where(col_row == i, lengths[b * step + i], limit)
        included = same & (col_pos < limit)
        scores = matmul_t(queries[b], rows_of(k_ref, b, cols)) * scaling
        score[b, :, :cols] = jnp.where(included, scores, -1e30)
        scores = matmul_t(queries[b], with_empty(key_norm, b)) * scaling
        score[b, :, cols:] = jnp.where(new_here, scores, -1e30)
    for b in range(blocks):
        top = jnp.maximum(jnp.max(score[b], axis=1, keepdims=True), -1e29).astype(BF).astype(F32)
        tops[b * many : (b + 1) * many, :] = jnp.broadcast_to(top, (many, LANES))
    for b in range(blocks):
        top = tops[b * many : (b + 1) * many, 0:1]
        weights = jnp.exp(score[b] - top).astype(BF)
        weight[b] = weights
        total = jnp.sum(weights.astype(F32), axis=1, keepdims=True)
        totals[b * many : (b + 1) * many, :] = jnp.broadcast_to(total, (many, LANES))
    for b in range(blocks):
        num[b * many : (b + 1) * many, :] = matmul(
            weight[b, :, :cols], rows_of(v_ref, b, cols)
        ) + matmul(weight[b, :, cols:], with_empty(new_value, b))

    lane = iota((rows, LANES), 1)
    for t in range(parts):
        slot = (tensor_pos % parts) ^ t
        side = jnp.zeros((rows, LANES), F32)
        for h in range(heads_own):
            own = pl.ds(t * heads_own + h, rows, stride=group)
            out_ref[slot, :, h * hd : (h + 1) * hd] = num[own, :].astype(BF)
            total = totals[own, :]
            high = total.astype(BF).astype(F32)
            side = jnp.where(lane == h, tops[own, :], side)
            side = jnp.where(lane == heads_own + h, high, side)
            side = jnp.where(lane == 2 * heads_own + h, total - high, side)
        out_ref[slot, :, heads_own * hd :] = side.astype(BF)
    ahead.wait()


def attention(
    flip, lengths, queries, new_keys, new_values, key_cache, value_cache, qg, kg, parts, more
):
    rows, heads, hd = queries.shape
    kvh, cache = key_cache.shape[1:3]
    group = heads // kvh
    blocks = rows // 8
    args = [lengths, queries, new_keys, new_values, key_cache, value_cache]
    later, *more = more
    share = later.shape[0] // 4
    args = [in_hbm(a) for a in (*args, qg.reshape(1, -1), kg.reshape(1, -1), later)]
    outs = [
        jax.ShapeDtypeStruct((parts // kvh, rows, heads // parts * hd + LANES), BF),
        pltpu.VMEM((share if flip else 3 * share, later.shape[1]), later.dtype),
    ]
    scratch = [
        pltpu.SMEM((rows,), I32),
        pltpu.VMEM((rows, group, hd), BF),
        pltpu.VMEM(new_keys.shape, BF),
        pltpu.VMEM(new_values.shape, BF),
        pltpu.VMEM((rows, cache, hd), BF),
        pltpu.VMEM((rows, cache, hd), BF),
        pltpu.VMEM((1, hd), F32),
        pltpu.VMEM((1, hd), F32),
        pltpu.VMEM((rows * kvh, hd), F32),
        pltpu.VMEM((rows * kvh, hd), F32),
        pltpu.VMEM((rows * group, hd), F32),
        pltpu.VMEM((rows * group, LANES), F32),
        pltpu.VMEM((rows * group, LANES), F32),
        pltpu.VMEM((blocks, 8 * group, 8 * (cache + 2)), F32),
        pltpu.VMEM((blocks, 8 * group, 8 * (cache + 2)), BF),
        pltpu.SemaphoreType.DMA((12,)),
    ]
    specs = [pl.BlockSpec(memory_space=pltpu.HBM)] * len(args)
    size = 2 * rows * group * hd * 8
    if flip == 0:
        expert_ids, gate_weights, lanes, earlier = more
        args += [in_hbm(expert_ids), in_hbm(gate_weights), earlier]
        specs += [pl.BlockSpec(memory_space=pltpu.HBM)] * 2 + [pl.BlockSpec(memory_space=pl.ANY)]
        outs.append(jax.ShapeDtypeStruct((expert_ids.shape[0], lanes), BF))
        scratch += [pltpu.VMEM(expert_ids.shape, I32), pltpu.VMEM(gate_weights.shape, F32)]
        size = size + 2 * later.size
    return pl.pallas_call(
        functools.partial(attention_kernel, flip),
        out_shape=tuple(outs),
        in_specs=specs,
        out_specs=(pl.BlockSpec(memory_space=pltpu.VMEM),) * len(outs),
        scratch_shapes=scratch,
        compiler_params=pltpu.CompilerParams(vmem_limit_bytes=16 * MIB),
        cost_estimate=pl.CostEstimate(flops=size, bytes_accessed=size, transcendentals=0),
        name="attention",
    )(*args)


def projection_kernel(parts, cuts, *refs):
    got = refs[:parts]
    w_refs, refs = refs[parts : parts + cuts], refs[parts + cuts :]
    out_ref, attn = refs
    tensor_pos = lax.axis_index("tensor")
    width = w_refs[0].shape[1]
    depth = attn.shape[1]
    share = out_ref.shape[2]
    hd = LANES
    heads_own = depth // hd
    size = 512
    sides = [g[:, depth:].astype(F32) for g in got]
    tops = [s[:, :heads_own] for s in sides]
    top = functools.reduce(jnp.maximum, tops)
    factors = [jnp.exp(t - top) for t in tops]
    totals = [
        f * (s[:, heads_own : 2 * heads_own] + s[:, 2 * heads_own : 3 * heads_own])
        for f, s in zip(factors, sides)
    ]
    total = functools.reduce(jnp.add, totals)
    factors = [f / total for f in factors]
    for h in range(heads_own):
        cols = slice(h * hd, (h + 1) * hd)
        terms = [g[:, cols].astype(F32) * f[:, h : h + 1] for g, f in zip(got, factors)]
        attn[:, cols] = functools.reduce(jnp.add, terms).astype(BF)
    ends = [0]
    for w_ref in w_refs:
        ends.append(ends[-1] + w_ref.shape[0])
    for start in range(0, width, size):
        cols = slice(start, start + size)
        result = functools.reduce(
            jnp.add,
            [
                matmul(attn[:, ends[k] : ends[k + 1]], w_ref[:, cols])
                for k, w_ref in enumerate(w_refs)
            ],
        )
        for t in range(parts):
            slot = tensor_pos ^ t
            block = result[t * share : (t + 1) * share].astype(BF)
            out_ref[slot & 1, slot >> 1, :, cols] = block


def projection(got, weights, share):
    parts = len(got)
    rows = got[0].shape[0]
    depth = sum(w.shape[0] for w in weights)
    width = weights[0].shape[1]
    vmem = pl.BlockSpec(memory_space=pltpu.VMEM)
    return pl.pallas_call(
        functools.partial(projection_kernel, parts, len(weights)),
        out_shape=jax.ShapeDtypeStruct((2, parts // 2, share, width), BF),
        in_specs=[vmem] * (parts + len(weights)),
        out_specs=vmem,
        scratch_shapes=[pltpu.VMEM((rows, depth), BF)],
        compiler_params=pltpu.CompilerParams(vmem_limit_bytes=12 * MIB),
        name="projection",
    )(*got, *weights)


def expert_kernel(slots, sizes, *refs):
    x_ref, gate, up, down_hbm = refs[:4]
    outs = refs[4 : 4 + len(sizes)]
    down, xc, act, res, sem = refs[4 + len(sizes) :]
    own = lax.axis_index("dp") * lax.axis_size("tensor") + lax.axis_index("tensor")
    rows = x_ref.shape[0]
    _, width, hidden = gate.shape
    padded = res.shape[0]
    fsize = 384
    dsize = 1024
    chunks = width // dsize

    def down_copy(i):
        cols = pl.ds(i * dsize, dsize)
        return pltpu.make_async_copy(down_hbm.at[0, :, cols], down.at[:, cols], sem.at[i])

    for i in range(chunks):
        down_copy(i).start()
    table = x_ref[:, width:]
    pick = (iota((16, table.shape[1]), 1) == own).astype(F32).astype(BF)
    named = matmul_t(pick, table) != 0.0
    before = (iota((rows, rows), 0) < iota((rows, rows), 1)).astype(F32).astype(BF)
    place = matmul(named.astype(F32).astype(BF), before)
    place = jnp.where(named, place, -1.0)[:1]
    take = (iota((slots, rows), 0).astype(F32) == place).astype(F32).astype(BF)
    for i in range(chunks):
        cols = slice(i * dsize, (i + 1) * dsize)
        xc[:, cols] = matmul(take, x_ref[:, cols]).astype(BF)

    lane = iota(table.shape, 1)
    weight = jnp.sum(jnp.where(lane == own, table.astype(F32), 0.0), axis=1, keepdims=True)
    named = jnp.broadcast_to((weight != 0.0).astype(F32), (rows, LANES)).astype(BF)
    after = (iota((rows, rows), 1) < iota((rows, rows), 0)).astype(F32).astype(BF)
    place = matmul(after, named)[:, :1]
    spread = jnp.where(iota((rows, padded), 1).astype(F32) == place, weight, 0.0).astype(BF)
    if padded > slots:
        res[slots:, :] = jnp.zeros((padded - slots, dsize), BF)

    for i in range(hidden // fsize):
        cols = slice(i * fsize, (i + 1) * fsize)
        g = matmul(xc[...], gate[0, :, cols])
        u = matmul(xc[...], up[0, :, cols])
        act[:, cols] = (g / (1.0 + jnp.exp(-g)) * u).astype(BF)
    for i in range(chunks):
        down_copy(i).wait()
        cols = slice(i * dsize, (i + 1) * dsize)
        res[:slots, :] = matmul(act[...], down[:, cols]).astype(BF)
        result, start = matmul(spread, res[...]), 0
        for size, out in zip(sizes, outs):
            out[:, cols] = result[start : start + size].astype(BF)
            start += size


def experts(x, expert_gate, expert_up, expert_down, share, sizes):
    rows = x.shape[0]
    _, width, hidden = expert_gate.shape
    slots = rows // share * CAP
    vmem = pl.BlockSpec(memory_space=pltpu.VMEM)
    return pl.pallas_call(
        functools.partial(expert_kernel, slots, sizes),
        out_shape=tuple(jax.ShapeDtypeStruct((size, width), BF) for size in sizes),
        in_specs=[vmem] * 3 + [pl.BlockSpec(memory_space=pltpu.HBM)],
        out_specs=(vmem,) * len(sizes),
        scratch_shapes=[
            pltpu.VMEM((hidden, width), BF),
            pltpu.VMEM((slots, width), BF),
            pltpu.VMEM((slots, hidden), BF),
            pltpu.VMEM((-(-slots // LANES) * LANES, 1024), BF),
            pltpu.SemaphoreType.DMA((width // 1024,)),
        ],
        compiler_params=pltpu.CompilerParams(vmem_limit_bytes=(16 + rows // 32) * MIB),
        name="experts",
    )(x, expert_gate, expert_up, in_hbm(expert_down))


class Plan:
    def __init__(self, dp, tensor):
        self.zlen = min(4, dp)
        xlen, ylen = dp // self.zlen, tensor // 2
        self.count = dp * tensor
        self.core = 1
        self.y = [2 * j for j in range(1, ylen)]
        self.z = [tensor * xlen * j for j in range(1, self.zlen)]
        self.x = [tensor * j for j in range(1, xlen)]
        self.diagonal = [jx + jy for jx in self.x for jy in self.y]

    def swap(self, value, flip):
        return lax.ppermute(value, ("dp", "tensor"), [(i, i ^ flip) for i in range(self.count)])

    def swaps(self, values, flips):
        pairs = list(zip(values, flips))[::-1]
        return [self.swap(value.astype(BF), flip) for value, flip in pairs][::-1]

    def spread(self, value, flips):
        return self.swaps([value] * len(flips), flips)


def total_of(values):
    return functools.reduce(jnp.add, [v.astype(F32) for v in values])


def shards(
    queries,
    new_keys,
    new_values,
    key_cache,
    value_cache,
    lengths,
    residual_in,
    query_gain,
    key_gain,
    out_proj,
    norm_gain,
    expert_ids,
    gate_weights,
    expert_gate,
    expert_up,
    expert_down,
):
    tensor = lax.axis_size("tensor")
    dp = lax.axis_size("dp")
    plan = Plan(dp, tensor)
    share, width = residual_in.shape
    lanes = -(-dp * tensor // LANES) * LANES

    inputs = (lengths, queries, new_keys, new_values, key_cache, value_cache, query_gain, key_gain)
    groups = key_cache.shape[1]
    got, local, weights = [], None, []
    for flip in reversed(range(groups)):
        more = (out_proj, expert_ids, gate_weights, lanes, local)
        results = attention(flip, *inputs, tensor, more)
        local = results[0]
        weights.append(results[1])
        for j in range(0, tensor // groups, 2):
            far = flip * (tensor // groups) + j
            pair = local[j : j + 2]
            if far:
                pair = plan.swap(pair, far)
            got += [pair[0], plan.swap(pair[1], plan.core)]
    table = results[2]
    partial = projection(got, weights, share)
    pair = total_of([partial[0], plan.swap(partial[1], plan.core)])
    projected = total_of([pair[0]] + plan.swaps(list(pair[1:]), plan.y))
    hidden = residual_in.astype(F32) + projected
    normed = rms_scale(hidden, norm_gain).astype(BF)

    mine = jnp.concatenate([normed, table], axis=1)
    others = plan.spread(mine, plan.z)
    first = mine + others[0][:, :1] * 0
    near_x = plan.spread(first, plan.x)
    near_y = plan.spread(first, plan.y)
    rest = jnp.concatenate(others)
    far_diagonal = plan.spread(rest, plan.diagonal)
    far_y = plan.spread(rest, plan.y)
    far_x = plan.spread(jnp.concatenate(others + near_y), plan.x)
    pieces = [jnp.concatenate([mine] + others + near_x + near_y)] + far_y + far_x + far_diagonal
    x = jnp.concatenate(pieces + [plan.swap(piece, plan.core) for piece in pieces])

    sizes = [piece.shape[0] for piece in pieces] * 2
    results = experts(x, expert_gate, expert_up, expert_down, share, sizes)

    half = len(pieces)
    sums = [
        total_of([results[i], plan.swap(results[half + i], plan.core)])
        for i in reversed(range(half))
    ][::-1]
    back = plan.swaps(sums[1:], plan.y + plan.x + plan.diagonal)
    height, x_end = rest.shape[0], len(plan.y) + len(plan.x)
    column = sums[0][: share + height]
    near = sums[0][share + height :].reshape(-1, share, width)
    through = [v[height:] for v in back[len(plan.y) : x_end]]
    through = total_of([near[len(plan.x) :].reshape(-1, width)] + through)
    others = total_of([v[:height] for v in back[::-1]] + [column[share:]])
    others = plan.swaps(list(others.reshape(-1, share, width)), plan.z)
    wait = back[len(plan.y)][:share, :1] * 0
    near_x = plan.swaps([value + wait for value in near[: len(plan.x)]], plan.x)
    near_y = plan.swaps(list(through.reshape(-1, share, width)), plan.y)
    moe_sum = total_of([column[:share]] + near_x + near_y + others)
    return (hidden + moe_sum).astype(BF)


def solution(mesh):
    return jax.shard_map(
        shards,
        mesh=mesh,
        in_specs=(
            P("dp", None, None),
            P("dp", None, None),
            P("dp", None, None),
            P("dp", None, "tensor", None),
            P("dp", None, "tensor", None),
            P("dp"),
            P(("dp", "tensor"), None),
            P(),
            P(),
            P("tensor", None),
            P(),
            P(("dp", "tensor"), None),
            P(("dp", "tensor"), None),
            P(("dp", "tensor"), None, None),
            P(("dp", "tensor"), None, None),
            P(("dp", "tensor"), None, None),
        ),
        out_specs=P(("dp", "tensor"), None),
        check_vma=False,
    )
```
